32 devices in a mesh: dp: 4 (over z), row: 2 (over x), col: 4 (over y, core).
Axes of the slice: x: 2, y: 2, z: 4, core: 2. Of those that a mesh axis runs over, the one named last changes fastest.
Arguments:
- block_input: bfloat16 [2560, 2560], P('dp', 'col'), may hold values from -6 to 6
- segment_ids: int32 [4, 640], P('dp'), may hold values from 0 to 1, never falling along the last dimension, each value on 1 to 560 neighbouring positions
- output_cotangent: bfloat16 [2560, 2560], P('dp', 'col'), may hold values from -6 to 6
- norm_gains: float32 [2, 2560], P(None, 'col'), may hold values from 0.5 to 1.5
- branch_weights: bfloat16 [2, 2560, 2560], P(None, 'col', 'row'), may hold values from -0.125 to 0.125
- mixer_vectors: float32 [8, 2560], P(None, 'row'), may hold values from -9 to 1.5
- gate_blocks: bfloat16 [2, 10, 256, 256], P(None, 'row'), may hold values from -0.375 to 0.375
- output_weights: bfloat16 [2560, 2560], P('row', 'col'), may hold values from -0.5 to 0.5
- expand_weights: bfloat16 [2, 2560, 7680], P(None, 'col', 'row'), may hold values from -0.125 to 0.125
- contract_weights: bfloat16 [7680, 2560], P('row', 'col'), may hold values from -0.1875 to 0.1875
- gains_momentum: float32 [2, 2560], P(None, 'col'), may hold values from -32 to 32
- branch_momentum: float32 [2, 4, 640, 2560], P(None, 'col', 'dp', 'row'), may hold values from -32 to 32
- vectors_momentum: float32 [8, 2560], P(None, 'row'), may hold values from -32 to 32
- gates_momentum: float32 [2, 10, 256, 256], P(None, 'row'), may hold values from -32 to 32
- output_momentum: float32 [2, 1280, 2560], P('row', 'dp', 'col'), may hold values from -32 to 32
- expand_momentum: float32 [2, 4, 640, 7680], P(None, 'col', 'dp', 'row'), may hold values from -32 to 32
- contract_momentum: float32 [2, 3840, 2560], P('row', 'dp', 'col'), may hold values from -32 to 32
Outputs:
- block_output: bfloat16 [2560, 2560], P('dp', 'col')
- input_grad: bfloat16 [2560, 2560], P('dp', 'col')
- gains_grad: float32 [2, 2560], P(None, 'col')
- branch_grad: float32 [2, 4, 640, 2560], P(None, 'col', 'dp', 'row')
- vectors_grad: float32 [8, 2560], P(None, 'row')
- gates_grad: float32 [2, 10, 256, 256], P(None, 'row')
- output_grad: float32 [2, 1280, 2560], P('row', 'dp', 'col')
- expand_grad: float32 [2, 4, 640, 7680], P(None, 'col', 'dp', 'row')
- contract_grad: float32 [2, 3840, 2560], P('row', 'dp', 'col')
- gains_new: float32 [2, 2560], P(None, 'col')
- branch_new: float32 [2, 4, 640, 2560], P(None, 'col', 'dp', 'row')
- vectors_new: float32 [8, 2560], P(None, 'row')
- gates_new: float32 [2, 10, 256, 256], P(None, 'row')
- output_new: float32 [2, 1280, 2560], P('row', 'dp', 'col')
- expand_new: float32 [2, 4, 640, 7680], P(None, 'col', 'dp', 'row')
- contract_new: float32 [2, 3840, 2560], P('row', 'dp', 'col')
- gains_moment: float32 [2, 2560], P(None, 'col')
- branch_moment: float32 [2, 4, 640, 2560], P(None, 'col', 'dp', 'row')
- vectors_moment: float32 [8, 2560], P(None, 'row')
- gates_moment: float32 [2, 10, 256, 256], P(None, 'row')
- output_moment: float32 [2, 1280, 2560], P('row', 'dp', 'col')
- expand_moment: float32 [2, 4, 640, 7680], P(None, 'col', 'dp', 'row')
- contract_moment: float32 [2, 3840, 2560], P('row', 'dp', 'col')
The draws below stay inside these ranges and needn't reach their ends.
All inputs are finite; a program needn't handle non-finite values.
Results may differ from the reference program's by a relative error of at most 0.012.
Values may be sent and summed in bfloat16 or wider, within the bound.
A program may use at most 256 MiB of HBM per device.

```python
import math
import jax
import jax.numpy as jnp
import numpy as np
from jax import lax

D = 2560
L = 2560
FF = 7680
H = 10
CONV = 4
GROUP = 128
TOK_DEV = 640
HS = 256
TOKENS = 2560
SEQ_MOST = 560
N_DP = 4
N_ROW = 2
N_COL = 4


def draw_mixer_vectors(key, part):
    first, second, third = jax.random.split(key, 3)
    taps = 0.5 * jnp.clip(jax.random.normal(first, (CONV, L), jnp.float32), -3.0, 3.0)
    biases = 0.5 * jnp.clip(jax.random.normal(second, (3, L), jnp.float32), -3.0, 3.0)
    rates = jax.random.uniform(third, (1, L), jnp.float32, -9.0, -2.0)
    return jnp.concatenate([taps, biases, rates], axis=0)


def steps_of(own_key, shape, pieces, smallest, high):
    def one(position, parts):
        draws = jax.random.uniform(jax.random.fold_in(jax.random.fold_in(own_key, 6), position), (parts,), jnp.float32, smallest / len(pieces), high / len(pieces))
        return jnp.repeat(jnp.exp(draws), shape[position] // parts).reshape((-1,) + (1,) * (len(shape) - position - 1))

    level = one(*pieces[0])
    for cut in pieces[1:]:
        level = level * one(*cut)
    return level


def length_profile(count, total, most, slope):
    loads = [(1 << 20) // math.isqrt(grade ** slope) + 1 for grade in range(2, count + 1)]
    rest, given = total - most - (count - 1), [1] * (count - 1)
    while rest > 0:
        movable = [i for i in range(count - 1) if given[i] < most]
        pool, budget = sum([loads[i] for i in movable]), rest
        for i in movable:
            more = min(most - given[i], max(1, budget * loads[i] // pool), rest)
            given[i] = given[i] + more
            rest = rest - more
    return np.array([most] + given)


def uneven(stream_key, number_of, total, bound, lean):
    if number_of == 2:
        one = jax.random.randint(stream_key, (), max(1, total - bound), min(bound, total - 1) + 1)
        return jnp.stack([one, total - one])
    sizes = jnp.asarray(length_profile(number_of, total, bound, lean), jnp.int32)
    pairs = (number_of - 1) // 2
    giver, sink = sizes[1:1 + 2 * pairs:2], sizes[2:2 + 2 * pairs:2]
    slack = jnp.minimum(giver - 1, bound - sink)
    shifted = jax.random.randint(jax.random.fold_in(stream_key, 1), (pairs,), 0, 1 << 20) % (slack + 1)
    sizes = sizes.at[1:1 + 2 * pairs:2].set(giver - shifted).at[2:2 + 2 * pairs:2].set(sink + shifted)
    return sizes[jax.random.permutation(jax.random.fold_in(stream_key, 2), number_of)]


def centred(stream_key, shape, width, limit, pieces=(), kind=jnp.bfloat16):
    values = jax.random.normal(stream_key, shape, jnp.float32) * width
    if len(pieces) > 0:
        values = steps_of(stream_key, shape, pieces, -0.22, 0.18) * values
    return jnp.clip(values, min=-limit, max=limit).astype(kind)


def setup_inputs(seed: int = 0) -> dict:
    seeds = jax.random.split(jax.random.key(seed), 18)
    block_input = centred(seeds[0], (TOKENS, D), 1.0, 6.0, ((0, 4), (1, 4)))
    segment_ids = jax.vmap(lambda own: jnp.searchsorted(jnp.cumsum(uneven(own, 2, TOK_DEV, SEQ_MOST, 2)), jnp.arange(TOK_DEV), side="right"))(jax.random.split(seeds[1], N_DP)).reshape((N_DP, TOK_DEV)).astype(jnp.int32)
    output_cotangent = centred(seeds[2], (TOKENS, D), 1.0, 6.0, ((0, 4), (1, 4)))
    norm_gains = jnp.clip(1.0 + 0.1 * jax.random.normal(seeds[3], (2, D), jnp.float32), 0.5, 1.5)
    branch_weights = centred(seeds[4], (2, D, L), D ** -0.5, 0.125, ((1, 4), (2, 2)))
    mixer_vectors = draw_mixer_vectors(jax.random.fold_in(seeds[17], 71), 0)
    gate_blocks = centred(seeds[6], (2, H, HS, HS), HS ** -0.5, 0.375, ((1, 2),))
    output_weights = centred(seeds[7], (L, D), (L // 16) ** -0.5, 0.5, ((0, 2), (1, 4)))
    expand_weights = centred(seeds[8], (2, D, FF), D ** -0.5, 0.125, ((1, 4), (2, 2)))
    contract_weights = centred(seeds[9], (FF, D), (FF // 8) ** -0.5, 0.1875, ((0, 2), (1, 4)))
    gains_momentum = centred(seeds[10], (2, D), (0.1 * TOKENS ** 0.5), 32.0, ((1, 4),), jnp.float32)
    branch_momentum = centred(seeds[11], (2, N_COL, D // N_COL, L), (0.1 * TOKENS ** 0.5), 32.0, ((1, 4), (2, 4), (3, 2)), jnp.float32)
    vectors_momentum = centred(seeds[12], (CONV + 4, L), (0.1 * TOKENS ** 0.5), 32.0, ((1, 2),), jnp.float32)
    gates_momentum = centred(seeds[13], (2, H, HS, HS), (0.1 * TOKENS ** 0.5), 32.0, ((1, 2),), jnp.float32)
    output_momentum = centred(seeds[14], (N_ROW, L // N_ROW, D), (0.1 * TOKENS ** 0.5), 32.0, ((0, 2), (1, 4), (2, 4)), jnp.float32)
    expand_momentum = centred(seeds[15], (2, N_COL, D // N_COL, FF), (0.1 * TOKENS ** 0.5), 32.0, ((1, 4), (2, 4), (3, 2)), jnp.float32)
    contract_momentum = centred(seeds[16], (N_ROW, FF // N_ROW, D), (0.1 * TOKENS ** 0.5), 32.0, ((0, 2), (1, 4), (2, 4)), jnp.float32)
    return dict(block_input=block_input, segment_ids=segment_ids, output_cotangent=output_cotangent, norm_gains=norm_gains, branch_weights=branch_weights, mixer_vectors=mixer_vectors, gate_blocks=gate_blocks, output_weights=output_weights, expand_weights=expand_weights, contract_weights=contract_weights, gains_momentum=gains_momentum, branch_momentum=branch_momentum, vectors_momentum=vectors_momentum, gates_momentum=gates_momentum, output_momentum=output_momentum, expand_momentum=expand_momentum, contract_momentum=contract_momentum)


@jax.custom_vjp
def low(v):
    return lax.optimization_barrier(v.astype(jnp.bfloat16)).astype(jnp.float32)

@jax.custom_vjp
def low_back(v):
    return v

def low_keep(v):
    return (low(v), None)

def low_pass(kept, grad):
    return (grad,)

def back_keep(v):
    return (v, None)

def back_low(kept, grad):
    return (low(grad),)
low.defvjp(low_keep, low_pass)
low_back.defvjp(back_keep, back_low)
eps_norm = 1e-06
eps_frob = 1e-07
poly_first = 3.4445
poly_second = -4.775
poly_third = 2.0315
momentum_rate = 0.9
muon_rate = 0.1
gate_rate = 0.02
vector_rate = 0.3
decay_scale = 8.0
highest = lax.Precision.HIGHEST

def matmul(left, right):
    return jnp.dot(left, right, precision=highest)

def gelu_tanh(value):
    return jax.nn.gelu(value, approximate=True)

def rms_norm(stream, gain):
    scale = lax.rsqrt(lax.optimization_barrier(jnp.mean(stream * stream, axis=1, keepdims=True)) + eps_norm)
    return stream * scale * gain[None, :]

def orthogonalize(block):
    rows, cols = block.shape
    work = low(block)
    if rows > cols:
        work = work.T
    work = low(work / (jnp.sqrt(jnp.sum(work * work)) + eps_frob))
    for step in range(5):
        gram = low(matmul(work, work.T))
        poly = low(poly_second * gram + poly_third * matmul(gram, gram))
        work = low(poly_first * work + matmul(poly, work))
    if rows > cols:
        work = work.T
    return work * max(1.0, rows / cols) ** 0.5

def muon_step(grad, moment, weight, row_parts, col_parts):
    new_moment = momentum_rate * moment + grad
    rows, cols = new_moment.shape
    brows = rows // row_parts
    bcols = cols // col_parts
    blocks = new_moment.reshape(row_parts, brows, col_parts, bcols).transpose(0, 2, 1, 3)
    orth = jax.vmap(orthogonalize)(blocks.reshape(row_parts * col_parts, brows, bcols))
    orth = orth.reshape(row_parts, col_parts, brows, bcols).transpose(0, 2, 1, 3).reshape(rows, cols)
    return (new_moment, weight - muon_rate * orth)

def grouped_step(grad, moment, weight, rate):
    new_moment = momentum_rate * moment + grad
    rows, cols = new_moment.shape
    grouped = new_moment.reshape(rows, cols // GROUP, GROUP)
    norm_sq = lax.optimization_barrier(jnp.mean(grouped * grouped, axis=2, keepdims=True))
    update = (grouped * lax.rsqrt(norm_sq + eps_norm)).reshape(rows, cols)
    return (new_moment, weight - rate * update)

def reference(block_input, segment_ids, output_cotangent, norm_gains, branch_weights, mixer_vectors, gate_blocks, output_weights, expand_weights, contract_weights, gains_momentum, branch_momentum, vectors_momentum, gates_momentum, output_momentum, expand_momentum, contract_momentum):
    seg_flat = segment_ids.reshape(-1)
    total = seg_flat.shape[0]
    block_count = total // TOK_DEV
    place = jnp.arange(total, dtype=jnp.int32) % TOK_DEV
    valid_list = []
    for shift in range(CONV):
        earlier = jnp.concatenate([jnp.full((shift,), -1, jnp.int32), seg_flat[:total - shift]])
        valid_list.append(((place >= shift) & (earlier == seg_flat)).astype(jnp.float32))
    masks = jnp.stack(valid_list)
    reset = masks[1] < 0.5

    def forward(stream, gains, branch, vectors, gates, outw, expand, contract):
        normed = low(rms_norm(stream, gains[0]))
        mixed = low_back(matmul(normed, branch[0]))
        gelu_in = low_back(matmul(normed, branch[1]))
        conv = jnp.zeros((total, L), jnp.float32) + vectors[CONV][None, :]
        for shift in range(CONV):
            moved = jnp.concatenate([jnp.zeros((shift, L), jnp.float32), mixed[:total - shift]], axis=0)
            conv = conv + vectors[shift][None, :] * moved * masks[shift][:, None]
        conv_low = low(conv).reshape(total, H, HS)
        gate_pre = jnp.einsum('thi,ghij->tghj', conv_low, gates, precision=highest).reshape(total, 2, L)
        gate_pre = low_back(gate_pre + vectors[CONV + 1:CONV + 3][None])
        input_gate = jax.nn.sigmoid(gate_pre[:, 0])
        decay_gate = jax.nn.sigmoid(gate_pre[:, 1])
        log_decay = -decay_scale * decay_gate * jax.nn.softplus(vectors[CONV + 3])[None, :]
        inject_scale = jnp.where(reset[:, None], 1.0, jnp.sqrt(1.0 - jnp.exp(2.0 * log_decay)))
        decay = jnp.where(reset[:, None], 0.0, jnp.exp(log_decay))
        inject = inject_scale * input_gate * conv

        def advance(carry, pair):
            carry = pair[0] * carry + pair[1]
            return (carry, carry)
        decay_blocks = decay.reshape(block_count, TOK_DEV, L).transpose(1, 0, 2)
        inject_blocks = inject.reshape(block_count, TOK_DEV, L).transpose(1, 0, 2)
        unused, states = lax.scan(advance, jnp.zeros((block_count, L), jnp.float32), (decay_blocks, inject_blocks))
        states = states.transpose(1, 0, 2).reshape(total, L)
        hidden = low(gelu_tanh(gelu_in) * states)
        middle = stream + low_back(matmul(hidden, outw))
        normed_two = low(rms_norm(middle, gains[1]))
        up_gate = low_back(matmul(normed_two, expand[0]))
        up_value = low_back(matmul(normed_two, expand[1]))
        activated = low(gelu_tanh(up_gate) * up_value)
        return middle + matmul(activated, contract)
    f32 = jnp.float32
    branch_full = branch_weights.astype(f32)
    expand_full = expand_weights.astype(f32)
    outw_full = output_weights.astype(f32)
    contract_full = contract_weights.astype(f32)
    gates_full = gate_blocks.astype(f32)
    result, pull = jax.vjp(forward, block_input.astype(f32), norm_gains, branch_full, mixer_vectors, gates_full, outw_full, expand_full, contract_full)
    grads = pull(output_cotangent.astype(f32))
    stream_grad, gains_grad, branch_g, vectors_grad, gates_grad, outw_g, expand_g, contract_g = grads
    branch_mom = branch_momentum.reshape(2, D, L)
    expand_mom = expand_momentum.reshape(2, D, FF)
    branch_moment_list = []
    branch_new_list = []
    expand_moment_list = []
    expand_new_list = []
    for which in range(2):
        moment_b, new_b = muon_step(branch_g[which], branch_mom[which], branch_full[which], N_COL, N_ROW)
        branch_moment_list.append(moment_b)
        branch_new_list.append(new_b)
        moment_e, new_e = muon_step(expand_g[which], expand_mom[which], expand_full[which], N_COL, N_ROW)
        expand_moment_list.append(moment_e)
        expand_new_list.append(new_e)
    output_moment, output_new = muon_step(outw_g, output_momentum.reshape(L, D), outw_full, N_ROW, N_COL)
    contract_moment, contract_new = muon_step(contract_g, contract_momentum.reshape(FF, D), contract_full, N_ROW, N_COL)
    gates_moment = momentum_rate * gates_momentum + gates_grad
    gate_sq = lax.optimization_barrier(jnp.mean(gates_moment * gates_moment, axis=(2, 3), keepdims=True))
    gates_new = gates_full - gate_rate * gates_moment * lax.rsqrt(gate_sq + eps_norm)
    vectors_moment, vectors_new = grouped_step(vectors_grad, vectors_momentum, mixer_vectors, vector_rate)
    gains_moment, gains_new = grouped_step(gains_grad, gains_momentum, norm_gains, vector_rate)
    branch_shape = (2, N_COL, D // N_COL, L)
    expand_shape = (2, N_COL, D // N_COL, FF)
    output_shape = (N_ROW, L // N_ROW, D)
    contract_shape = (N_ROW, FF // N_ROW, D)
    return (result.astype(jnp.bfloat16), stream_grad.astype(jnp.bfloat16), gains_grad, branch_g.reshape(branch_shape), vectors_grad, gates_grad, outw_g.reshape(output_shape), expand_g.reshape(expand_shape), contract_g.reshape(contract_shape), gains_new, jnp.stack(branch_new_list).reshape(branch_shape), vectors_new, gates_new, output_new.reshape(output_shape), jnp.stack(expand_new_list).reshape(expand_shape), contract_new.reshape(contract_shape), gains_moment, jnp.stack(branch_moment_list).reshape(branch_shape), vectors_moment, gates_moment, output_moment.reshape(output_shape), jnp.stack(expand_moment_list).reshape(expand_shape), contract_moment.reshape(contract_shape))
```

```python
import functools

import jax
import jax.numpy as jnp
from jax import lax
from jax.experimental import pallas as pl
from jax.experimental.pallas import tpu as pltpu
from jax.sharding import PartitionSpec as P

CONV = 4
GROUP = 128
HS = 256


eps_norm = 1e-06
eps_frob = 1e-07
poly_first = 3.4445
poly_second = -4.775
poly_third = 2.0315
momentum_rate = 0.9
muon_rate = 0.1
gate_rate = 0.02
vector_rate = 0.3
decay_scale = 8.0


def broadcast(value, axis, source):
    kept = jnp.where(lax.axis_index(axis) == source, value, 0).astype(value.dtype)
    return lax.psum(kept, axis)


def from_behind(value, axis, steps):
    count = lax.axis_size(axis)
    initial, last = (max(0, -steps), min(count, count - steps))
    return lax.ppermute(value, axis, [(source, source + steps) for source in range(initial, last)])


def prefix(value, axis, combine, identity, reverse):
    count, here = (lax.axis_size(axis), lax.axis_index(axis))
    joined = lax.all_gather(jnp.stack(value), axis)
    everything = tuple(joined[:, k] for k in range(len(value)))
    start = jax.tree.map(
        lambda part, zero: jnp.broadcast_to(jnp.asarray(zero, part.dtype), part.shape),
        value,
        identity,
    )

    def lap(k, before):
        at = count - 1 - k if reverse else k
        reached = at > here if reverse else at < here
        new = combine(before, jax.tree.map(lambda part: part[at], everything))
        return jax.tree.map(lambda a, b: jnp.where(reached, a, b), new, before)

    return lax.fori_loop(0, count, lap, start)


def gelu_tanh(value):
    return jax.nn.gelu(value, approximate=True)


def product(left, right):
    return jnp.dot(left, right, preferred_element_type=jnp.float32)


def product_tn(left, right):
    return lax.dot_general(
        left, right, (((0,), (0,)), ((), ())), preferred_element_type=jnp.float32
    )


def product_nt(left, right):
    return lax.dot_general(
        left, right, (((1,), (1,)), ((), ())), preferred_element_type=jnp.float32
    )


def link(first, second):
    return (first[0] * second[0], second[0] * first[1] + second[1])


def scan_kernel(reverse, decay_ref, value_ref, prod_ref, sum_ref):
    rows, lanes = decay_ref.shape
    groups = rows // 8

    def lap(k, carry):
        base = pl.multiple_of((groups - 1 - k if reverse else k) * 8, 8)
        decay = decay_ref[pl.ds(base, 8), :]
        value = value_ref[pl.ds(base, 8), :]
        prod, total = carry
        prods, totals = [None] * 8, [None] * 8
        for j in range(7, -1, -1) if reverse else range(8):
            prod = decay[j : j + 1] * prod
            total = decay[j : j + 1] * total + value[j : j + 1]
            prods[j], totals[j] = prod, total
        prod_ref[pl.ds(base, 8), :] = jnp.concatenate(prods, axis=0)
        sum_ref[pl.ds(base, 8), :] = jnp.concatenate(totals, axis=0)
        return (prod, total)

    start = (jnp.ones((1, lanes), jnp.float32), jnp.zeros((1, lanes), jnp.float32))
    lax.fori_loop(0, groups, lap, start)


def linear_scan(decay, value, reverse):
    shape = jax.ShapeDtypeStruct(decay.shape, jnp.float32)
    return pl.pallas_call(
        functools.partial(scan_kernel, reverse),
        out_shape=(shape, shape),
        compiler_params=pltpu.CompilerParams(vmem_limit_bytes=16 * 1024 * 1024),
    )(decay, value)


MESH = pl.DeviceIdType.MESH
MIB = 1024 * 1024


def col_places():
    me = lax.axis_index("col")
    near_bit = lax.rem(me, 2)
    far_bit = lax.div(me, 2)
    return (me, near_bit, far_bit, me + 1 - 2 * near_bit, lax.rem(me + 2, 4))


def greet(axis_places):
    barrier = pltpu.get_barrier_semaphore()
    for axis, place in axis_places:
        pl.semaphore_signal(barrier, inc=1, device_id={axis: place}, device_id_type=MESH)
    pl.semaphore_wait(barrier, len(axis_places))


def dot_nn(left, right):
    return lax.dot_general(
        left, right, (((1,), (0,)), ((), ())), preferred_element_type=jnp.float32
    )


def dot_nt(left, right):
    return lax.dot_general(
        left, right, (((1,), (1,)), ((), ())), preferred_element_type=jnp.float32
    )


def columns_of(j, width, per):
    return (lax.div(j, per), pl.ds(pl.multiple_of(lax.rem(j, per) * width, width), width))


def spread_kernel(
    flip, lhs, w, out, wbuf, send1, recv1, own, send2, recv2, wsem, s1s, s1r, s2s, s2r
):
    chunks, rows, width = send2.shape
    per = out.shape[2] // width
    me, near_bit, far_bit, near, far = col_places()
    depth = lhs.shape[3]

    def w_copy(j):
        k, cols = columns_of(j, width, per)
        return pltpu.make_async_copy(
            w.at[cols, :] if flip else w.at[k, :, cols], wbuf.at[j], wsem.at[j]
        )

    def near_copy(j):
        return pltpu.make_async_remote_copy(
            src_ref=send1.at[j],
            dst_ref=recv1.at[j],
            send_sem=s1s.at[j],
            recv_sem=s1r.at[j],
            device_id={"col": near},
            device_id_type=MESH,
        )

    def far_copy(j):
        return pltpu.make_async_remote_copy(
            src_ref=send2.at[j],
            dst_ref=recv2.at[j],
            send_sem=s2s.at[j],
            recv_sem=s2r.at[j],
            device_id={"col": far},
            device_id_type=MESH,
        )

    def loop(count, act):
        def lap(j, carry):
            act(j)
            return carry

        lax.fori_loop(0, count, lap, 0)

    loop(chunks, lambda j: w_copy(j).start())
    greet((("col", near), ("col", far)))
    dot = dot_nt if flip else dot_nn

    def first(j):
        w_copy(j).wait()
        part = wbuf[j]
        theirs = dot(lhs[:, 1 - near_bit].reshape(2 * rows, depth), part)
        send1[j] = theirs.astype(jnp.bfloat16).reshape(2, rows, width)
        near_copy(j).start()
        mine = dot(lhs[:, near_bit].reshape(2 * rows, depth), part)
        own[j] = mine.reshape(2, rows, width)

    def second(j):
        near_copy(j).wait_recv()
        going = own[j, 1 - far_bit] + recv1[j, 1 - far_bit].astype(jnp.float32)
        send2[j] = going.astype(jnp.bfloat16)
        far_copy(j).start()
        own[j, far_bit] = own[j, far_bit] + recv1[j, far_bit].astype(jnp.float32)

    def third(j):
        far_copy(j).wait_recv()
        k, cols = columns_of(j, width, per)
        out[k, :, cols] = own[j, far_bit] + recv2[j].astype(jnp.float32)

    first(0)

    def both(j):
        first(j + 1)
        second(j)

    loop(chunks - 1, both)
    second(chunks - 1)
    loop(chunks, third)

    def drain(j):
        near_copy(j).wait_send()
        far_copy(j).wait_send()

    loop(chunks, drain)


def spread_product(lhs, w, flip, width, collective):
    tokens, depth = lhs.shape
    rows = tokens // 4
    pairs = 1 if flip else w.shape[0]
    total = w.shape[0] if flip else w.shape[2]
    chunks = pairs * total // width
    tile = (width, depth) if flip else (depth, width)
    bf16, f32 = jnp.bfloat16, jnp.float32
    return pl.pallas_call(
        functools.partial(spread_kernel, flip),
        out_shape=jax.ShapeDtypeStruct((pairs, rows, total), f32),
        in_specs=[pl.BlockSpec(memory_space=pltpu.VMEM), pl.BlockSpec(memory_space=pl.ANY)],
        out_specs=pl.BlockSpec(memory_space=pltpu.VMEM),
        scratch_shapes=[
            pltpu.VMEM((chunks,) + tile, bf16),
            pltpu.VMEM((chunks, 2, rows, width), bf16),
            pltpu.VMEM((chunks, 2, rows, width), bf16),
            pltpu.VMEM((chunks, 2, rows, width), f32),
            pltpu.VMEM((chunks, rows, width), bf16),
            pltpu.VMEM((chunks, rows, width), bf16),
        ]
        + [pltpu.SemaphoreType.DMA((chunks,))] * 5,
        compiler_params=pltpu.CompilerParams(
            collective_id=collective, has_side_effects=True, vmem_limit_bytes=56 * MIB
        ),
    )(lhs.reshape(2, 2, rows, depth), w)


def meet_kernel(flip, grad_mode, *refs):
    if grad_mode:
        piece, w, side, prod, grad_out = refs[:5]
        refs = refs[5:]
    else:
        piece, w, all_out, prod = refs[:4]
        refs = refs[4:]
    wbuf, buf, acc, sendx, recvx, wsem, osem, ns, nr, fs, fr, rs, rr, xs, xr = refs[:15]
    if grad_mode:
        stage, gsem = refs[15:]
    chunks, _, _, rows, width = buf.shape
    per = piece.shape[2] // width
    me, near_bit, far_bit, near, far = col_places()
    across = 1 - lax.axis_index("row")
    f32, bf16 = jnp.float32, jnp.bfloat16

    def w_copy(j):
        k, cols = columns_of(j, width, per)
        return pltpu.make_async_copy(
            w.at[k, :, cols] if flip else w.at[cols, :], wbuf.at[j], wsem.at[j]
        )

    def move(j, source, near_place, far_place, sems, target):
        return pltpu.make_async_remote_copy(
            src_ref=source,
            dst_ref=buf.at[j, far_place, near_place],
            send_sem=sems[0].at[j],
            recv_sem=sems[1].at[j],
            device_id={"col": target},
            device_id_type=MESH,
        )

    def piece_at(j):
        k, cols = columns_of(j, width, per)
        return piece.at[k, :, cols]

    def far_copy(j):
        return move(j, piece_at(j), near_bit, far_bit, (fs, fr), far)

    def near_copy(j):
        return move(j, piece_at(j), near_bit, far_bit, (ns, nr), near)

    def relay(j):
        return move(j, buf.at[j, 1 - far_bit, near_bit], near_bit, 1 - far_bit, (rs, rr), near)

    def out_copy(j):
        k, cols = columns_of(j, width, per)
        return pltpu.make_async_copy(buf.at[j], all_out.at[k, :, :, :, cols], osem.at[j])

    def cross(half):
        return pltpu.make_async_remote_copy(
            src_ref=sendx.at[half],
            dst_ref=recvx.at[half],
            send_sem=xs.at[half],
            recv_sem=xr.at[half],
            device_id={"row": across},
            device_id_type=MESH,
        )

    def loop(count, act):
        def lap(j, carry):
            act(j)
            return carry

        lax.fori_loop(0, count, lap, 0)

    loop(chunks, lambda j: w_copy(j).start())
    greet((("col", near), ("col", far), ("row", across)))

    def begin(j):
        far_copy(j).start()
        near_copy(j).start()
        k, cols = columns_of(j, width, per)
        buf[j, far_bit, near_bit] = piece[k, :, cols]

    loop(chunks, begin)
    acc[...] = jnp.zeros_like(acc)
    dot = dot_nt if flip else dot_nn

    def add(j, half):
        both = buf[j, half].reshape(2 * rows, width)
        acc[half] = acc[half] + dot(both, wbuf[j])

    def here(j):
        near_copy(j).wait_recv()
        w_copy(j).wait()
        add(j, far_bit)

    loop(chunks, here)
    sendx[far_bit] = acc[far_bit].astype(bf16)
    cross(far_bit).start()

    def grad_copy(j):
        return grad_moves(j)

    if grad_mode == "wide":
        parts = grad_out.shape[0]

        def grad_moves(j):
            k, cols = columns_of(j, width, per)
            return pltpu.make_async_copy(
                stage.at[lax.rem(j, 2)], grad_out.at[:, k, :, cols], gsem.at[lax.rem(j, 2)]
            )

        def grad_part(j):
            block = buf[j].reshape(4 * rows, width)
            total = dot_nn(side[...], block).astype(bf16)
            stage[lax.rem(j, 2)] = total.reshape(stage.shape[1:])

    if grad_mode == "tall":

        def grad_moves(j):
            return pltpu.make_async_copy(
                stage.at[lax.rem(j, 2)],
                grad_out.at[pl.ds(pl.multiple_of(j * width, width), width), :],
                gsem.at[lax.rem(j, 2)],
            )

        def grad_part(j):
            block = buf[j].reshape(4 * rows, width)
            stage[lax.rem(j, 2)] = dot_nn(block.T, side[...]).astype(bf16)

    def pass_on(j):
        far_copy(j).wait_recv()
        relay(j).start()

    def there(j):
        relay(j).wait_recv()
        if not grad_mode:
            out_copy(j).start()
        add(j, 1 - far_bit)
        if grad_mode:

            @pl.when(j >= 2)
            def _():
                grad_moves(j - 2).wait()

            grad_part(j)
            grad_moves(j).start()

    pass_on(0)

    def both(j):
        pass_on(j + 1)
        there(j)

    loop(chunks - 1, both)
    there(chunks - 1)
    sendx[1 - far_bit] = acc[1 - far_bit].astype(bf16)
    cross(1 - far_bit).start()

    def settle(half):
        cross(half).wait_recv()
        prod[half] = sendx[half].astype(f32) + recvx[half].astype(f32)

    settle(far_bit)
    settle(1 - far_bit)

    def drain(j):
        near_copy(j).wait_send()
        far_copy(j).wait_send()
        relay(j).wait_send()
        if not grad_mode:
            out_copy(j).wait()

    loop(chunks, drain)
    cross(far_bit).wait_send()
    cross(1 - far_bit).wait_send()
    if grad_mode:
        for j in range(max(0, chunks - 2), chunks):
            grad_moves(j).wait()


def meet_product(piece, w, flip, width, collective, side=None, grad_mode=None, parts=1):
    pairs, rows, total = piece.shape
    features = w.shape[1]
    chunks = pairs * total // width
    tile = (features, width) if flip else (width, features)
    bf16, f32 = jnp.bfloat16, jnp.float32
    inputs, in_specs = (
        [piece, w],
        [pl.BlockSpec(memory_space=pltpu.VMEM), pl.BlockSpec(memory_space=pl.ANY)],
    )
    shapes = [jax.ShapeDtypeStruct((2, 2 * rows, features), f32)]
    out_specs = [pl.BlockSpec(memory_space=pltpu.VMEM)]
    scratch = [
        pltpu.VMEM((chunks,) + tile, bf16),
        pltpu.VMEM((chunks, 2, 2, rows, width), bf16),
        pltpu.VMEM((2, 2 * rows, features), f32),
        pltpu.VMEM((2, 2 * rows, features), bf16),
        pltpu.VMEM((2, 2 * rows, features), bf16),
    ]
    scratch += [pltpu.SemaphoreType.DMA((chunks,))] * 8 + [pltpu.SemaphoreType.DMA((2,))] * 2
    if grad_mode:
        inputs.append(side)
        in_specs.append(pl.BlockSpec(memory_space=pltpu.VMEM))
        out_specs.append(pl.BlockSpec(memory_space=pl.ANY))
        if grad_mode == "wide":
            shape = (parts, pairs, side.shape[0] // parts, total)
            stage = (2, parts, side.shape[0] // parts, width)
        else:
            shape = (total, side.shape[1])
            stage = (2, width, side.shape[1])
        shapes.append(jax.ShapeDtypeStruct(shape, bf16))
        scratch += [pltpu.VMEM(stage, bf16), pltpu.SemaphoreType.DMA((2,))]
    else:
        shapes.insert(0, jax.ShapeDtypeStruct((pairs, 2, 2, rows, total), bf16))
        out_specs.insert(0, pl.BlockSpec(memory_space=pl.ANY))
    result = pl.pallas_call(
        functools.partial(meet_kernel, flip, grad_mode),
        out_shape=tuple(shapes),
        in_specs=in_specs,
        out_specs=out_specs,
        scratch_shapes=scratch,
        compiler_params=pltpu.CompilerParams(
            collective_id=collective, has_side_effects=True, vmem_limit_bytes=56 * MIB
        ),
    )(*inputs)
    if grad_mode:
        return (result[0].reshape(4 * rows, features), result[1])
    return (result[0].reshape(pairs, 4 * rows, total), result[1].reshape(4 * rows, features))


def block_steps(x, acc, gram, poly):
    side, total = x.shape
    step = 256
    count = total // step
    span = 1280 if total % 1280 == 0 else step
    f32, bf16 = jnp.float32, jnp.bfloat16

    def tile(k, size):
        return pl.ds(pl.multiple_of(k * size, size), size)

    def square(k, total):
        values = x[:, tile(k, step)].astype(f32)
        return total + jnp.sum(values * values, axis=0, keepdims=True)

    sums = lax.fori_loop(0, count, square, jnp.zeros((1, step), f32))
    norm = jnp.sqrt(jnp.sum(sums, axis=1, keepdims=True)) + eps_frob

    def divide(k, carry):
        x[:, tile(k, step)] = (x[:, tile(k, step)].astype(f32) / norm).astype(bf16)
        return carry

    lax.fori_loop(0, count, divide, 0)

    def lap(k, carry):
        acc[...] = jnp.zeros_like(acc)

        def add(j, inner):
            block = x[:, tile(j, span)]
            acc[:step, :step] = acc[:step, :step] + dot_nt(block[:step], block[:step])
            acc[step:, :] = acc[step:, :] + dot_nt(block[step:], block)
            return inner

        lax.fori_loop(0, total // span, add, 0)
        acc[:step, step:] = acc[step:, :step].T
        low = acc[...].astype(bf16)
        gram[...] = low
        square_gram = dot_nn(low, gram[...])
        poly[...] = (poly_second * low.astype(f32) + poly_third * square_gram).astype(bf16)

        def advance(j, inner):
            block = x[:, tile(j, span)]
            fresh = poly_first * block.astype(f32) + dot_nn(poly[...], block)
            x[:, tile(j, span)] = fresh.astype(bf16)
            return inner

        lax.fori_loop(0, total // span, advance, 0)
        return carry

    lax.fori_loop(0, 5, lap, 0)


def work_space(side):
    return [
        pltpu.VMEM((side, side), jnp.float32),
        pltpu.VMEM((side, side), jnp.bfloat16),
        pltpu.VMEM((side, side), jnp.bfloat16),
    ]


def gates_kernel(conv, first, second, out, full, came, send_sem, recv_sem):
    me = lax.axis_index("col")
    count = out.shape[0]
    greet([("col", lax.rem(me + step, 4)) for step in range(1, 4)])
    for k, grads in enumerate((first, second)):
        for head in range(conv.shape[1] // HS):
            columns = slice(head * HS, (head + 1) * HS)
            block = dot_nn(conv[:, columns].T, grads[:, columns])
            full[k * HS : (k + 1) * HS, columns] = block.astype(jnp.bfloat16)

    def part(place):
        return full.at[pl.ds(pl.multiple_of(place * count, count), count)]

    def copy(step):
        target = lax.rem(me + step, 4)
        return pltpu.make_async_remote_copy(
            src_ref=part(target),
            dst_ref=came.at[step - 1],
            send_sem=send_sem.at[step - 1],
            recv_sem=recv_sem.at[step - 1],
            device_id={"col": target},
            device_id_type=MESH,
        )

    for step in range(1, 4):
        copy(step).start()
    total = part(me)[...].astype(jnp.float32)
    for step in range(1, 4):
        copy(step).wait_recv()
        total = total + came[step - 1].astype(jnp.float32)
    out[...] = total.astype(jnp.bfloat16)
    for step in range(1, 4):
        copy(step).wait_send()


def gates_product(conv, first, second):
    lanes = conv.shape[1]
    count = 2 * HS // 4
    bf16 = jnp.bfloat16
    return pl.pallas_call(
        gates_kernel,
        out_shape=jax.ShapeDtypeStruct((count, lanes), bf16),
        in_specs=[pl.BlockSpec(memory_space=pltpu.VMEM)] * 3,
        out_specs=pl.BlockSpec(memory_space=pltpu.VMEM),
        scratch_shapes=[
            pltpu.VMEM((2 * HS, lanes), bf16),
            pltpu.VMEM((3, count, lanes), bf16),
            pltpu.SemaphoreType.DMA((3,)),
            pltpu.SemaphoreType.DMA((3,)),
        ],
        compiler_params=pltpu.CompilerParams(
            collective_id=12, has_side_effects=True, vmem_limit_bytes=16 * MIB
        ),
    )(conv, first, second)


def token_total(values):
    return lax.psum(values, "col")


def dp_sum(grad):
    low = grad.astype(jnp.bfloat16)
    return lax.psum_scatter(low, "dp", scatter_dimension=0, tiled=True).astype(jnp.float32)


def pair_sum(grad, dp_count):
    if grad.shape[0] == dp_count:
        return lax.psum_scatter(grad, "dp", scatter_dimension=0)
    return lax.psum_scatter(grad[0], "dp", scatter_dimension=1, tiled=True)


def owner_send(block, root):
    return broadcast(block, "dp", root)


def norm_forward(stream, gain, width):
    total = token_total(jnp.sum(stream * stream, axis=1))
    scale = lax.rsqrt(total / width + eps_norm)
    return (scale, stream * scale[:, None] * gain[None, :])


def norm_backward(stream, scale, gain, grad_normed, width):
    weighted = grad_normed * gain[None, :]
    inner = token_total(jnp.sum(stream * weighted, axis=1))
    grad_stream = (
        scale[:, None] * weighted - stream * (scale * scale * scale * inner / width)[:, None]
    )
    grad_gain = jnp.sum(grad_normed * stream * scale[:, None], axis=0)
    return (grad_stream, grad_gain)


def orthogonalize(block):
    work = block
    values = work.astype(jnp.float32)
    work = (values / (jnp.sqrt(jnp.sum(values * values)) + eps_frob)).astype(jnp.bfloat16)
    for step in range(5):
        gram = product_nt(work, work).astype(jnp.bfloat16)
        poly = (poly_second * gram.astype(jnp.float32) + poly_third * product(gram, gram)).astype(
            jnp.bfloat16
        )
        work = (poly_first * work.astype(jnp.float32) + product(poly, work)).astype(jnp.bfloat16)
    return work


def owner_results(blocks, dp_place, dp_count):
    results = [None, None, None, None, None, None]
    for members in ((0, 1, 2), (3, 4, 5)):
        flipped = [blocks[number].shape[0] > blocks[number].shape[1] for number in members]
        wide = [
            blocks[number].T if turn else blocks[number] for number, turn in zip(members, flipped)
        ]
        chosen = wide[0]
        for number, candidate in zip(members[1:], wide[1:]):
            chosen = jnp.where(dp_place == number % dp_count, candidate, chosen)
        done = orthogonalize(chosen)
        for number, turn in zip(members, flipped):
            kept = jnp.where(dp_place == number % dp_count, done, jnp.zeros_like(done))
            results[number] = kept.T if turn else kept
    return results


def dp_moves(moves, sems):
    local_sem, send_sem, recv_sem = sems
    me = lax.axis_index("dp")

    def remote(k, sender, target):
        pairs, source, destination = moves[k]
        return pltpu.make_async_remote_copy(
            src_ref=source(sender, target),
            dst_ref=destination(sender, target),
            send_sem=send_sem.at[k, target],
            recv_sem=recv_sem.at[k, sender],
            device_id={"dp": target},
            device_id_type=MESH,
        )

    def local(k, place):
        pairs, source, destination = moves[k]
        return pltpu.make_async_copy(
            source(place, place), destination(place, place), local_sem.at[k]
        )

    def each(chosen, act):
        for k in chosen:
            for sender, target in moves[k][0]:
                act(k, sender, target)

    def start_one(k, sender, target):
        @pl.when(me == sender)
        def _():
            if sender == target:
                local(k, sender).start()
            else:
                remote(k, sender, target).start()

    def arrive_one(k, sender, target):
        @pl.when(me == target)
        def _():
            if sender == target:
                local(k, sender).wait()
            else:
                remote(k, sender, target).wait_recv()

    def sent_one(k, sender, target):
        if sender != target:

            @pl.when(me == sender)
            def _():
                remote(k, sender, target).wait_send()

    return (
        lambda *chosen: each(chosen, start_one),
        lambda *chosen: each(chosen, arrive_one),
        lambda *chosen: each(chosen, sent_one),
    )


def rows_at(ref, place):
    def pick(sender, target):
        index = sender if place == "sender" else target
        count = ref.shape[0] // 4
        return ref.at[pl.ds(index * count, count)]

    return pick


def entry(ref, place):
    return lambda sender, target: ref.at[sender if place == "sender" else target]


def whole(ref):
    return lambda sender, target: ref


def to_owner(owner):
    return [(sender, owner) for sender in ((owner + step) % 4 for step in range(4))]


def from_owner(owner):
    return [(owner, target) for target in ((owner + step) % 4 for step in range(4))]


SMALL_OWNER, CON_OWNER, GATE_OWNER, UP_OWNER = (0, 1, 2, 3)


def pieces_at_owner(e0, e1, con, later):
    me = lax.axis_index("dp")
    rows = e0.shape[0]
    packed = jnp.concatenate(
        [con[k * rows : (k + 1) * rows] for k in range(con.shape[0] // rows)], axis=1
    )

    def piece_for(owner):
        return jnp.where(owner == GATE_OWNER, e0, jnp.where(owner == UP_OWNER, e1, packed))

    leaving = [piece_for(lax.rem(me + step, 4)) for step in range(4)]
    leaving, later = lax.optimization_barrier((leaving, later))
    pieces = leaving[:1]
    for step in range(1, 4):
        pairs = [(sender, (sender + step) % 4) for sender in range(4)]
        pairs = [pair for pair in pairs if pair[1] != SMALL_OWNER]
        pieces.append(lax.ppermute(leaving[step], "dp", pairs))
    return (pieces, later)


def share_parts(axis, buf, send_sem, recv_sem):
    me = lax.axis_index(axis)

    def copy(step):
        return pltpu.make_async_remote_copy(
            src_ref=buf.at[me],
            dst_ref=buf.at[me],
            send_sem=send_sem.at[step],
            recv_sem=recv_sem.at[step],
            device_id={axis: lax.rem(me + step, 4)},
            device_id_type=MESH,
        )

    def start(value):
        buf[me] = value
        for step in range(1, 4):
            copy(step).start()

    def arrive():
        for step in range(1, 4):
            copy(step).wait_recv()

    def finish():
        for step in range(1, 4):
            copy(step).wait_send()

    return (start, arrive, finish)


def tail_kernel(*refs):
    large, (b0, b1, out) = refs[:4], refs[4:7]
    gates_piece, col_part, dp_part = refs[7:10]
    e0_o, e1_o, con_o, b0_o, b1_o, out_o, gates_o, col_o, dp_o = refs[10:19]
    x, packed, pieces, first, second, third, out_v, acc, gram, poly, load_sem = refs[19:30]
    col_buf, dp_buf, gates_dp, gates_col = refs[30:34]
    shares = [
        share_parts("col", col_buf, *refs[34:36]),
        share_parts("dp", dp_buf, *refs[36:38]),
        share_parts("dp", gates_dp, *refs[38:40]),
        share_parts("col", gates_col, *refs[40:42]),
    ]
    sems = refs[42:]
    place = lax.axis_index("col")
    me = lax.axis_index("dp")
    small = out.shape[0]
    width = pieces.shape[1]
    side = x.shape[0]
    rows = side // 4
    moves = [
        (to_owner(SMALL_OWNER), whole(b0), rows_at(first, "sender")),
        (to_owner(SMALL_OWNER), whole(b1), rows_at(second, "sender")),
        (to_owner(SMALL_OWNER), whole(out), entry(out_v, "sender")),
        (from_owner(GATE_OWNER), rows_at(x, "target"), whole(e0_o)),
        (from_owner(UP_OWNER), rows_at(x, "target"), whole(e1_o)),
        (from_owner(CON_OWNER), entry(pieces, "target"), whole(con_o)),
        (from_owner(SMALL_OWNER), rows_at(first, "target"), whole(b0_o)),
        (from_owner(SMALL_OWNER), rows_at(second, "target"), whole(b1_o)),
        (from_owner(SMALL_OWNER), entry(out_v, "target"), whole(out_o)),
    ]
    start, arrive, sent = dp_moves(moves, sems)
    greet(
        [("dp", lax.rem(me + step, 4)) for step in range(1, 4)]
        + [("col", lax.rem(place + step, 4)) for step in range(1, 4)]
    )
    shares[0][0](col_part[...])
    shares[2][0](gates_piece[...])
    start(0, 1, 2)
    shares[0][1]()
    summed = col_buf[0] + col_buf[1] + col_buf[2] + col_buf[3]
    col_o[...] = summed
    shares[1][0](jnp.concatenate([summed[:8], dp_part[...]], axis=0))
    shares[2][1]()
    shares[3][0](gates_dp[...].reshape(gates_col.shape[1:]))

    def load(owner, target):
        copies = [
            pltpu.make_async_copy(large[step], target((owner - step) % 4), load_sem.at[step])
            for step in range(4)
        ]
        for copy in copies:
            copy.start()
        for copy in copies:
            copy.wait()

    @pl.when(me == CON_OWNER)
    def _():
        load(CON_OWNER, lambda j: packed.at[j])
        for j in range(4):
            for k in range(width // rows):
                first_column = j * width + k * rows
                x[:, first_column : first_column + rows] = packed[j, :, k * side : (k + 1) * side].T

    @pl.when(me == GATE_OWNER)
    def _():
        load(GATE_OWNER, lambda j: x.at[pl.ds(j * rows, rows)])

    @pl.when(me == UP_OWNER)
    def _():
        load(UP_OWNER, lambda j: x.at[pl.ds(j * rows, rows)])

    @pl.when(me != SMALL_OWNER)
    def _():
        block_steps(x, acc, gram, poly)

    @pl.when(me == CON_OWNER)
    def _():
        for j in range(4):
            pieces[j] = x[:, j * width : (j + 1) * width].T

    start(3, 4, 5)
    for k, part in enumerate((first, second, third)):
        arrive(k)

        @pl.when(me == SMALL_OWNER)
        def _():
            if k == 2:
                for j in range(4):
                    part[:, j * small : (j + 1) * small] = out_v[j].T
            block_steps(part, acc, gram, poly)
            if k == 2:
                for j in range(4):
                    out_v[j] = part[:, j * small : (j + 1) * small].T

        start(6 + k)
    shares[1][1]()
    dp_o[...] = dp_buf[0] + dp_buf[1] + dp_buf[2] + dp_buf[3]
    shares[3][1]()
    gates_o[...] = gates_col[...].reshape(gates_o.shape)
    arrive(6, 7, 8, 3, 4, 5)
    sent(0, 1, 2, 3, 4, 5, 6, 7, 8)
    for share in shares:
        share[2]()


def finish_blocks(large, con_shape, b0, b1, out, gates_piece, col_part, dp_part):
    piece = large[0].shape
    rows, total = piece
    side = 4 * rows
    f32, bf16 = jnp.float32, jnp.bfloat16
    shape = jax.ShapeDtypeStruct
    small = pltpu.VMEM((side, b0.shape[1]), bf16)
    quarter = (4 * gates_piece.shape[0], gates_piece.shape[1])
    anywhere = pl.BlockSpec(memory_space=pl.ANY)
    local = pl.BlockSpec(memory_space=pltpu.VMEM)
    sems = pltpu.SemaphoreType.DMA
    shapes = [shape(s, bf16) for s in (piece, piece, con_shape, b0.shape, b1.shape, out.shape)]
    shapes += [shape((4 * quarter[0], quarter[1]), bf16), shape(col_part.shape, f32)]
    shapes += [shape(col_part.shape, f32)]
    return pl.pallas_call(
        tail_kernel,
        out_shape=tuple(shapes),
        in_specs=[anywhere] * 7 + [local] * 3,
        out_specs=[anywhere] * 6 + [local] * 3,
        scratch_shapes=[
            pltpu.VMEM((side, total), bf16),
            pltpu.VMEM((4,) + piece, bf16),
            pltpu.VMEM((4,) + con_shape, bf16),
            small,
            small,
            small,
            pltpu.VMEM((4,) + out.shape, bf16),
        ]
        + work_space(side)
        + [sems((4,))]
        + [
            pltpu.VMEM((4,) + col_part.shape, f32),
            pltpu.VMEM((4,) + col_part.shape, f32),
            pltpu.VMEM((4,) + gates_piece.shape, bf16),
            pltpu.VMEM((4,) + quarter, bf16),
        ]
        + [sems((4,))] * 8
        + [sems((9,)), sems((9, 4)), sems((9, 4))],
        compiler_params=pltpu.CompilerParams(
            collective_id=0, has_side_effects=True, vmem_limit_bytes=40 * MIB
        ),
    )(*large, b0, b1, out, gates_piece, col_part, dp_part)


def grouped_step(grad, moment, weight, rate):
    new_moment = momentum_rate * moment + grad
    rows, cols = new_moment.shape
    grouped = new_moment.reshape(rows, cols // GROUP, GROUP)
    norm_sq = jnp.mean(grouped * grouped, axis=2, keepdims=True)
    update = (grouped * lax.rsqrt(norm_sq + eps_norm)).reshape(rows, cols)
    return (new_moment, weight - rate * update)


def shards(
    block_input,
    segment_ids,
    output_cotangent,
    norm_gains,
    branch_weights,
    mixer_vectors,
    gate_blocks,
    output_weights,
    expand_weights,
    contract_weights,
    gains_momentum,
    branch_momentum,
    vectors_momentum,
    gates_momentum,
    output_momentum,
    expand_momentum,
    contract_momentum,
):
    f32 = jnp.float32
    bf16 = jnp.bfloat16
    col_count = lax.axis_size("col")
    col_place = lax.axis_index("col")
    dp_count = lax.axis_size("dp")
    dp_place = lax.axis_index("dp")
    group_rows = block_input.shape[0]
    rows = group_rows // col_count
    lanes = mixer_vectors.shape[1]
    heads_here = lanes // HS
    feature_count = block_input.shape[1]
    width = feature_count * col_count
    first_row = col_place * rows
    reach = CONV - 1
    seg_row = segment_ids[0]
    seg_ext = jnp.concatenate(
        [jnp.full((reach,), -1, jnp.int32), seg_row, jnp.full((reach,), -2, jnp.int32)]
    )
    seg_here = lax.dynamic_slice_in_dim(seg_ext, first_row + reach, rows + reach)
    masks = []
    for shift in range(CONV):
        earlier = lax.dynamic_slice_in_dim(seg_ext, first_row + reach - shift, rows + reach)
        masks.append((earlier == seg_here).astype(f32))
    reset_rows = masks[1][:rows] < 0.5
    stream = block_input.astype(f32)
    scale_one, normed_one = norm_forward(stream, norm_gains[0], width)
    normed_low = normed_one.astype(bf16)

    branch_pre = spread_product(normed_low, branch_weights, False, 640, 2)
    contract_term = product_nt(output_cotangent, contract_weights).astype(bf16)
    contract_term, branch_pre = lax.optimization_barrier((contract_term, branch_pre))
    grad_activated = lax.psum_scatter(contract_term, "col", scatter_dimension=0, tiled=True)
    mixed = branch_pre[0]
    gelu_in = branch_pre[1]
    edge = from_behind(mixed[rows - reach :], "col", 1)
    extended = jnp.concatenate([edge, mixed], axis=0)
    windows = []
    conv_out = jnp.zeros((rows, lanes), f32) + mixer_vectors[CONV][None, :]
    for shift in range(CONV):
        window = extended[reach - shift : reach - shift + rows] * masks[shift][:rows, None]
        windows.append(window)
        conv_out = conv_out + mixer_vectors[shift][None, :] * window
    conv_low = conv_out.astype(bf16).reshape(rows, heads_here, HS)
    gate_pre = jnp.einsum(
        "thi,ghij->tghj", conv_low, gate_blocks, preferred_element_type=f32
    ).reshape(rows, 2, lanes)
    gate_pre = gate_pre + mixer_vectors[CONV + 1 : CONV + 3][None]

    def recurrence_terms(conv_values, gate_values, rate_values):
        input_gate = jax.nn.sigmoid(gate_values[:, 0])
        decay_gate = jax.nn.sigmoid(gate_values[:, 1])
        log_decay = -decay_scale * decay_gate * jax.nn.softplus(rate_values)[None, :]
        inject_scale = jnp.where(reset_rows[:, None], 1.0, jnp.sqrt(1.0 - jnp.exp(2.0 * log_decay)))
        decay_values = jnp.where(reset_rows[:, None], 0.0, jnp.exp(log_decay))
        return (decay_values, inject_scale * input_gate * conv_values)

    (decay, inject), pull_terms = jax.vjp(
        recurrence_terms, conv_out, gate_pre, mixer_vectors[CONV + 3]
    )
    local_a, local_b = linear_scan(decay, inject, False)
    identity = (jnp.ones((lanes,), f32), jnp.zeros((lanes,), f32))
    incoming = prefix((local_a[-1], local_b[-1]), "col", link, identity, False)
    carried = incoming[1]
    state = local_a * carried[None, :] + local_b
    gelu_out, pull_gelu = jax.vjp(gelu_tanh, gelu_in)
    hidden = (gelu_out * state).astype(bf16)
    hidden_all, branch_out = meet_product(hidden[None], output_weights, False, 256, 3)
    middle = stream + branch_out
    scale_two, normed_two = norm_forward(middle, norm_gains[1], width)
    normed_two_low = normed_two.astype(bf16)

    expand_pre = spread_product(normed_two_low, expand_weights, False, 768, 4)

    def geglu(gate_values, up_values):
        return gelu_tanh(gate_values) * up_values

    activated, pull_geglu = jax.vjp(geglu, expand_pre[0], expand_pre[1])
    activated_low = activated.astype(bf16)
    contracted, contract_grad = meet_product(
        activated_low[None], contract_weights, False, 768, 5, output_cotangent, "tall"
    )
    block_output = (middle + contracted).astype(bf16)
    cot_values = output_cotangent.astype(f32)
    grad_activated = grad_activated.astype(f32)
    grad_gate, grad_up = pull_geglu(grad_activated)
    grad_expand_low = jnp.stack([grad_gate, grad_up]).astype(bf16)
    grad_expand_low, contract_grad = lax.optimization_barrier((grad_expand_low, contract_grad))
    parts = dp_count if feature_count % (16 * dp_count) == 0 else 1
    grad_normed_two, expand_grad = meet_product(
        grad_expand_low, expand_weights, True, 768, 7, normed_two_low.T, "wide", parts
    )
    grad_middle_norm, gain_two_grad = norm_backward(
        middle, scale_two, norm_gains[1], grad_normed_two, width
    )
    grad_middle = cot_values + grad_middle_norm
    grad_branch_low = grad_middle.astype(bf16)
    output_grad = product_tn(hidden_all[0], grad_branch_low)
    grad_hidden = spread_product(grad_branch_low, output_weights, True, 256, 8)[0]
    grad_state = grad_hidden * gelu_out
    (grad_gelu_in,) = pull_gelu(grad_hidden * state)
    shifted_decay = jnp.concatenate([decay[1:], jnp.ones((1, lanes), f32)], axis=0)
    back_a, back_b = linear_scan(shifted_decay, grad_state, True)
    from_later = prefix((decay[0] * back_a[0], decay[0] * back_b[0]), "col", link, identity, True)
    grad_total = back_a * from_later[1][None, :] + back_b
    previous = jnp.concatenate([carried[None, :], state[:-1]], axis=0)
    grad_conv_direct, grad_gate_pre, grad_rate = pull_terms((grad_total * previous, grad_total))
    grad_gate_low = grad_gate_pre.astype(bf16)
    grad_gate_heads = grad_gate_low.reshape(rows, 2, heads_here, HS)
    grad_conv = grad_conv_direct + jnp.einsum(
        "tghj,ghij->thi", grad_gate_heads, gate_blocks, preferred_element_type=f32
    ).reshape(rows, lanes)
    parts = dp_count if feature_count % (16 * dp_count) == 0 else 1
    planes = dp_count == 4 and parts == 4 and 2 * feature_count <= lanes and group_rows <= lanes
    gate_bias_grad = jnp.sum(grad_gate_low.astype(f32), axis=0)
    after = from_behind(grad_conv[:reach], "col", -1)
    grad_conv_ext = jnp.concatenate([grad_conv, after], axis=0)
    grad_mixed = jnp.zeros((rows, lanes), f32)
    tap_grads = []
    for shift in range(CONV):
        masked = grad_conv_ext * masks[shift][:, None]
        grad_mixed = grad_mixed + mixer_vectors[shift][None, :] * masked[shift : shift + rows]
        tap_grads.append(jnp.sum(grad_conv * windows[shift], axis=0))
    vector_rows = tap_grads + [
        jnp.sum(grad_conv, axis=0),
        gate_bias_grad[0],
        gate_bias_grad[1],
        grad_rate,
    ]
    vectors_grad = jnp.stack(vector_rows)
    grad_branch_pre = jnp.stack([grad_mixed, grad_gelu_in]).astype(bf16)
    grad_normed_one, branch_grad = meet_product(
        grad_branch_pre, branch_weights, True, 640, 9, normed_low.T, "wide", parts
    )
    weights_full = (
        branch_weights[0],
        branch_weights[1],
        output_weights,
        expand_weights[0],
        expand_weights[1],
        contract_weights,
    )
    if planes:
        contract_sum = pair_sum(contract_grad.reshape((4, -1) + contract_grad.shape[1:]), 4)
        expand_grad, contract_sum = lax.optimization_barrier((expand_grad, contract_sum))
        expand_sum = pair_sum(expand_grad, 4)
        con_low = (momentum_rate * contract_momentum[0] + contract_sum).astype(bf16)
        weighted = grad_normed_one * norm_gains[0][None, :]
        inner_part = jnp.sum(stream * weighted, axis=1)
        gain_one_grad = jnp.sum(grad_normed_one * stream * scale_one[:, None], axis=0)
        col_part = jnp.concatenate(
            [
                vectors_grad,
                jnp.pad(inner_part, (0, lanes - group_rows))[None],
                jnp.zeros((7, lanes), f32),
            ]
        )
        gains_row = jnp.concatenate([gain_one_grad, gain_two_grad])
        dp_part = jnp.pad(gains_row[None], ((0, 7), (0, lanes - 2 * feature_count)))
        gates_part = gates_product(
            conv_low.reshape(rows, lanes), grad_gate_low[:, 0], grad_gate_low[:, 1]
        )
        piece_rows = branch_grad.shape[2]
        small_grad = jnp.concatenate(
            [
                branch_grad.reshape(4, 2 * piece_rows, lanes),
                output_grad.astype(bf16).reshape(4, piece_rows, lanes),
                gates_part.reshape(4, -1, lanes),
            ],
            axis=1,
        )
        con_low, expand_sum, col_part, dp_part, small_grad = lax.optimization_barrier(
            (con_low, expand_sum, col_part, dp_part, small_grad)
        )
        expand_low = (momentum_rate * expand_momentum[:, 0] + expand_sum).astype(bf16)
        small_grad, expand_sum = lax.optimization_barrier((small_grad, expand_sum))
        large, (expand_sum, contract_sum) = pieces_at_owner(
            expand_low[0], expand_low[1], con_low, (expand_sum, contract_sum)
        )
        small_sum = pair_sum(small_grad, 4)
        branch_sum = small_sum[: 2 * piece_rows].reshape(2, piece_rows, lanes)
        output_sum = small_sum[2 * piece_rows : 3 * piece_rows].reshape(output_momentum.shape[1:])
        branch_low = (momentum_rate * branch_momentum[:, 0] + branch_sum).astype(bf16)
        output_low = (momentum_rate * output_momentum[0] + output_sum).astype(bf16)
        e0, e1, con, b0, b1, out, gates_all, col_total, dp_total = finish_blocks(
            large,
            con_low.shape,
            branch_low[0],
            branch_low[1],
            output_low,
            small_sum[3 * piece_rows :],
            col_part,
            dp_part,
        )
        pieces = [piece.astype(f32) for piece in (b0, b1, out, e0, e1, con)]
        output_sum = output_sum.astype(f32)
        gates_total = gates_all.reshape(2, HS, heads_here, HS).transpose(0, 2, 1, 3).astype(f32)
        vectors_total = dp_total[:8]
        gains_total = dp_total[8, : 2 * feature_count].reshape(2, feature_count)
        inner = col_total[8, :group_rows]
        grad_stream_norm = (
            scale_one[:, None] * weighted
            - stream * (scale_one * scale_one * scale_one * inner / width)[:, None]
        )
    else:
        grad_stream_norm, gain_one_grad = norm_backward(
            stream, scale_one, norm_gains[0], grad_normed_one, width
        )
        vectors_total, gains_total = lax.psum(
            (lax.psum(vectors_grad, "col"), jnp.stack([gain_one_grad, gain_two_grad])), "dp"
        )
        gates_grad = jnp.einsum(
            "thi,tghj->ghij", conv_low, grad_gate_heads, preferred_element_type=f32
        ).astype(bf16)
        branch_sum = pair_sum(branch_grad, dp_count)
        expand_sum = pair_sum(expand_grad, dp_count)
        output_sum = dp_sum(output_grad)
        contract_sum = dp_sum(contract_grad)
        gates_total = lax.psum(gates_grad, ("dp", "col")).astype(f32)
        pieces = None
    input_grad = (grad_middle + grad_stream_norm).astype(bf16)
    branch_sum = branch_sum.astype(f32)
    expand_sum = expand_sum.astype(f32)
    contract_sum = contract_sum.astype(f32)
    summed = (
        branch_sum[0],
        branch_sum[1],
        output_sum,
        expand_sum[0],
        expand_sum[1],
        contract_sum,
    )
    moments_old = (
        branch_momentum[0, 0],
        branch_momentum[1, 0],
        output_momentum[0],
        expand_momentum[0, 0],
        expand_momentum[1, 0],
        contract_momentum[0],
    )
    moments_new = tuple(momentum_rate * old + fresh for old, fresh in zip(moments_old, summed))
    block_shapes = [
        (summed[number].shape[0] * dp_count, summed[number].shape[1]) for number in range(6)
    ]
    if pieces is None:
        lows = [moment.astype(bf16) for moment in moments_new]
        gathered = [lax.all_gather(low, "dp", axis=0, tiled=True) for low in lows]
        orth = owner_results(gathered, dp_place, dp_count)
        pieces = [
            lax.dynamic_slice_in_dim(
                owner_send(orth[number], number % dp_count),
                dp_place * summed[number].shape[0],
                summed[number].shape[0],
                0,
            ).astype(f32)
            for number in range(6)
        ]
    new_pieces = []
    for number in range(6):
        block_rows, block_cols = block_shapes[number]
        piece_rows = summed[number].shape[0]
        weight_piece = lax.dynamic_slice_in_dim(
            weights_full[number], dp_place * piece_rows, piece_rows, 0
        ).astype(f32)
        new_pieces.append(
            weight_piece - muon_rate * max(1.0, block_rows / block_cols) ** 0.5 * pieces[number]
        )
    gates_moment = momentum_rate * gates_momentum + gates_total
    gate_sq = jnp.mean(gates_moment * gates_moment, axis=(2, 3), keepdims=True)
    gates_new = gate_blocks.astype(f32) - gate_rate * gates_moment * lax.rsqrt(gate_sq + eps_norm)
    vectors_moment, vectors_new = grouped_step(
        vectors_total, vectors_momentum, mixer_vectors, vector_rate
    )
    gains_moment, gains_new = grouped_step(gains_total, gains_momentum, norm_gains, vector_rate)
    return (
        block_output,
        input_grad,
        gains_total,
        jnp.stack([summed[0], summed[1]])[:, None],
        vectors_total,
        gates_total,
        summed[2][None],
        jnp.stack([summed[3], summed[4]])[:, None],
        summed[5][None],
        gains_new,
        jnp.stack([new_pieces[0], new_pieces[1]])[:, None],
        vectors_new,
        gates_new,
        new_pieces[2][None],
        jnp.stack([new_pieces[3], new_pieces[4]])[:, None],
        new_pieces[5][None],
        gains_moment,
        jnp.stack([moments_new[0], moments_new[1]])[:, None],
        vectors_moment,
        gates_moment,
        moments_new[2][None],
        jnp.stack([moments_new[3], moments_new[4]])[:, None],
        moments_new[5][None],
    )


def solution(mesh):
    return jax.shard_map(
        shards,
        mesh=mesh,
        in_specs=(
            P("dp", "col"),
            P("dp", None),
            P("dp", "col"),
            P(None, "col"),
            P(None, "col", "row"),
            P(None, "row"),
            P(None, "row", None, None),
            P("row", "col"),
            P(None, "col", "row"),
            P("row", "col"),
            P(None, "col"),
            P(None, "col", "dp", "row"),
            P(None, "row"),
            P(None, "row", None, None),
            P("row", "dp", "col"),
            P(None, "col", "dp", "row"),
            P("row", "dp", "col"),
        ),
        out_specs=(
            P("dp", "col"),
            P("dp", "col"),
            P(None, "col"),
            P(None, "col", "dp", "row"),
            P(None, "row"),
            P(None, "row", None, None),
            P("row", "dp", "col"),
            P(None, "col", "dp", "row"),
            P("row", "dp", "col"),
            P(None, "col"),
            P(None, "col", "dp", "row"),
            P(None, "row"),
            P(None, "row", None, None),
            P("row", "dp", "col"),
            P(None, "col", "dp", "row"),
            P("row", "dp", "col"),
            P(None, "col"),
            P(None, "col", "dp", "row"),
            P(None, "row"),
            P(None, "row", None, None),
            P("row", "dp", "col"),
            P(None, "col", "dp", "row"),
            P("row", "dp", "col"),
        ),
        check_vma=False,
    )
```

```python
import functools

import jax
import jax.numpy as jnp
from jax import lax
from jax.experimental import pallas as pl
from jax.experimental.pallas import tpu as pltpu
from jax.sharding import PartitionSpec as P

CONV = 4
GROUP = 128
HS = 256


eps_norm = 1e-06
eps_frob = 1e-07
poly_first = 3.4445
poly_second = -4.775
poly_third = 2.0315
momentum_rate = 0.9
muon_rate = 0.1
gate_rate = 0.02
vector_rate = 0.3
decay_scale = 8.0


def broadcast(value, axis, source):
    kept = jnp.where(lax.axis_index(axis) == source, value, 0).astype(value.dtype)
    return lax.psum(kept, axis)


def from_behind(value, axis, steps):
    count = lax.axis_size(axis)
    initial, last = (max(0, -steps), min(count, count - steps))
    return lax.ppermute(value, axis, [(source, source + steps) for source in range(initial, last)])


def prefix(value, axis, combine, identity, reverse):
    count, here = (lax.axis_size(axis), lax.axis_index(axis))
    joined = lax.all_gather(jnp.stack(value), axis)
    everything = tuple(joined[:, k] for k in range(len(value)))
    start = jax.tree.map(
        lambda part, zero: jnp.broadcast_to(jnp.asarray(zero, part.dtype), part.shape),
        value,
        identity,
    )

    def lap(k, before):
        at = count - 1 - k if reverse else k
        reached = at > here if reverse else at < here
        new = combine(before, jax.tree.map(lambda part: part[at], everything))
        return jax.tree.map(lambda a, b: jnp.where(reached, a, b), new, before)

    return lax.fori_loop(0, count, lap, start)


def gelu_tanh(value):
    return jax.nn.gelu(value, approximate=True)


def product(left, right):
    return jnp.dot(left, right, preferred_element_type=jnp.float32)


def product_tn(left, right):
    return lax.dot_general(
        left, right, (((0,), (0,)), ((), ())), preferred_element_type=jnp.float32
    )


def product_nt(left, right):
    return lax.dot_general(
        left, right, (((1,), (1,)), ((), ())), preferred_element_type=jnp.float32
    )


def link(first, second):
    return (first[0] * second[0], second[0] * first[1] + second[1])


def scan_kernel(reverse, decay_ref, value_ref, prod_ref, sum_ref):
    rows, lanes = decay_ref.shape
    groups = rows // 8

    def lap(k, carry):
        base = pl.multiple_of((groups - 1 - k if reverse else k) * 8, 8)
        decay = decay_ref[pl.ds(base, 8), :]
        value = value_ref[pl.ds(base, 8), :]
        prod, total = carry
        prods, totals = [None] * 8, [None] * 8
        for j in range(7, -1, -1) if reverse else range(8):
            prod = decay[j : j + 1] * prod
            total = decay[j : j + 1] * total + value[j : j + 1]
            prods[j], totals[j] = prod, total
        prod_ref[pl.ds(base, 8), :] = jnp.concatenate(prods, axis=0)
        sum_ref[pl.ds(base, 8), :] = jnp.concatenate(totals, axis=0)
        return (prod, total)

    start = (jnp.ones((1, lanes), jnp.float32), jnp.zeros((1, lanes), jnp.float32))
    lax.fori_loop(0, groups, lap, start)


def linear_scan(decay, value, reverse):
    shape = jax.ShapeDtypeStruct(decay.shape, jnp.float32)
    return pl.pallas_call(
        functools.partial(scan_kernel, reverse),
        out_shape=(shape, shape),
        compiler_params=pltpu.CompilerParams(vmem_limit_bytes=16 * 1024 * 1024),
    )(decay, value)


MESH = pl.DeviceIdType.MESH
MIB = 1024 * 1024


def col_places():
    me = lax.axis_index("col")
    near_bit = lax.rem(me, 2)
    far_bit = lax.div(me, 2)
    return (me, near_bit, far_bit, me + 1 - 2 * near_bit, lax.rem(me + 2, 4))


def greet(axis_places):
    barrier = pltpu.get_barrier_semaphore()
    for axis, place in axis_places:
        pl.semaphore_signal(barrier, inc=1, device_id={axis: place}, device_id_type=MESH)
    pl.semaphore_wait(barrier, len(axis_places))


def dot_nn(left, right):
    return lax.dot_general(
        left, right, (((1,), (0,)), ((), ())), preferred_element_type=jnp.float32
    )


def dot_nt(left, right):
    return lax.dot_general(
        left, right, (((1,), (1,)), ((), ())), preferred_element_type=jnp.float32
    )


def columns_of(j, width, per):
    return (lax.div(j, per), pl.ds(pl.multiple_of(lax.rem(j, per) * width, width), width))


def share_parts(axis, buf, send_sem, recv_sem):
    me = lax.axis_index(axis)

    def copy(step):
        return pltpu.make_async_remote_copy(
            src_ref=buf.at[me],
            dst_ref=buf.at[me],
            send_sem=send_sem.at[step],
            recv_sem=recv_sem.at[step],
            device_id={axis: lax.rem(me + step, 4)},
            device_id_type=MESH,
        )

    def start(value):
        buf[me] = value
        for step in range(1, 4):
            copy(step).start()

    def arrive():
        for step in range(1, 4):
            copy(step).wait_recv()

    def finish():
        for step in range(1, 4):
            copy(step).wait_send()

    return (start, arrive, finish)


def col_peers():
    me = lax.axis_index("col")
    return [("col", lax.rem(me + step, 4)) for step in range(1, 4)]


def row_scales(values, share, buf):
    tokens, features = values.shape
    start, arrive, finish = share
    squares = jnp.sum(values * values, axis=1, keepdims=True)
    start(jnp.broadcast_to(squares, (tokens, 128)).T[:8])
    arrive()
    total = buf[0] + buf[1] + buf[2] + buf[3]
    scales = lax.rsqrt(total / (4 * features) + eps_norm)
    finish()
    return (scales, jnp.broadcast_to(scales[:1], (128, tokens)).T[:, :1])


def spread_kernel(
    flip, normed, *refs
):
    if normed:
        stream, gain, w, out, low_out, scale_out, lhs, nbuf, nsend, nrecv = refs[:10]
        refs = refs[10:]
    else:
        lhs, w, out = refs[:3]
        refs = refs[3:]
    wbuf, send1, recv1, own, send2, recv2, wsem, s1s, s1r, s2s, s2r = refs
    chunks, rows, width = send2.shape
    per = out.shape[2] // width
    me, near_bit, far_bit, near, far = col_places()
    depth = lhs.shape[3]

    def w_copy(j):
        k, cols = columns_of(j, width, per)
        return pltpu.make_async_copy(
            w.at[cols, :] if flip else w.at[k, :, cols], wbuf.at[j], wsem.at[j]
        )

    def near_copy(j):
        return pltpu.make_async_remote_copy(
            src_ref=send1.at[j],
            dst_ref=recv1.at[j],
            send_sem=s1s.at[j],
            recv_sem=s1r.at[j],
            device_id={"col": near},
            device_id_type=MESH,
        )

    def far_copy(j):
        return pltpu.make_async_remote_copy(
            src_ref=send2.at[j],
            dst_ref=recv2.at[j],
            send_sem=s2s.at[j],
            recv_sem=s2r.at[j],
            device_id={"col": far},
            device_id_type=MESH,
        )

    def loop(count, act):
        def lap(j, carry):
            act(j)
            return carry

        lax.fori_loop(0, count, lap, 0)

    loop(chunks, lambda j: w_copy(j).start())
    if normed:
        greet(col_peers())
        values = stream[...].astype(jnp.float32)
        scales, column = row_scales(values, share_parts("col", nbuf, nsend, nrecv), nbuf)
        scale_out[...] = scales
        low = (values * column * gain[...]).astype(jnp.bfloat16)
        low_out[...] = low
        lhs[...] = low.reshape(lhs.shape)
    else:
        greet((("col", near), ("col", far)))
    dot = dot_nt if flip else dot_nn

    def first(j):
        w_copy(j).wait()
        part = wbuf[j]
        theirs = dot(lhs[:, 1 - near_bit].reshape(2 * rows, depth), part)
        send1[j] = theirs.astype(jnp.bfloat16).reshape(2, rows, width)
        near_copy(j).start()
        mine = dot(lhs[:, near_bit].reshape(2 * rows, depth), part)
        own[j] = mine.reshape(2, rows, width)

    def second(j):
        near_copy(j).wait_recv()
        going = own[j, 1 - far_bit] + recv1[j, 1 - far_bit].astype(jnp.float32)
        send2[j] = going.astype(jnp.bfloat16)
        far_copy(j).start()
        own[j, far_bit] = own[j, far_bit] + recv1[j, far_bit].astype(jnp.float32)

    def third(j):
        far_copy(j).wait_recv()
        k, cols = columns_of(j, width, per)
        out[k, :, cols] = own[j, far_bit] + recv2[j].astype(jnp.float32)

    first(0)

    def both(j):
        first(j + 1)
        second(j)

    loop(chunks - 1, both)
    second(chunks - 1)
    loop(chunks, third)

    def drain(j):
        near_copy(j).wait_send()
        far_copy(j).wait_send()

    loop(chunks, drain)


def spread_product(lhs, w, flip, width, collective, gain=None):
    tokens, depth = lhs.shape
    rows = tokens // 4
    pairs = 1 if flip else w.shape[0]
    total = w.shape[0] if flip else w.shape[2]
    chunks = pairs * total // width
    tile = (width, depth) if flip else (depth, width)
    bf16, f32 = jnp.bfloat16, jnp.float32
    local = pl.BlockSpec(memory_space=pltpu.VMEM)
    shapes = [jax.ShapeDtypeStruct((pairs, rows, total), f32)]
    scratch = []
    if gain is None:
        inputs = [lhs.reshape(2, 2, rows, depth)]
    else:
        inputs = [lhs, gain[None]]
        shapes += [
            jax.ShapeDtypeStruct((tokens, depth), bf16),
            jax.ShapeDtypeStruct((8, tokens), f32),
        ]
        scratch = [pltpu.VMEM((2, 2, rows, depth), bf16), pltpu.VMEM((4, 8, tokens), f32)]
        scratch += [pltpu.SemaphoreType.DMA((4,))] * 2
    result = pl.pallas_call(
        functools.partial(spread_kernel, flip, gain is not None),
        out_shape=tuple(shapes),
        in_specs=[local] * len(inputs) + [pl.BlockSpec(memory_space=pl.ANY)],
        out_specs=[local] * len(shapes),
        scratch_shapes=scratch
        + [
            pltpu.VMEM((chunks,) + tile, bf16),
            pltpu.VMEM((chunks, 2, rows, width), bf16),
            pltpu.VMEM((chunks, 2, rows, width), bf16),
            pltpu.VMEM((chunks, 2, rows, width), f32),
            pltpu.VMEM((chunks, rows, width), bf16),
            pltpu.VMEM((chunks, rows, width), bf16),
        ]
        + [pltpu.SemaphoreType.DMA((chunks,))] * 5,
        compiler_params=pltpu.CompilerParams(
            collective_id=collective, has_side_effects=True, vmem_limit_bytes=56 * MIB
        ),
    )(*inputs, w)
    return result[0] if gain is None else result


def meet_kernel(flip, grad_mode, *refs):
    if grad_mode:
        piece, w, side, prod, grad_out = refs[:5]
        refs = refs[5:]
    else:
        piece, w, stream, gain, all_out, prod, low_out, scale_out = refs[:8]
        nbuf, nsend, nrecv = refs[-3:]
        refs = refs[8:-3]
    wbuf, buf, acc, sendx, recvx, wsem, osem, ns, nr, fs, fr, rs, rr, xs, xr = refs[:15]
    if grad_mode:
        stage, gsem = refs[15:]
    chunks, _, _, rows, width = buf.shape
    per = piece.shape[2] // width
    me, near_bit, far_bit, near, far = col_places()
    across = 1 - lax.axis_index("row")
    f32, bf16 = jnp.float32, jnp.bfloat16

    def w_copy(j):
        k, cols = columns_of(j, width, per)
        return pltpu.make_async_copy(
            w.at[k, :, cols] if flip else w.at[cols, :], wbuf.at[j], wsem.at[j]
        )

    def move(j, source, near_place, far_place, sems, target):
        return pltpu.make_async_remote_copy(
            src_ref=source,
            dst_ref=buf.at[j, far_place, near_place],
            send_sem=sems[0].at[j],
            recv_sem=sems[1].at[j],
            device_id={"col": target},
            device_id_type=MESH,
        )

    def piece_at(j):
        k, cols = columns_of(j, width, per)
        return piece.at[k, :, cols]

    def far_copy(j):
        return move(j, piece_at(j), near_bit, far_bit, (fs, fr), far)

    def near_copy(j):
        return move(j, piece_at(j), near_bit, far_bit, (ns, nr), near)

    def relay(j):
        return move(j, buf.at[j, 1 - far_bit, near_bit], near_bit, 1 - far_bit, (rs, rr), near)

    def out_copy(j):
        k, cols = columns_of(j, width, per)
        return pltpu.make_async_copy(buf.at[j], all_out.at[k, :, :, :, cols], osem.at[j])

    def cross(half):
        return pltpu.make_async_remote_copy(
            src_ref=sendx.at[half],
            dst_ref=recvx.at[half],
            send_sem=xs.at[half],
            recv_sem=xr.at[half],
            device_id={"row": across},
            device_id_type=MESH,
        )

    def loop(count, act):
        def lap(j, carry):
            act(j)
            return carry

        lax.fori_loop(0, count, lap, 0)

    loop(chunks, lambda j: w_copy(j).start())
    greet((("col", near), ("col", far), ("row", across)))

    def begin(j):
        far_copy(j).start()
        near_copy(j).start()
        k, cols = columns_of(j, width, per)
        buf[j, far_bit, near_bit] = piece[k, :, cols]

    loop(chunks, begin)
    acc[...] = jnp.zeros_like(acc)
    dot = dot_nt if flip else dot_nn

    def add(j, half):
        both = buf[j, half].reshape(2 * rows, width)
        acc[half] = acc[half] + dot(both, wbuf[j])

    def here(j):
        near_copy(j).wait_recv()
        w_copy(j).wait()
        add(j, far_bit)

    loop(chunks, here)
    sendx[far_bit] = acc[far_bit].astype(bf16)
    cross(far_bit).start()

    def grad_copy(j):
        return grad_moves(j)

    if grad_mode == "wide":
        parts = grad_out.shape[0]

        def grad_moves(j):
            k, cols = columns_of(j, width, per)
            return pltpu.make_async_copy(
                stage.at[lax.rem(j, 2)], grad_out.at[:, k, :, cols], gsem.at[lax.rem(j, 2)]
            )

        def grad_part(j):
            block = buf[j].reshape(4 * rows, width)
            total = dot_nn(side[...], block).astype(bf16)
            stage[lax.rem(j, 2)] = total.reshape(stage.shape[1:])

    if grad_mode == "tall":

        def grad_moves(j):
            return pltpu.make_async_copy(
                stage.at[lax.rem(j, 2)],
                grad_out.at[pl.ds(pl.multiple_of(j * width, width), width), :],
                gsem.at[lax.rem(j, 2)],
            )

        def grad_part(j):
            block = buf[j].reshape(4 * rows, width)
            stage[lax.rem(j, 2)] = dot_nn(block.T, side[...]).astype(bf16)

    def pass_on(j):
        far_copy(j).wait_recv()
        relay(j).start()

    def there(j):
        relay(j).wait_recv()
        if not grad_mode:
            out_copy(j).start()
        add(j, 1 - far_bit)
        if grad_mode:

            @pl.when(j >= 2)
            def _():
                grad_moves(j - 2).wait()

            grad_part(j)
            grad_moves(j).start()

    pass_on(0)

    def both(j):
        pass_on(j + 1)
        there(j)

    loop(chunks - 1, both)
    there(chunks - 1)
    sendx[1 - far_bit] = acc[1 - far_bit].astype(bf16)
    cross(1 - far_bit).start()

    def settle(half):
        cross(half).wait_recv()
        prod[half] = sendx[half].astype(f32) + recvx[half].astype(f32)

    settle(far_bit)
    settle(1 - far_bit)
    if not grad_mode:
        values = prod[...].reshape(stream.shape) + stream[...].astype(f32)
        prod[...] = values.reshape(prod.shape)
        scales, column = row_scales(values, share_parts("col", nbuf, nsend, nrecv), nbuf)
        scale_out[...] = scales
        low_out[...] = (values * column * gain[...]).astype(bf16)

    def drain(j):
        near_copy(j).wait_send()
        far_copy(j).wait_send()
        relay(j).wait_send()
        if not grad_mode:
            out_copy(j).wait()

    loop(chunks, drain)
    cross(far_bit).wait_send()
    cross(1 - far_bit).wait_send()
    if grad_mode:
        for j in range(max(0, chunks - 2), chunks):
            grad_moves(j).wait()


def meet_product(piece, w, flip, width, collective, side=None, grad_mode=None, parts=1, stream=None, gain=None):
    pairs, rows, total = piece.shape
    features = w.shape[1]
    chunks = pairs * total // width
    tile = (features, width) if flip else (width, features)
    bf16, f32 = jnp.bfloat16, jnp.float32
    inputs, in_specs = (
        [piece, w],
        [pl.BlockSpec(memory_space=pltpu.VMEM), pl.BlockSpec(memory_space=pl.ANY)],
    )
    shapes = [jax.ShapeDtypeStruct((2, 2 * rows, features), f32)]
    out_specs = [pl.BlockSpec(memory_space=pltpu.VMEM)]
    scratch = [
        pltpu.VMEM((chunks,) + tile, bf16),
        pltpu.VMEM((chunks, 2, 2, rows, width), bf16),
        pltpu.VMEM((2, 2 * rows, features), f32),
        pltpu.VMEM((2, 2 * rows, features), bf16),
        pltpu.VMEM((2, 2 * rows, features), bf16),
    ]
    scratch += [pltpu.SemaphoreType.DMA((chunks,))] * 8 + [pltpu.SemaphoreType.DMA((2,))] * 2
    if grad_mode:
        inputs.append(side)
        in_specs.append(pl.BlockSpec(memory_space=pltpu.VMEM))
        out_specs.append(pl.BlockSpec(memory_space=pl.ANY))
        if grad_mode == "wide":
            shape = (parts, pairs, side.shape[0] // parts, total)
            stage = (2, parts, side.shape[0] // parts, width)
        else:
            shape = (total, side.shape[1])
            stage = (2, width, side.shape[1])
        shapes.append(jax.ShapeDtypeStruct(shape, bf16))
        scratch += [pltpu.VMEM(stage, bf16), pltpu.SemaphoreType.DMA((2,))]
    else:
        local = pl.BlockSpec(memory_space=pltpu.VMEM)
        inputs += [stream, gain[None]]
        in_specs += [local, local]
        shapes.insert(0, jax.ShapeDtypeStruct((pairs, 2, 2, rows, total), bf16))
        out_specs.insert(0, pl.BlockSpec(memory_space=pl.ANY))
        shapes.append(jax.ShapeDtypeStruct((4 * rows, features), bf16))
        shapes.append(jax.ShapeDtypeStruct((8, 4 * rows), f32))
        out_specs += [local, local]
        scratch += [pltpu.VMEM((4, 8, 4 * rows), f32)] + [pltpu.SemaphoreType.DMA((4,))] * 2
    result = pl.pallas_call(
        functools.partial(meet_kernel, flip, grad_mode),
        out_shape=tuple(shapes),
        in_specs=in_specs,
        out_specs=out_specs,
        scratch_shapes=scratch,
        compiler_params=pltpu.CompilerParams(
            collective_id=collective, has_side_effects=True, vmem_limit_bytes=56 * MIB
        ),
    )(*inputs)
    if grad_mode:
        return (result[0].reshape(4 * rows, features), result[1])
    return (
        result[0].reshape(pairs, 4 * rows, total),
        result[1].reshape(4 * rows, features),
        result[2],
        result[3][0],
    )


def block_steps(x, acc, gram, poly):
    side, total = x.shape
    step = 256
    count = total // step
    span = 1280 if total % 1280 == 0 else step
    f32, bf16 = jnp.float32, jnp.bfloat16

    def tile(k, size):
        return pl.ds(pl.multiple_of(k * size, size), size)

    def square(k, total):
        values = x[:, tile(k, step)].astype(f32)
        return total + jnp.sum(values * values, axis=0, keepdims=True)

    sums = lax.fori_loop(0, count, square, jnp.zeros((1, step), f32))
    norm = jnp.sqrt(jnp.sum(sums, axis=1, keepdims=True)) + eps_frob

    def divide(k, carry):
        x[:, tile(k, step)] = (x[:, tile(k, step)].astype(f32) / norm).astype(bf16)
        return carry

    lax.fori_loop(0, count, divide, 0)

    def lap(k, carry):
        acc[...] = jnp.zeros_like(acc)

        def add(j, inner):
            block = x[:, tile(j, span)]
            acc[:step, :step] = acc[:step, :step] + dot_nt(block[:step], block[:step])
            acc[step:, :] = acc[step:, :] + dot_nt(block[step:], block)
            return inner

        lax.fori_loop(0, total // span, add, 0)
        acc[:step, step:] = acc[step:, :step].T
        low = acc[...].astype(bf16)
        gram[...] = low
        square_gram = dot_nn(low, gram[...])
        poly[...] = (poly_second * low.astype(f32) + poly_third * square_gram).astype(bf16)

        def advance(j, inner):
            block = x[:, tile(j, span)]
            fresh = poly_first * block.astype(f32) + dot_nn(poly[...], block)
            x[:, tile(j, span)] = fresh.astype(bf16)
            return inner

        lax.fori_loop(0, total // span, advance, 0)
        return carry

    lax.fori_loop(0, 5, lap, 0)


def work_space(side):
    return [
        pltpu.VMEM((side, side), jnp.float32),
        pltpu.VMEM((side, side), jnp.bfloat16),
        pltpu.VMEM((side, side), jnp.bfloat16),
    ]


def gates_kernel(conv, first, second, out, full, came, send_sem, recv_sem):
    me = lax.axis_index("col")
    count = out.shape[0]
    greet([("col", lax.rem(me + step, 4)) for step in range(1, 4)])
    for k, grads in enumerate((first, second)):
        for head in range(conv.shape[1] // HS):
            columns = slice(head * HS, (head + 1) * HS)
            block = dot_nn(conv[:, columns].T, grads[:, columns])
            full[k * HS : (k + 1) * HS, columns] = block.astype(jnp.bfloat16)

    def part(place):
        return full.at[pl.ds(pl.multiple_of(place * count, count), count)]

    def copy(step):
        target = lax.rem(me + step, 4)
        return pltpu.make_async_remote_copy(
            src_ref=part(target),
            dst_ref=came.at[step - 1],
            send_sem=send_sem.at[step - 1],
            recv_sem=recv_sem.at[step - 1],
            device_id={"col": target},
            device_id_type=MESH,
        )

    for step in range(1, 4):
        copy(step).start()
    total = part(me)[...].astype(jnp.float32)
    for step in range(1, 4):
        copy(step).wait_recv()
        total = total + came[step - 1].astype(jnp.float32)
    out[...] = total.astype(jnp.bfloat16)
    for step in range(1, 4):
        copy(step).wait_send()


def gates_product(conv, first, second):
    lanes = conv.shape[1]
    count = 2 * HS // 4
    bf16 = jnp.bfloat16
    return pl.pallas_call(
        gates_kernel,
        out_shape=jax.ShapeDtypeStruct((count, lanes), bf16),
        in_specs=[pl.BlockSpec(memory_space=pltpu.VMEM)] * 3,
        out_specs=pl.BlockSpec(memory_space=pltpu.VMEM),
        scratch_shapes=[
            pltpu.VMEM((2 * HS, lanes), bf16),
            pltpu.VMEM((3, count, lanes), bf16),
            pltpu.SemaphoreType.DMA((3,)),
            pltpu.SemaphoreType.DMA((3,)),
        ],
        compiler_params=pltpu.CompilerParams(
            collective_id=12, has_side_effects=True, vmem_limit_bytes=16 * MIB
        ),
    )(conv, first, second)


def token_total(values):
    return lax.psum(values, "col")


def dp_sum(grad):
    low = grad.astype(jnp.bfloat16)
    return lax.psum_scatter(low, "dp", scatter_dimension=0, tiled=True).astype(jnp.float32)


def pair_sum(grad, dp_count):
    if grad.shape[0] == dp_count:
        return lax.psum_scatter(grad, "dp", scatter_dimension=0)
    return lax.psum_scatter(grad[0], "dp", scatter_dimension=1, tiled=True)


def owner_send(block, root):
    return broadcast(block, "dp", root)


def norm_backward(stream, scale, gain, grad_normed, width):
    weighted = grad_normed * gain[None, :]
    inner = token_total(jnp.sum(stream * weighted, axis=1))
    grad_stream = (
        scale[:, None] * weighted - stream * (scale * scale * scale * inner / width)[:, None]
    )
    grad_gain = jnp.sum(grad_normed * stream * scale[:, None], axis=0)
    return (grad_stream, grad_gain)


def orthogonalize(block):
    work = block
    values = work.astype(jnp.float32)
    work = (values / (jnp.sqrt(jnp.sum(values * values)) + eps_frob)).astype(jnp.bfloat16)
    for step in range(5):
        gram = product_nt(work, work).astype(jnp.bfloat16)
        poly = (poly_second * gram.astype(jnp.float32) + poly_third * product(gram, gram)).astype(
            jnp.bfloat16
        )
        work = (poly_first * work.astype(jnp.float32) + product(poly, work)).astype(jnp.bfloat16)
    return work


def owner_results(blocks, dp_place, dp_count):
    results = [None, None, None, None, None, None]
    for members in ((0, 1, 2), (3, 4, 5)):
        flipped = [blocks[number].shape[0] > blocks[number].shape[1] for number in members]
        wide = [
            blocks[number].T if turn else blocks[number] for number, turn in zip(members, flipped)
        ]
        chosen = wide[0]
        for number, candidate in zip(members[1:], wide[1:]):
            chosen = jnp.where(dp_place == number % dp_count, candidate, chosen)
        done = orthogonalize(chosen)
        for number, turn in zip(members, flipped):
            kept = jnp.where(dp_place == number % dp_count, done, jnp.zeros_like(done))
            results[number] = kept.T if turn else kept
    return results


def dp_moves(moves, sems):
    local_sem, send_sem, recv_sem = sems
    me = lax.axis_index("dp")

    def remote(k, sender, target):
        pairs, source, destination = moves[k]
        return pltpu.make_async_remote_copy(
            src_ref=source(sender, target),
            dst_ref=destination(sender, target),
            send_sem=send_sem.at[k, target],
            recv_sem=recv_sem.at[k, sender],
            device_id={"dp": target},
            device_id_type=MESH,
        )

    def local(k, place):
        pairs, source, destination = moves[k]
        return pltpu.make_async_copy(
            source(place, place), destination(place, place), local_sem.at[k]
        )

    def each(chosen, act):
        for k in chosen:
            for sender, target in moves[k][0]:
                act(k, sender, target)

    def start_one(k, sender, target):
        @pl.when(me == sender)
        def _():
            if sender == target:
                local(k, sender).start()
            else:
                remote(k, sender, target).start()

    def arrive_one(k, sender, target):
        @pl.when(me == target)
        def _():
            if sender == target:
                local(k, sender).wait()
            else:
                remote(k, sender, target).wait_recv()

    def sent_one(k, sender, target):
        if sender != target:

            @pl.when(me == sender)
            def _():
                remote(k, sender, target).wait_send()

    return (
        lambda *chosen: each(chosen, start_one),
        lambda *chosen: each(chosen, arrive_one),
        lambda *chosen: each(chosen, sent_one),
    )


def rows_at(ref, place):
    def pick(sender, target):
        index = sender if place == "sender" else target
        count = ref.shape[0] // 4
        return ref.at[pl.ds(index * count, count)]

    return pick


def entry(ref, place):
    return lambda sender, target: ref.at[sender if place == "sender" else target]


def whole(ref):
    return lambda sender, target: ref


def to_owner(owner):
    return [(sender, owner) for sender in ((owner + step) % 4 for step in range(4))]


def from_owner(owner):
    return [(owner, target) for target in ((owner + step) % 4 for step in range(4))]


SMALL_OWNER, CON_OWNER, GATE_OWNER, UP_OWNER = (0, 1, 2, 3)


def pieces_at_owner(e0, e1, con, later):
    me = lax.axis_index("dp")
    rows = e0.shape[0]
    packed = jnp.concatenate(
        [con[k * rows : (k + 1) * rows] for k in range(con.shape[0] // rows)], axis=1
    )

    def piece_for(owner):
        return jnp.where(owner == GATE_OWNER, e0, jnp.where(owner == UP_OWNER, e1, packed))

    leaving = [piece_for(lax.rem(me + step, 4)) for step in range(4)]
    leaving, later = lax.optimization_barrier((leaving, later))
    pieces = leaving[:1]
    for step in range(1, 4):
        pairs = [(sender, (sender + step) % 4) for sender in range(4)]
        pairs = [pair for pair in pairs if pair[1] != SMALL_OWNER]
        pieces.append(lax.ppermute(leaving[step], "dp", pairs))
    return (pieces, later)


def tail_kernel(*refs):
    large, (b0, b1, out) = refs[:4], refs[4:7]
    gates_piece, col_part, dp_part = refs[7:10]
    expand_o, con_o, branch_o, out_o, gates_o, col_o, dp_o = refs[10:17]
    x, packed, pieces, first, second, third, out_v, acc, gram, poly, load_sem = refs[17:28]
    col_buf, dp_buf, gates_dp, gates_col = refs[28:32]
    shares = [
        share_parts("col", col_buf, *refs[32:34]),
        share_parts("dp", dp_buf, *refs[34:36]),
        share_parts("dp", gates_dp, *refs[36:38]),
        share_parts("col", gates_col, *refs[38:40]),
    ]
    sems = refs[40:]
    place = lax.axis_index("col")
    me = lax.axis_index("dp")
    small = out.shape[0]
    width = pieces.shape[1]
    side = x.shape[0]
    rows = side // 4
    moves = [
        (to_owner(SMALL_OWNER), whole(b0), rows_at(first, "sender")),
        (to_owner(SMALL_OWNER), whole(b1), rows_at(second, "sender")),
        (to_owner(SMALL_OWNER), whole(out), entry(out_v, "sender")),
        (from_owner(GATE_OWNER), rows_at(x, "target"), whole(expand_o.at[0])),
        (from_owner(UP_OWNER), rows_at(x, "target"), whole(expand_o.at[1])),
        (from_owner(CON_OWNER), entry(pieces, "target"), whole(con_o)),
        (from_owner(SMALL_OWNER), rows_at(first, "target"), whole(branch_o.at[0])),
        (from_owner(SMALL_OWNER), rows_at(second, "target"), whole(branch_o.at[1])),
        (from_owner(SMALL_OWNER), entry(out_v, "target"), whole(out_o)),
    ]
    start, arrive, sent = dp_moves(moves, sems)
    greet(
        [("dp", lax.rem(me + step, 4)) for step in range(1, 4)]
        + [("col", lax.rem(place + step, 4)) for step in range(1, 4)]
    )
    shares[0][0](col_part[...])
    shares[2][0](gates_piece[...])
    start(0, 1, 2)
    shares[0][1]()
    summed = col_buf[0] + col_buf[1] + col_buf[2] + col_buf[3]
    col_o[...] = summed
    shares[1][0](jnp.concatenate([summed[:8], dp_part[...]], axis=0))
    shares[2][1]()
    shares[3][0](gates_dp[...].reshape(gates_col.shape[1:]))

    def load(owner, target):
        copies = [
            pltpu.make_async_copy(large[step], target((owner - step) % 4), load_sem.at[step])
            for step in range(4)
        ]
        for copy in copies:
            copy.start()
        for copy in copies:
            copy.wait()

    @pl.when(me == CON_OWNER)
    def _():
        load(CON_OWNER, lambda j: packed.at[j])
        for j in range(4):
            for k in range(width // rows):
                first_column = j * width + k * rows
                x[:, first_column : first_column + rows] = packed[j, :, k * side : (k + 1) * side].T

    @pl.when(me == GATE_OWNER)
    def _():
        load(GATE_OWNER, lambda j: x.at[pl.ds(j * rows, rows)])

    @pl.when(me == UP_OWNER)
    def _():
        load(UP_OWNER, lambda j: x.at[pl.ds(j * rows, rows)])

    @pl.when(me != SMALL_OWNER)
    def _():
        block_steps(x, acc, gram, poly)

    @pl.when(me == CON_OWNER)
    def _():
        for j in range(4):
            pieces[j] = x[:, j * width : (j + 1) * width].T

    start(3, 4, 5)
    for k, part in enumerate((first, second, third)):
        arrive(k)

        @pl.when(me == SMALL_OWNER)
        def _():
            if k == 2:
                for j in range(4):
                    part[:, j * small : (j + 1) * small] = out_v[j].T
            block_steps(part, acc, gram, poly)
            if k == 2:
                for j in range(4):
                    out_v[j] = part[:, j * small : (j + 1) * small].T

        start(6 + k)
    shares[1][1]()
    dp_o[...] = dp_buf[0] + dp_buf[1] + dp_buf[2] + dp_buf[3]
    shares[3][1]()
    half = gates_col.shape[1]
    for k in range(2):
        for head in range(gates_o.shape[1]):
            columns = slice(head * HS, (head + 1) * HS)
            for j in range(HS // half):
                lines = slice(j * half, (j + 1) * half)
                gates_o[k, head, lines, :] = gates_col[k * (HS // half) + j][:, columns]
    arrive(6, 7, 8, 3, 4, 5)
    sent(0, 1, 2, 3, 4, 5, 6, 7, 8)
    for share in shares:
        share[2]()


def finish_blocks(large, con_shape, b0, b1, out, gates_piece, col_part, dp_part):
    piece = large[0].shape
    rows, total = piece
    side = 4 * rows
    f32, bf16 = jnp.float32, jnp.bfloat16
    shape = jax.ShapeDtypeStruct
    small = pltpu.VMEM((side, b0.shape[1]), bf16)
    quarter = (4 * gates_piece.shape[0], gates_piece.shape[1])
    anywhere = pl.BlockSpec(memory_space=pl.ANY)
    local = pl.BlockSpec(memory_space=pltpu.VMEM)
    sems = pltpu.SemaphoreType.DMA
    shapes = [shape(s, bf16) for s in ((2,) + piece, con_shape, (2,) + b0.shape, out.shape)]
    shapes += [shape((2, quarter[1] // HS, HS, HS), bf16), shape(col_part.shape, f32)]
    shapes += [shape(col_part.shape, f32)]
    return pl.pallas_call(
        tail_kernel,
        out_shape=tuple(shapes),
        in_specs=[anywhere] * 7 + [local] * 3,
        out_specs=[anywhere] * 4 + [local] * 3,
        scratch_shapes=[
            pltpu.VMEM((side, total), bf16),
            pltpu.VMEM((4,) + piece, bf16),
            pltpu.VMEM((4,) + con_shape, bf16),
            small,
            small,
            small,
            pltpu.VMEM((4,) + out.shape, bf16),
        ]
        + work_space(side)
        + [sems((4,))]
        + [
            pltpu.VMEM((4,) + col_part.shape, f32),
            pltpu.VMEM((4,) + col_part.shape, f32),
            pltpu.VMEM((4,) + gates_piece.shape, bf16),
            pltpu.VMEM((4,) + quarter, bf16),
        ]
        + [sems((4,))] * 8
        + [sems((9,)), sems((9, 4)), sems((9, 4))],
        compiler_params=pltpu.CompilerParams(
            collective_id=0, has_side_effects=True, vmem_limit_bytes=40 * MIB
        ),
    )(*large, b0, b1, out, gates_piece, col_part, dp_part)


def grouped_step(grad, moment, weight, rate):
    new_moment = momentum_rate * moment + grad
    rows, cols = new_moment.shape
    grouped = new_moment.reshape(rows, cols // GROUP, GROUP)
    norm_sq = jnp.mean(grouped * grouped, axis=2, keepdims=True)
    update = (grouped * lax.rsqrt(norm_sq + eps_norm)).reshape(rows, cols)
    return (new_moment, weight - rate * update)


def shards(
    block_input,
    segment_ids,
    output_cotangent,
    norm_gains,
    branch_weights,
    mixer_vectors,
    gate_blocks,
    output_weights,
    expand_weights,
    contract_weights,
    gains_momentum,
    branch_momentum,
    vectors_momentum,
    gates_momentum,
    output_momentum,
    expand_momentum,
    contract_momentum,
):
    f32 = jnp.float32
    bf16 = jnp.bfloat16
    col_count = lax.axis_size("col")
    col_place = lax.axis_index("col")
    dp_count = lax.axis_size("dp")
    dp_place = lax.axis_index("dp")
    group_rows = block_input.shape[0]
    rows = group_rows // col_count
    lanes = mixer_vectors.shape[1]
    heads_here = lanes // HS
    feature_count = block_input.shape[1]
    width = feature_count * col_count
    first_row = col_place * rows
    reach = CONV - 1
    seg_row = segment_ids[0]
    seg_ext = jnp.concatenate(
        [jnp.full((reach,), -1, jnp.int32), seg_row, jnp.full((reach,), -2, jnp.int32)]
    )
    seg_here = lax.dynamic_slice_in_dim(seg_ext, first_row + reach, rows + reach)
    masks = []
    for shift in range(CONV):
        earlier = lax.dynamic_slice_in_dim(seg_ext, first_row + reach - shift, rows + reach)
        masks.append((earlier == seg_here).astype(f32))
    reset_rows = masks[1][:rows] < 0.5
    stream = block_input.astype(f32)
    branch_pre, normed_low, scale_rows = spread_product(
        block_input, branch_weights, False, 640, 2, norm_gains[0]
    )
    scale_one = scale_rows[0]
    contract_term = product_nt(output_cotangent, contract_weights).astype(bf16)
    contract_term, branch_pre = lax.optimization_barrier((contract_term, branch_pre))
    grad_activated = lax.psum_scatter(contract_term, "col", scatter_dimension=0, tiled=True)
    mixed = branch_pre[0]
    gelu_in = branch_pre[1]
    edge = from_behind(mixed[rows - reach :], "col", 1)
    extended = jnp.concatenate([edge, mixed], axis=0)
    windows = []
    conv_out = jnp.zeros((rows, lanes), f32) + mixer_vectors[CONV][None, :]
    for shift in range(CONV):
        window = extended[reach - shift : reach - shift + rows] * masks[shift][:rows, None]
        windows.append(window)
        conv_out = conv_out + mixer_vectors[shift][None, :] * window
    conv_low = conv_out.astype(bf16).reshape(rows, heads_here, HS)
    gate_pre = jnp.einsum(
        "thi,ghij->tghj", conv_low, gate_blocks, preferred_element_type=f32
    ).reshape(rows, 2, lanes)
    gate_pre = gate_pre + mixer_vectors[CONV + 1 : CONV + 3][None]

    def recurrence_terms(conv_values, gate_values, rate_values):
        input_gate = jax.nn.sigmoid(gate_values[:, 0])
        decay_gate = jax.nn.sigmoid(gate_values[:, 1])
        log_decay = -decay_scale * decay_gate * jax.nn.softplus(rate_values)[None, :]
        inject_scale = jnp.where(reset_rows[:, None], 1.0, jnp.sqrt(1.0 - jnp.exp(2.0 * log_decay)))
        decay_values = jnp.where(reset_rows[:, None], 0.0, jnp.exp(log_decay))
        return (decay_values, inject_scale * input_gate * conv_values)

    (decay, inject), pull_terms = jax.vjp(
        recurrence_terms, conv_out, gate_pre, mixer_vectors[CONV + 3]
    )
    local_a, local_b = linear_scan(decay, inject, False)
    identity = (jnp.ones((lanes,), f32), jnp.zeros((lanes,), f32))
    incoming = prefix((local_a[-1], local_b[-1]), "col", link, identity, False)
    carried = incoming[1]
    state = local_a * carried[None, :] + local_b
    gelu_out, pull_gelu = jax.vjp(gelu_tanh, gelu_in)
    hidden = (gelu_out * state).astype(bf16)
    hidden_all, middle, normed_two_low, scale_two = meet_product(
        hidden[None],
        output_weights,
        False,
        256,
        3,
        stream=block_input,
        gain=norm_gains[1],
    )
    expand_pre = spread_product(normed_two_low, expand_weights, False, 768, 4)

    def geglu(gate_values, up_values):
        return gelu_tanh(gate_values) * up_values

    activated, pull_geglu = jax.vjp(geglu, expand_pre[0], expand_pre[1])
    activated_low = activated.astype(bf16)
    contracted, contract_grad = meet_product(
        activated_low[None], contract_weights, False, 768, 5, output_cotangent, "tall"
    )
    block_output = (middle + contracted).astype(bf16)
    cot_values = output_cotangent.astype(f32)
    grad_activated = grad_activated.astype(f32)
    grad_gate, grad_up = pull_geglu(grad_activated)
    grad_expand_low = jnp.stack([grad_gate, grad_up]).astype(bf16)
    grad_expand_low, contract_grad = lax.optimization_barrier((grad_expand_low, contract_grad))
    parts = dp_count if feature_count % (16 * dp_count) == 0 else 1
    grad_normed_two, expand_grad = meet_product(
        grad_expand_low, expand_weights, True, 768, 7, normed_two_low.T, "wide", parts
    )
    grad_middle_norm, gain_two_grad = norm_backward(
        middle, scale_two, norm_gains[1], grad_normed_two, width
    )
    grad_middle = cot_values + grad_middle_norm
    grad_branch_low = grad_middle.astype(bf16)
    output_grad = product_tn(hidden_all[0], grad_branch_low)
    grad_hidden = spread_product(grad_branch_low, output_weights, True, 256, 8)[0]
    grad_state = grad_hidden * gelu_out
    (grad_gelu_in,) = pull_gelu(grad_hidden * state)
    shifted_decay = jnp.concatenate([decay[1:], jnp.ones((1, lanes), f32)], axis=0)
    back_a, back_b = linear_scan(shifted_decay, grad_state, True)
    from_later = prefix((decay[0] * back_a[0], decay[0] * back_b[0]), "col", link, identity, True)
    grad_total = back_a * from_later[1][None, :] + back_b
    previous = jnp.concatenate([carried[None, :], state[:-1]], axis=0)
    grad_conv_direct, grad_gate_pre, grad_rate = pull_terms((grad_total * previous, grad_total))
    grad_gate_low = grad_gate_pre.astype(bf16)
    grad_gate_heads = grad_gate_low.reshape(rows, 2, heads_here, HS)
    grad_conv = grad_conv_direct + jnp.einsum(
        "tghj,ghij->thi", grad_gate_heads, gate_blocks, preferred_element_type=f32
    ).reshape(rows, lanes)
    parts = dp_count if feature_count % (16 * dp_count) == 0 else 1
    planes = dp_count == 4 and parts == 4 and 2 * feature_count <= lanes and group_rows <= lanes
    gate_bias_grad = jnp.sum(grad_gate_low.astype(f32), axis=0)
    after = from_behind(grad_conv[:reach], "col", -1)
    grad_conv_ext = jnp.concatenate([grad_conv, after], axis=0)
    grad_mixed = jnp.zeros((rows, lanes), f32)
    tap_grads = []
    for shift in range(CONV):
        masked = grad_conv_ext * masks[shift][:, None]
        grad_mixed = grad_mixed + mixer_vectors[shift][None, :] * masked[shift : shift + rows]
        tap_grads.append(jnp.sum(grad_conv * windows[shift], axis=0))
    vector_rows = tap_grads + [
        jnp.sum(grad_conv, axis=0),
        gate_bias_grad[0],
        gate_bias_grad[1],
        grad_rate,
    ]
    vectors_grad = jnp.stack(vector_rows)
    grad_branch_pre = jnp.stack([grad_mixed, grad_gelu_in]).astype(bf16)
    grad_normed_one, branch_grad = meet_product(
        grad_branch_pre, branch_weights, True, 640, 9, normed_low.T, "wide", parts
    )
    if planes:
        contract_sum = pair_sum(contract_grad.reshape((4, -1) + contract_grad.shape[1:]), 4)
        expand_grad, contract_sum = lax.optimization_barrier((expand_grad, contract_sum))
        expand_sum = pair_sum(expand_grad, 4)
        con_low = (momentum_rate * contract_momentum[0] + contract_sum).astype(bf16)
        weighted = grad_normed_one * norm_gains[0][None, :]
        inner_part = jnp.sum(stream * weighted, axis=1)
        gain_one_grad = jnp.sum(grad_normed_one * stream * scale_one[:, None], axis=0)
        col_part = jnp.concatenate(
            [
                vectors_grad,
                jnp.pad(inner_part, (0, lanes - group_rows))[None],
                jnp.zeros((7, lanes), f32),
            ]
        )
        gains_row = jnp.concatenate([gain_one_grad, gain_two_grad])
        dp_part = jnp.pad(gains_row[None], ((0, 7), (0, lanes - 2 * feature_count)))
        gates_part = gates_product(
            conv_low.reshape(rows, lanes), grad_gate_low[:, 0], grad_gate_low[:, 1]
        )
        piece_rows = branch_grad.shape[2]
        small_grad = jnp.concatenate(
            [
                branch_grad.reshape(4, 2 * piece_rows, lanes),
                output_grad.astype(bf16).reshape(4, piece_rows, lanes),
                gates_part.reshape(4, -1, lanes),
            ],
            axis=1,
        )
        con_low, expand_sum, col_part, dp_part, small_grad = lax.optimization_barrier(
            (con_low, expand_sum, col_part, dp_part, small_grad)
        )
        expand_low = (momentum_rate * expand_momentum[:, 0] + expand_sum).astype(bf16)
        small_grad, expand_sum = lax.optimization_barrier((small_grad, expand_sum))
        large, (expand_sum, contract_sum) = pieces_at_owner(
            expand_low[0], expand_low[1], con_low, (expand_sum, contract_sum)
        )
        small_sum = pair_sum(small_grad, 4)
        branch_sum = small_sum[: 2 * piece_rows].reshape(2, piece_rows, lanes)
        output_sum = small_sum[2 * piece_rows : 3 * piece_rows].reshape(output_momentum.shape[1:])
        branch_low = (momentum_rate * branch_momentum[:, 0] + branch_sum).astype(bf16)
        output_low = (momentum_rate * output_momentum[0] + output_sum).astype(bf16)
        expand_orth, con, branch_orth, out, gates_all, col_total, dp_total = finish_blocks(
            large,
            con_low.shape,
            branch_low[0],
            branch_low[1],
            output_low,
            small_sum[3 * piece_rows :],
            col_part,
            dp_part,
        )
        output_sum = output_sum.astype(f32)
        gates_total = gates_all.astype(f32)
        vectors_total = dp_total[:8]
        gains_total = dp_total[8, : 2 * feature_count].reshape(2, feature_count)
        inner = col_total[8, :group_rows]
        grad_stream_norm = (
            scale_one[:, None] * weighted
            - stream * (scale_one * scale_one * scale_one * inner / width)[:, None]
        )
    else:
        grad_stream_norm, gain_one_grad = norm_backward(
            stream, scale_one, norm_gains[0], grad_normed_one, width
        )
        vectors_total, gains_total = lax.psum(
            (lax.psum(vectors_grad, "col"), jnp.stack([gain_one_grad, gain_two_grad])), "dp"
        )
        gates_grad = jnp.einsum(
            "thi,tghj->ghij", conv_low, grad_gate_heads, preferred_element_type=f32
        ).astype(bf16)
        branch_sum = pair_sum(branch_grad, dp_count)
        expand_sum = pair_sum(expand_grad, dp_count)
        output_sum = dp_sum(output_grad)
        contract_sum = dp_sum(contract_grad)
        gates_total = lax.psum(gates_grad, ("dp", "col")).astype(f32)
    input_grad = (grad_middle + grad_stream_norm).astype(bf16)
    branch_sum = branch_sum.astype(f32)
    expand_sum = expand_sum.astype(f32)
    contract_sum = contract_sum.astype(f32)
    branch_moment = momentum_rate * branch_momentum[:, 0] + branch_sum
    expand_moment = momentum_rate * expand_momentum[:, 0] + expand_sum
    output_moment = momentum_rate * output_momentum[0] + output_sum
    contract_moment = momentum_rate * contract_momentum[0] + contract_sum
    if not planes:
        moments = (*branch_moment, output_moment, *expand_moment, contract_moment)
        lows = [moment.astype(bf16) for moment in moments]
        gathered = [lax.all_gather(low, "dp", axis=0, tiled=True) for low in lows]
        orth = owner_results(gathered, dp_place, dp_count)
        pieces = [
            lax.dynamic_slice_in_dim(
                owner_send(orth[number], number % dp_count),
                dp_place * lows[number].shape[0],
                lows[number].shape[0],
                0,
            )
            for number in range(6)
        ]
        branch_orth, expand_orth = jnp.stack(pieces[:2]), jnp.stack(pieces[3:5])
        out, con = pieces[2], pieces[5]

    def stepped(weight, orth, axis):
        count = orth.shape[axis]
        piece = lax.dynamic_slice_in_dim(weight, dp_place * count, count, axis).astype(f32)
        tall = max(1.0, weight.shape[axis] / weight.shape[axis + 1]) ** 0.5
        return piece - muon_rate * tall * orth.astype(f32)

    branch_new = stepped(branch_weights, branch_orth, 1)
    expand_new = stepped(expand_weights, expand_orth, 1)
    output_new = stepped(output_weights, out, 0)
    contract_new = stepped(contract_weights, con, 0)
    gates_moment = momentum_rate * gates_momentum + gates_total
    gate_sq = jnp.mean(gates_moment * gates_moment, axis=(2, 3), keepdims=True)
    gates_new = gate_blocks.astype(f32) - gate_rate * gates_moment * lax.rsqrt(gate_sq + eps_norm)
    vectors_moment, vectors_new = grouped_step(
        vectors_total, vectors_momentum, mixer_vectors, vector_rate
    )
    gains_moment, gains_new = grouped_step(gains_total, gains_momentum, norm_gains, vector_rate)
    return (
        block_output,
        input_grad,
        gains_total,
        branch_sum[:, None],
        vectors_total,
        gates_total,
        output_sum[None],
        expand_sum[:, None],
        contract_sum[None],
        gains_new,
        branch_new[:, None],
        vectors_new,
        gates_new,
        output_new[None],
        expand_new[:, None],
        contract_new[None],
        gains_moment,
        branch_moment[:, None],
        vectors_moment,
        gates_moment,
        output_moment[None],
        expand_moment[:, None],
        contract_moment[None],
    )


def solution(mesh):
    return jax.shard_map(
        shards,
        mesh=mesh,
        in_specs=(
            P("dp", "col"),
            P("dp", None),
            P("dp", "col"),
            P(None, "col"),
            P(None, "col", "row"),
            P(None, "row"),
            P(None, "row", None, None),
            P("row", "col"),
            P(None, "col", "row"),
            P("row", "col"),
            P(None, "col"),
            P(None, "col", "dp", "row"),
            P(None, "row"),
            P(None, "row", None, None),
            P("row", "dp", "col"),
            P(None, "col", "dp", "row"),
            P("row", "dp", "col"),
        ),
        out_specs=(
            P("dp", "col"),
            P("dp", "col"),
            P(None, "col"),
            P(None, "col", "dp", "row"),
            P(None, "row"),
            P(None, "row", None, None),
            P("row", "dp", "col"),
            P(None, "col", "dp", "row"),
            P("row", "dp", "col"),
            P(None, "col"),
            P(None, "col", "dp", "row"),
            P(None, "row"),
            P(None, "row", None, None),
            P("row", "dp", "col"),
            P(None, "col", "dp", "row"),
            P("row", "dp", "col"),
            P(None, "col"),
            P(None, "col", "dp", "row"),
            P(None, "row"),
            P(None, "row", None, None),
            P("row", "dp", "col"),
            P(None, "col", "dp", "row"),
            P("row", "dp", "col"),
        ),
        check_vma=False,
    )
```

```python
import functools

import jax
import jax.numpy as jnp
from jax import lax
from jax.experimental import pallas as pl
from jax.experimental.pallas import tpu as pltpu
from jax.sharding import PartitionSpec as P

CONV = 4
GROUP = 128
HS = 256


eps_norm = 1e-06
eps_frob = 1e-07
poly_first = 3.4445
poly_second = -4.775
poly_third = 2.0315
momentum_rate = 0.9
muon_rate = 0.1
gate_rate = 0.02
vector_rate = 0.3
decay_scale = 8.0


def broadcast(value, axis, source):
    kept = jnp.where(lax.axis_index(axis) == source, value, 0).astype(value.dtype)
    return lax.psum(kept, axis)


def from_behind(value, axis, steps):
    count = lax.axis_size(axis)
    initial, last = (max(0, -steps), min(count, count - steps))
    return lax.ppermute(value, axis, [(source, source + steps) for source in range(initial, last)])


def prefix(value, axis, combine, identity, reverse):
    count, here = (lax.axis_size(axis), lax.axis_index(axis))
    joined = lax.all_gather(jnp.stack(value), axis)
    everything = tuple(joined[:, k] for k in range(len(value)))
    start = jax.tree.map(
        lambda part, zero: jnp.broadcast_to(jnp.asarray(zero, part.dtype), part.shape),
        value,
        identity,
    )

    def lap(k, before):
        at = count - 1 - k if reverse else k
        reached = at > here if reverse else at < here
        new = combine(before, jax.tree.map(lambda part: part[at], everything))
        return jax.tree.map(lambda a, b: jnp.where(reached, a, b), new, before)

    return lax.fori_loop(0, count, lap, start)


def gelu_tanh(value):
    return jax.nn.gelu(value, approximate=True)


def product(left, right):
    return jnp.dot(left, right, preferred_element_type=jnp.float32)


def product_tn(left, right):
    return lax.dot_general(
        left, right, (((0,), (0,)), ((), ())), preferred_element_type=jnp.float32
    )


def product_nt(left, right):
    return lax.dot_general(
        left, right, (((1,), (1,)), ((), ())), preferred_element_type=jnp.float32
    )


def link(first, second):
    return (first[0] * second[0], second[0] * first[1] + second[1])


def scan_kernel(reverse, decay_ref, value_ref, prod_ref, sum_ref):
    rows, lanes = decay_ref.shape
    groups = rows // 8

    def lap(k, carry):
        base = pl.multiple_of((groups - 1 - k if reverse else k) * 8, 8)
        decay = decay_ref[pl.ds(base, 8), :]
        value = value_ref[pl.ds(base, 8), :]
        prod, total = carry
        prods, totals = [None] * 8, [None] * 8
        for j in range(7, -1, -1) if reverse else range(8):
            prod = decay[j : j + 1] * prod
            total = decay[j : j + 1] * total + value[j : j + 1]
            prods[j], totals[j] = prod, total
        prod_ref[pl.ds(base, 8), :] = jnp.concatenate(prods, axis=0)
        sum_ref[pl.ds(base, 8), :] = jnp.concatenate(totals, axis=0)
        return (prod, total)

    start = (jnp.ones((1, lanes), jnp.float32), jnp.zeros((1, lanes), jnp.float32))
    lax.fori_loop(0, groups, lap, start)


def linear_scan(decay, value, reverse):
    shape = jax.ShapeDtypeStruct(decay.shape, jnp.float32)
    return pl.pallas_call(
        functools.partial(scan_kernel, reverse),
        out_shape=(shape, shape),
        compiler_params=pltpu.CompilerParams(vmem_limit_bytes=16 * 1024 * 1024),
    )(decay, value)


MESH = pl.DeviceIdType.MESH
MIB = 1024 * 1024


def col_places():
    me = lax.axis_index("col")
    near_bit = lax.rem(me, 2)
    far_bit = lax.div(me, 2)
    return (me, near_bit, far_bit, me + 1 - 2 * near_bit, lax.rem(me + 2, 4))


def greet(axis_places):
    barrier = pltpu.get_barrier_semaphore()
    for axis, place in axis_places:
        pl.semaphore_signal(barrier, inc=1, device_id={axis: place}, device_id_type=MESH)
    pl.semaphore_wait(barrier, len(axis_places))


def dot_nn(left, right):
    return lax.dot_general(
        left, right, (((1,), (0,)), ((), ())), preferred_element_type=jnp.float32
    )


def dot_nt(left, right):
    return lax.dot_general(
        left, right, (((1,), (1,)), ((), ())), preferred_element_type=jnp.float32
    )


def columns_of(j, width, per):
    return (lax.div(j, per), pl.ds(pl.multiple_of(lax.rem(j, per) * width, width), width))


def share_parts(axis, buf, send_sem, recv_sem):
    me = lax.axis_index(axis)

    def copy(step):
        return pltpu.make_async_remote_copy(
            src_ref=buf.at[me],
            dst_ref=buf.at[me],
            send_sem=send_sem.at[step],
            recv_sem=recv_sem.at[step],
            device_id={axis: lax.rem(me + step, 4)},
            device_id_type=MESH,
        )

    def start(value):
        buf[me] = value
        for step in range(1, 4):
            copy(step).start()

    def arrive():
        for step in range(1, 4):
            copy(step).wait_recv()

    def finish():
        for step in range(1, 4):
            copy(step).wait_send()

    return (start, arrive, finish)


def col_peers():
    me = lax.axis_index("col")
    return [("col", lax.rem(me + step, 4)) for step in range(1, 4)]


def row_scales(values, share, buf):
    tokens, features = values.shape
    start, arrive, finish = share
    squares = jnp.sum(values * values, axis=1, keepdims=True)
    start(jnp.broadcast_to(squares, (tokens, 128)).T[:8])
    arrive()
    total = buf[0] + buf[1] + buf[2] + buf[3]
    scales = lax.rsqrt(total / (4 * features) + eps_norm)
    finish()
    return (scales, jnp.broadcast_to(scales[:1], (128, tokens)).T[:, :1])


def spread_kernel(
    flip, normed, *refs
):
    if normed:
        stream, gain, w, out, low_out, scale_out, lhs, nbuf, nsend, nrecv = refs[:10]
        refs = refs[10:]
    else:
        lhs, w, out = refs[:3]
        refs = refs[3:]
    wbuf, send1, recv1, own, send2, recv2, wsem, s1s, s1r, s2s, s2r = refs
    chunks, rows, width = send2.shape
    per = out.shape[2] // width
    me, near_bit, far_bit, near, far = col_places()
    depth = lhs.shape[3]

    def w_copy(j):
        k, cols = columns_of(j, width, per)
        return pltpu.make_async_copy(
            w.at[cols, :] if flip else w.at[k, :, cols], wbuf.at[j], wsem.at[j]
        )

    def near_copy(j):
        return pltpu.make_async_remote_copy(
            src_ref=send1.at[j],
            dst_ref=recv1.at[j],
            send_sem=s1s.at[j],
            recv_sem=s1r.at[j],
            device_id={"col": near},
            device_id_type=MESH,
        )

    def far_copy(j):
        return pltpu.make_async_remote_copy(
            src_ref=send2.at[j],
            dst_ref=recv2.at[j],
            send_sem=s2s.at[j],
            recv_sem=s2r.at[j],
            device_id={"col": far},
            device_id_type=MESH,
        )

    def loop(count, act):
        def lap(j, carry):
            act(j)
            return carry

        lax.fori_loop(0, count, lap, 0)

    loop(chunks, lambda j: w_copy(j).start())
    if normed:
        greet(col_peers())
        values = stream[...].astype(jnp.float32)
        scales, column = row_scales(values, share_parts("col", nbuf, nsend, nrecv), nbuf)
        scale_out[...] = scales
        low = (values * column * gain[...]).astype(jnp.bfloat16)
        low_out[...] = low
        lhs[...] = low.reshape(lhs.shape)
    else:
        greet((("col", near), ("col", far)))
    dot = dot_nt if flip else dot_nn

    def first(j):
        w_copy(j).wait()
        part = wbuf[j]
        theirs = dot(lhs[:, 1 - near_bit].reshape(2 * rows, depth), part)
        send1[j] = theirs.astype(jnp.bfloat16).reshape(2, rows, width)
        near_copy(j).start()
        mine = dot(lhs[:, near_bit].reshape(2 * rows, depth), part)
        own[j] = mine.reshape(2, rows, width)

    def second(j):
        near_copy(j).wait_recv()
        going = own[j, 1 - far_bit] + recv1[j, 1 - far_bit].astype(jnp.float32)
        send2[j] = going.astype(jnp.bfloat16)
        far_copy(j).start()
        own[j, far_bit] = own[j, far_bit] + recv1[j, far_bit].astype(jnp.float32)

    def third(j):
        far_copy(j).wait_recv()
        k, cols = columns_of(j, width, per)
        out[k, :, cols] = own[j, far_bit] + recv2[j].astype(jnp.float32)

    first(0)

    def both(j):
        first(j + 1)
        second(j)

    loop(chunks - 1, both)
    second(chunks - 1)
    loop(chunks, third)

    def drain(j):
        near_copy(j).wait_send()
        far_copy(j).wait_send()

    loop(chunks, drain)


def spread_product(lhs, w, flip, width, collective, gain=None):
    tokens, depth = lhs.shape
    rows = tokens // 4
    pairs = 1 if flip else w.shape[0]
    total = w.shape[0] if flip else w.shape[2]
    chunks = pairs * total // width
    tile = (width, depth) if flip else (depth, width)
    bf16, f32 = jnp.bfloat16, jnp.float32
    local = pl.BlockSpec(memory_space=pltpu.VMEM)
    shapes = [jax.ShapeDtypeStruct((pairs, rows, total), f32)]
    scratch = []
    if gain is None:
        inputs = [lhs.reshape(2, 2, rows, depth)]
    else:
        inputs = [lhs, gain[None]]
        shapes += [
            jax.ShapeDtypeStruct((tokens, depth), bf16),
            jax.ShapeDtypeStruct((8, tokens), f32),
        ]
        scratch = [pltpu.VMEM((2, 2, rows, depth), bf16), pltpu.VMEM((4, 8, tokens), f32)]
        scratch += [pltpu.SemaphoreType.DMA((4,))] * 2
    result = pl.pallas_call(
        functools.partial(spread_kernel, flip, gain is not None),
        out_shape=tuple(shapes),
        in_specs=[local] * len(inputs) + [pl.BlockSpec(memory_space=pl.ANY)],
        out_specs=[local] * len(shapes),
        scratch_shapes=scratch
        + [
            pltpu.VMEM((chunks,) + tile, bf16),
            pltpu.VMEM((chunks, 2, rows, width), bf16),
            pltpu.VMEM((chunks, 2, rows, width), bf16),
            pltpu.VMEM((chunks, 2, rows, width), f32),
            pltpu.VMEM((chunks, rows, width), bf16),
            pltpu.VMEM((chunks, rows, width), bf16),
        ]
        + [pltpu.SemaphoreType.DMA((chunks,))] * 5,
        compiler_params=pltpu.CompilerParams(
            collective_id=collective, has_side_effects=True, vmem_limit_bytes=56 * MIB
        ),
    )(*inputs, w)
    return result[0] if gain is None else result


def meet_kernel(flip, grad_mode, *refs):
    lone = grad_mode == "lone"
    if lone:
        piece, side, all_out, grad_out, buf, osem, ns, nr, fs, fr, rs, rr, stage, gsem = refs
    elif grad_mode:
        piece, w, side, prod, grad_out = refs[:5]
        refs = refs[5:]
    else:
        piece, w, stream, gain, all_out, prod, low_out, scale_out = refs[:8]
        nbuf, nsend, nrecv = refs[-3:]
        refs = refs[8:-3]
    if not lone:
        wbuf, buf, acc, sendx, recvx, wsem, osem, ns, nr, fs, fr, rs, rr, xs, xr = refs[:15]
    if grad_mode and not lone:
        stage, gsem = refs[15:]
    chunks, _, _, rows, width = buf.shape
    per = piece.shape[2] // width
    me, near_bit, far_bit, near, far = col_places()
    across = 1 - lax.axis_index("row")
    f32, bf16 = jnp.float32, jnp.bfloat16

    def w_copy(j):
        k, cols = columns_of(j, width, per)
        return pltpu.make_async_copy(
            w.at[k, :, cols] if flip else w.at[cols, :], wbuf.at[j], wsem.at[j]
        )

    def move(j, source, near_place, far_place, sems, target):
        return pltpu.make_async_remote_copy(
            src_ref=source,
            dst_ref=buf.at[j, far_place, near_place],
            send_sem=sems[0].at[j],
            recv_sem=sems[1].at[j],
            device_id={"col": target},
            device_id_type=MESH,
        )

    def piece_at(j):
        k, cols = columns_of(j, width, per)
        return piece.at[k, :, cols]

    def far_copy(j):
        return move(j, piece_at(j), near_bit, far_bit, (fs, fr), far)

    def near_copy(j):
        return move(j, piece_at(j), near_bit, far_bit, (ns, nr), near)

    def relay(j):
        return move(j, buf.at[j, 1 - far_bit, near_bit], near_bit, 1 - far_bit, (rs, rr), near)

    def out_copy(j):
        k, cols = columns_of(j, width, per)
        return pltpu.make_async_copy(buf.at[j], all_out.at[k, :, :, :, cols], osem.at[j])

    def cross(half):
        return pltpu.make_async_remote_copy(
            src_ref=sendx.at[half],
            dst_ref=recvx.at[half],
            send_sem=xs.at[half],
            recv_sem=xr.at[half],
            device_id={"row": across},
            device_id_type=MESH,
        )

    def loop(count, act):
        def lap(j, carry):
            act(j)
            return carry

        lax.fori_loop(0, count, lap, 0)

    if not lone:
        loop(chunks, lambda j: w_copy(j).start())
    if lone:
        greet((("col", near), ("col", far)))
    elif grad_mode:
        greet((("col", near), ("col", far), ("row", across)))
    else:
        greet(col_peers() + [("row", across)])

    def begin(j):
        far_copy(j).start()
        near_copy(j).start()
        k, cols = columns_of(j, width, per)
        buf[j, far_bit, near_bit] = piece[k, :, cols]

    loop(chunks, begin)
    if not lone:
        acc[...] = jnp.zeros_like(acc)
    dot = dot_nt if flip else dot_nn

    def add(j, half):
        both = buf[j, half].reshape(2 * rows, width)
        acc[half] = acc[half] + dot(both, wbuf[j])

    def here(j):
        near_copy(j).wait_recv()
        if not lone:
            w_copy(j).wait()
            add(j, far_bit)

    loop(chunks, here)
    if not lone:
        sendx[far_bit] = acc[far_bit].astype(bf16)
        cross(far_bit).start()

    def grad_copy(j):
        return grad_moves(j)

    if grad_mode == "wide":
        parts = grad_out.shape[0]

        def grad_moves(j):
            k, cols = columns_of(j, width, per)
            return pltpu.make_async_copy(
                stage.at[lax.rem(j, 2)], grad_out.at[:, k, :, cols], gsem.at[lax.rem(j, 2)]
            )

        def grad_part(j):
            block = buf[j].reshape(4 * rows, width)
            total = dot_nn(side[...], block).astype(bf16)
            stage[lax.rem(j, 2)] = total.reshape(stage.shape[1:])

    if lone:

        def grad_moves(j):
            return pltpu.make_async_copy(
                stage.at[lax.rem(j, 2)],
                grad_out.at[pl.ds(pl.multiple_of(j * width, width), width), :],
                gsem.at[lax.rem(j, 2)],
            )

        def grad_part(j):
            block = buf[j].reshape(4 * rows, width)
            stage[lax.rem(j, 2)] = dot_nn(block.T, side[...]).astype(bf16)

    def pass_on(j):
        far_copy(j).wait_recv()
        relay(j).start()

    def there(j):
        relay(j).wait_recv()
        if lone or not grad_mode:
            out_copy(j).start()
        if not lone:
            add(j, 1 - far_bit)
        if grad_mode:

            @pl.when(j >= 2)
            def _():
                grad_moves(j - 2).wait()

            grad_part(j)
            grad_moves(j).start()

    pass_on(0)

    def both(j):
        pass_on(j + 1)
        there(j)

    loop(chunks - 1, both)
    there(chunks - 1)
    if not lone:
        sendx[1 - far_bit] = acc[1 - far_bit].astype(bf16)
        cross(1 - far_bit).start()

        def settle(half):
            cross(half).wait_recv()
            prod[half] = sendx[half].astype(f32) + recvx[half].astype(f32)

        settle(far_bit)
        settle(1 - far_bit)
    if not grad_mode:
        values = prod[...].reshape(stream.shape) + stream[...].astype(f32)
        prod[...] = values.reshape(prod.shape)
        scales, column = row_scales(values, share_parts("col", nbuf, nsend, nrecv), nbuf)
        scale_out[...] = scales
        low_out[...] = (values * column * gain[...]).astype(bf16)

    def drain(j):
        near_copy(j).wait_send()
        far_copy(j).wait_send()
        relay(j).wait_send()
        if lone or not grad_mode:
            out_copy(j).wait()

    loop(chunks, drain)
    if not lone:
        cross(far_bit).wait_send()
        cross(1 - far_bit).wait_send()
    if grad_mode:
        for j in range(max(0, chunks - 2), chunks):
            grad_moves(j).wait()


def meet_gradient(piece, width, collective, side):
    pairs, rows, total = piece.shape
    chunks = pairs * total // width
    bf16 = jnp.bfloat16
    local = pl.BlockSpec(memory_space=pltpu.VMEM)
    anywhere = pl.BlockSpec(memory_space=pl.ANY)
    everything, gradient = pl.pallas_call(
        functools.partial(meet_kernel, False, "lone"),
        out_shape=(
            jax.ShapeDtypeStruct((pairs, 2, 2, rows, total), bf16),
            jax.ShapeDtypeStruct((total, side.shape[1]), bf16),
        ),
        in_specs=[local, local],
        out_specs=[anywhere, anywhere],
        scratch_shapes=[pltpu.VMEM((chunks, 2, 2, rows, width), bf16)]
        + [pltpu.SemaphoreType.DMA((chunks,))] * 7
        + [pltpu.VMEM((2, width, side.shape[1]), bf16), pltpu.SemaphoreType.DMA((2,))],
        compiler_params=pltpu.CompilerParams(
            collective_id=collective, has_side_effects=True, vmem_limit_bytes=40 * MIB
        ),
    )(piece, side)
    return (everything.reshape(pairs, 4 * rows, total), gradient)


def meet_product(piece, w, flip, width, collective, side=None, grad_mode=None, parts=1, stream=None, gain=None):
    pairs, rows, total = piece.shape
    features = w.shape[1]
    chunks = pairs * total // width
    tile = (features, width) if flip else (width, features)
    bf16, f32 = jnp.bfloat16, jnp.float32
    inputs, in_specs = (
        [piece, w],
        [pl.BlockSpec(memory_space=pltpu.VMEM), pl.BlockSpec(memory_space=pl.ANY)],
    )
    shapes = [jax.ShapeDtypeStruct((2, 2 * rows, features), f32)]
    out_specs = [pl.BlockSpec(memory_space=pltpu.VMEM)]
    scratch = [
        pltpu.VMEM((chunks,) + tile, bf16),
        pltpu.VMEM((chunks, 2, 2, rows, width), bf16),
        pltpu.VMEM((2, 2 * rows, features), f32),
        pltpu.VMEM((2, 2 * rows, features), bf16),
        pltpu.VMEM((2, 2 * rows, features), bf16),
    ]
    scratch += [pltpu.SemaphoreType.DMA((chunks,))] * 8 + [pltpu.SemaphoreType.DMA((2,))] * 2
    if grad_mode:
        inputs.append(side)
        in_specs.append(pl.BlockSpec(memory_space=pltpu.VMEM))
        out_specs.append(pl.BlockSpec(memory_space=pl.ANY))
        if grad_mode == "wide":
            shape = (parts, pairs, side.shape[0] // parts, total)
            stage = (2, parts, side.shape[0] // parts, width)
        else:
            shape = (total, side.shape[1])
            stage = (2, width, side.shape[1])
        shapes.append(jax.ShapeDtypeStruct(shape, bf16))
        scratch += [pltpu.VMEM(stage, bf16), pltpu.SemaphoreType.DMA((2,))]
    else:
        local = pl.BlockSpec(memory_space=pltpu.VMEM)
        inputs += [stream, gain[None]]
        in_specs += [local, local]
        shapes.insert(0, jax.ShapeDtypeStruct((pairs, 2, 2, rows, total), bf16))
        out_specs.insert(0, pl.BlockSpec(memory_space=pl.ANY))
        shapes.append(jax.ShapeDtypeStruct((4 * rows, features), bf16))
        shapes.append(jax.ShapeDtypeStruct((8, 4 * rows), f32))
        out_specs += [local, local]
        scratch += [pltpu.VMEM((4, 8, 4 * rows), f32)] + [pltpu.SemaphoreType.DMA((4,))] * 2
    result = pl.pallas_call(
        functools.partial(meet_kernel, flip, grad_mode),
        out_shape=tuple(shapes),
        in_specs=in_specs,
        out_specs=out_specs,
        scratch_shapes=scratch,
        compiler_params=pltpu.CompilerParams(
            collective_id=collective, has_side_effects=True, vmem_limit_bytes=56 * MIB
        ),
    )(*inputs)
    if grad_mode:
        return (result[0].reshape(4 * rows, features), result[1])
    return (
        result[0].reshape(pairs, 4 * rows, total),
        result[1].reshape(4 * rows, features),
        result[2],
        result[3][0],
    )


def block_steps(x, acc, gram, poly):
    side, total = x.shape
    step = 256
    count = total // step
    span = 1280 if total % 1280 == 0 else step
    f32, bf16 = jnp.float32, jnp.bfloat16

    def tile(k, size):
        return pl.ds(pl.multiple_of(k * size, size), size)

    def square(k, total):
        values = x[:, tile(k, step)].astype(f32)
        return total + jnp.sum(values * values, axis=0, keepdims=True)

    sums = lax.fori_loop(0, count, square, jnp.zeros((1, step), f32))
    norm = jnp.sqrt(jnp.sum(sums, axis=1, keepdims=True)) + eps_frob

    def divide(k, carry):
        x[:, tile(k, step)] = (x[:, tile(k, step)].astype(f32) / norm).astype(bf16)
        return carry

    lax.fori_loop(0, count, divide, 0)

    def lap(k, carry):
        acc[...] = jnp.zeros_like(acc)

        def add(j, inner):
            block = x[:, tile(j, span)]
            acc[:step, :step] = acc[:step, :step] + dot_nt(block[:step], block[:step])
            acc[step:, :] = acc[step:, :] + dot_nt(block[step:], block)
            return inner

        lax.fori_loop(0, total // span, add, 0)
        acc[:step, step:] = acc[step:, :step].T
        low = acc[...].astype(bf16)
        gram[...] = low
        square_gram = dot_nn(low, gram[...])
        poly[...] = (poly_second * low.astype(f32) + poly_third * square_gram).astype(bf16)

        def advance(j, inner):
            block = x[:, tile(j, span)]
            fresh = poly_first * block.astype(f32) + dot_nn(poly[...], block)
            x[:, tile(j, span)] = fresh.astype(bf16)
            return inner

        lax.fori_loop(0, total // span, advance, 0)
        return carry

    lax.fori_loop(0, 5, lap, 0)


def work_space(side):
    return [
        pltpu.VMEM((side, side), jnp.float32),
        pltpu.VMEM((side, side), jnp.bfloat16),
        pltpu.VMEM((side, side), jnp.bfloat16),
    ]


def gates_kernel(conv, first, second, out, full, came, send_sem, recv_sem):
    me = lax.axis_index("col")
    count = out.shape[0]
    greet([("col", lax.rem(me + step, 4)) for step in range(1, 4)])
    for k, grads in enumerate((first, second)):
        for head in range(conv.shape[1] // HS):
            columns = slice(head * HS, (head + 1) * HS)
            block = dot_nn(conv[:, columns].T, grads[:, columns])
            full[k * HS : (k + 1) * HS, columns] = block.astype(jnp.bfloat16)

    def part(place):
        return full.at[pl.ds(pl.multiple_of(place * count, count), count)]

    def copy(step):
        target = lax.rem(me + step, 4)
        return pltpu.make_async_remote_copy(
            src_ref=part(target),
            dst_ref=came.at[step - 1],
            send_sem=send_sem.at[step - 1],
            recv_sem=recv_sem.at[step - 1],
            device_id={"col": target},
            device_id_type=MESH,
        )

    for step in range(1, 4):
        copy(step).start()
    total = part(me)[...].astype(jnp.float32)
    for step in range(1, 4):
        copy(step).wait_recv()
        total = total + came[step - 1].astype(jnp.float32)
    out[...] = total.astype(jnp.bfloat16)
    for step in range(1, 4):
        copy(step).wait_send()


def gates_product(conv, first, second):
    lanes = conv.shape[1]
    count = 2 * HS // 4
    bf16 = jnp.bfloat16
    return pl.pallas_call(
        gates_kernel,
        out_shape=jax.ShapeDtypeStruct((count, lanes), bf16),
        in_specs=[pl.BlockSpec(memory_space=pltpu.VMEM)] * 3,
        out_specs=pl.BlockSpec(memory_space=pltpu.VMEM),
        scratch_shapes=[
            pltpu.VMEM((2 * HS, lanes), bf16),
            pltpu.VMEM((3, count, lanes), bf16),
            pltpu.SemaphoreType.DMA((3,)),
            pltpu.SemaphoreType.DMA((3,)),
        ],
        compiler_params=pltpu.CompilerParams(
            collective_id=12, has_side_effects=True, vmem_limit_bytes=16 * MIB
        ),
    )(conv, first, second)


def token_total(values):
    return lax.psum(values, "col")


def dp_sum(grad):
    low = grad.astype(jnp.bfloat16)
    return lax.psum_scatter(low, "dp", scatter_dimension=0, tiled=True).astype(jnp.float32)


def pair_sum(grad, dp_count):
    if grad.shape[0] == dp_count:
        return lax.psum_scatter(grad, "dp", scatter_dimension=0)
    return lax.psum_scatter(grad[0], "dp", scatter_dimension=1, tiled=True)


def owner_send(block, root):
    return broadcast(block, "dp", root)


def norm_backward(stream, scale, gain, grad_normed, width):
    weighted = grad_normed * gain[None, :]
    inner = token_total(jnp.sum(stream * weighted, axis=1))
    grad_stream = (
        scale[:, None] * weighted - stream * (scale * scale * scale * inner / width)[:, None]
    )
    grad_gain = jnp.sum(grad_normed * stream * scale[:, None], axis=0)
    return (grad_stream, grad_gain)


def orthogonalize(block):
    work = block
    values = work.astype(jnp.float32)
    work = (values / (jnp.sqrt(jnp.sum(values * values)) + eps_frob)).astype(jnp.bfloat16)
    for step in range(5):
        gram = product_nt(work, work).astype(jnp.bfloat16)
        poly = (poly_second * gram.astype(jnp.float32) + poly_third * product(gram, gram)).astype(
            jnp.bfloat16
        )
        work = (poly_first * work.astype(jnp.float32) + product(poly, work)).astype(jnp.bfloat16)
    return work


def owner_results(blocks, dp_place, dp_count):
    results = [None, None, None, None, None, None]
    for members in ((0, 1, 2), (3, 4, 5)):
        flipped = [blocks[number].shape[0] > blocks[number].shape[1] for number in members]
        wide = [
            blocks[number].T if turn else blocks[number] for number, turn in zip(members, flipped)
        ]
        chosen = wide[0]
        for number, candidate in zip(members[1:], wide[1:]):
            chosen = jnp.where(dp_place == number % dp_count, candidate, chosen)
        done = orthogonalize(chosen)
        for number, turn in zip(members, flipped):
            kept = jnp.where(dp_place == number % dp_count, done, jnp.zeros_like(done))
            results[number] = kept.T if turn else kept
    return results


def dp_moves(moves, sems):
    local_sem, send_sem, recv_sem = sems
    me = lax.axis_index("dp")

    def remote(k, sender, target):
        pairs, source, destination = moves[k]
        return pltpu.make_async_remote_copy(
            src_ref=source(sender, target),
            dst_ref=destination(sender, target),
            send_sem=send_sem.at[k, target],
            recv_sem=recv_sem.at[k, sender],
            device_id={"dp": target},
            device_id_type=MESH,
        )

    def local(k, place):
        pairs, source, destination = moves[k]
        return pltpu.make_async_copy(
            source(place, place), destination(place, place), local_sem.at[k]
        )

    def each(chosen, act):
        for k in chosen:
            for sender, target in moves[k][0]:
                act(k, sender, target)

    def start_one(k, sender, target):
        @pl.when(me == sender)
        def _():
            if sender == target:
                local(k, sender).start()
            else:
                remote(k, sender, target).start()

    def arrive_one(k, sender, target):
        @pl.when(me == target)
        def _():
            if sender == target:
                local(k, sender).wait()
            else:
                remote(k, sender, target).wait_recv()

    def sent_one(k, sender, target):
        if sender != target:

            @pl.when(me == sender)
            def _():
                remote(k, sender, target).wait_send()

    return (
        lambda *chosen: each(chosen, start_one),
        lambda *chosen: each(chosen, arrive_one),
        lambda *chosen: each(chosen, sent_one),
    )


def rows_at(ref, place):
    def pick(sender, target):
        index = sender if place == "sender" else target
        count = ref.shape[0] // 4
        return ref.at[pl.ds(index * count, count)]

    return pick


def entry(ref, place):
    return lambda sender, target: ref.at[sender if place == "sender" else target]


def whole(ref):
    return lambda sender, target: ref


def to_owner(owner):
    return [(sender, owner) for sender in ((owner + step) % 4 for step in range(4))]


def from_owner(owner):
    return [(owner, target) for target in ((owner + step) % 4 for step in range(4))]


SMALL_OWNER, CON_OWNER, GATE_OWNER, UP_OWNER = (2, 1, 3, 0)


def pieces_at_owner(e0, e1, con, later):
    me = lax.axis_index("dp")
    rows = e0.shape[0]
    packed = jnp.concatenate(
        [con[k * rows : (k + 1) * rows] for k in range(con.shape[0] // rows)], axis=1
    )

    def piece_for(owner):
        return jnp.where(owner == GATE_OWNER, e0, jnp.where(owner == UP_OWNER, e1, packed))

    leaving = [piece_for(lax.rem(me + step, 4)) for step in range(4)]
    leaving, later = lax.optimization_barrier((leaving, later))
    pieces = leaving[:1]
    for step in range(1, 4):
        pairs = [(sender, (sender + step) % 4) for sender in range(4)]
        pairs = [pair for pair in pairs if pair[1] != SMALL_OWNER]
        pieces.append(lax.ppermute(leaving[step], "dp", pairs))
    return (pieces, later)


def tail_kernel(*refs):
    large, (b0, b1, out) = refs[:4], refs[4:7]
    gates_piece, col_part, dp_part = refs[7:10]
    expand_o, con_o, branch_o, out_o, gates_o, col_o, dp_o = refs[10:17]
    x, packed, pieces, first, second, third, out_v, acc, gram, poly, load_sem = refs[17:28]
    col_buf, dp_buf, gates_dp, gates_col = refs[28:32]
    shares = [
        share_parts("col", col_buf, *refs[32:34]),
        share_parts("dp", dp_buf, *refs[34:36]),
        share_parts("dp", gates_dp, *refs[36:38]),
        share_parts("col", gates_col, *refs[38:40]),
    ]
    sems = refs[40:]
    place = lax.axis_index("col")
    me = lax.axis_index("dp")
    small = out.shape[0]
    width = pieces.shape[1]
    side = x.shape[0]
    rows = side // 4
    moves = [
        (to_owner(SMALL_OWNER), whole(b0), rows_at(first, "sender")),
        (to_owner(SMALL_OWNER), whole(b1), rows_at(second, "sender")),
        (to_owner(SMALL_OWNER), whole(out), entry(out_v, "sender")),
        (from_owner(GATE_OWNER), rows_at(x, "target"), whole(expand_o.at[0])),
        (from_owner(UP_OWNER), rows_at(x, "target"), whole(expand_o.at[1])),
        (from_owner(CON_OWNER), entry(pieces, "target"), whole(con_o)),
        (from_owner(SMALL_OWNER), rows_at(first, "target"), whole(branch_o.at[0])),
        (from_owner(SMALL_OWNER), rows_at(second, "target"), whole(branch_o.at[1])),
        (from_owner(SMALL_OWNER), entry(out_v, "target"), whole(out_o)),
    ]
    start, arrive, sent = dp_moves(moves, sems)
    greet(
        [("dp", lax.rem(me + step, 4)) for step in range(1, 4)]
        + [("col", lax.rem(place + step, 4)) for step in range(1, 4)]
    )
    shares[0][0](col_part[...])
    shares[2][0](gates_piece[...])
    start(0, 1, 2)
    shares[0][1]()
    summed = col_buf[0] + col_buf[1] + col_buf[2] + col_buf[3]
    col_o[...] = summed
    shares[1][0](jnp.concatenate([summed[:8], dp_part[...]], axis=0))
    shares[2][1]()
    shares[3][0](gates_dp[...].reshape(gates_col.shape[1:]))

    def load(owner, target):
        copies = [
            pltpu.make_async_copy(large[step], target((owner - step) % 4), load_sem.at[step])
            for step in range(4)
        ]
        for copy in copies:
            copy.start()
        for copy in copies:
            copy.wait()

    @pl.when(me == CON_OWNER)
    def _():
        load(CON_OWNER, lambda j: packed.at[j])
        for j in range(4):
            for k in range(width // rows):
                first_column = j * width + k * rows
                x[:, first_column : first_column + rows] = packed[j, :, k * side : (k + 1) * side].T

    @pl.when(me == GATE_OWNER)
    def _():
        load(GATE_OWNER, lambda j: x.at[pl.ds(j * rows, rows)])

    @pl.when(me == UP_OWNER)
    def _():
        load(UP_OWNER, lambda j: x.at[pl.ds(j * rows, rows)])

    @pl.when(me != SMALL_OWNER)
    def _():
        block_steps(x, acc, gram, poly)

    @pl.when(me == CON_OWNER)
    def _():
        for j in range(4):
            pieces[j] = x[:, j * width : (j + 1) * width].T

    start(3, 4, 5)
    for k, part in enumerate((first, second, third)):
        arrive(k)

        @pl.when(me == SMALL_OWNER)
        def _():
            if k == 2:
                for j in range(4):
                    part[:, j * small : (j + 1) * small] = out_v[j].T
            block_steps(part, acc, gram, poly)
            if k == 2:
                for j in range(4):
                    out_v[j] = part[:, j * small : (j + 1) * small].T

        start(6 + k)
    shares[1][1]()
    dp_o[...] = dp_buf[0] + dp_buf[1] + dp_buf[2] + dp_buf[3]
    shares[3][1]()
    half = gates_col.shape[1]
    for k in range(2):
        for head in range(gates_o.shape[1]):
            columns = slice(head * HS, (head + 1) * HS)
            for j in range(HS // half):
                lines = slice(j * half, (j + 1) * half)
                gates_o[k, head, lines, :] = gates_col[k * (HS // half) + j][:, columns]
    arrive(6, 7, 8, 3, 4, 5)
    sent(0, 1, 2, 3, 4, 5, 6, 7, 8)
    for share in shares:
        share[2]()


def finish_blocks(large, con_shape, b0, b1, out, gates_piece, col_part, dp_part):
    piece = large[0].shape
    rows, total = piece
    side = 4 * rows
    f32, bf16 = jnp.float32, jnp.bfloat16
    shape = jax.ShapeDtypeStruct
    small = pltpu.VMEM((side, b0.shape[1]), bf16)
    quarter = (4 * gates_piece.shape[0], gates_piece.shape[1])
    anywhere = pl.BlockSpec(memory_space=pl.ANY)
    local = pl.BlockSpec(memory_space=pltpu.VMEM)
    sems = pltpu.SemaphoreType.DMA
    shapes = [shape(s, bf16) for s in ((2,) + piece, con_shape, (2,) + b0.shape, out.shape)]
    shapes += [shape((2, quarter[1] // HS, HS, HS), bf16), shape(col_part.shape, f32)]
    shapes += [shape(col_part.shape, f32)]
    return pl.pallas_call(
        tail_kernel,
        out_shape=tuple(shapes),
        in_specs=[anywhere] * 7 + [local] * 3,
        out_specs=[anywhere] * 4 + [local] * 3,
        scratch_shapes=[
            pltpu.VMEM((side, total), bf16),
            pltpu.VMEM((4,) + piece, bf16),
            pltpu.VMEM((4,) + con_shape, bf16),
            small,
            small,
            small,
            pltpu.VMEM((4,) + out.shape, bf16),
        ]
        + work_space(side)
        + [sems((4,))]
        + [
            pltpu.VMEM((4,) + col_part.shape, f32),
            pltpu.VMEM((4,) + col_part.shape, f32),
            pltpu.VMEM((4,) + gates_piece.shape, bf16),
            pltpu.VMEM((4,) + quarter, bf16),
        ]
        + [sems((4,))] * 8
        + [sems((9,)), sems((9, 4)), sems((9, 4))],
        compiler_params=pltpu.CompilerParams(
            collective_id=0, has_side_effects=True, vmem_limit_bytes=40 * MIB
        ),
    )(*large, b0, b1, out, gates_piece, col_part, dp_part)


def grouped_step(grad, moment, weight, rate):
    new_moment = momentum_rate * moment + grad
    rows, cols = new_moment.shape
    grouped = new_moment.reshape(rows, cols // GROUP, GROUP)
    norm_sq = jnp.mean(grouped * grouped, axis=2, keepdims=True)
    update = (grouped * lax.rsqrt(norm_sq + eps_norm)).reshape(rows, cols)
    return (new_moment, weight - rate * update)


def shards(
    block_input,
    segment_ids,
    output_cotangent,
    norm_gains,
    branch_weights,
    mixer_vectors,
    gate_blocks,
    output_weights,
    expand_weights,
    contract_weights,
    gains_momentum,
    branch_momentum,
    vectors_momentum,
    gates_momentum,
    output_momentum,
    expand_momentum,
    contract_momentum,
):
    f32 = jnp.float32
    bf16 = jnp.bfloat16
    col_count = lax.axis_size("col")
    col_place = lax.axis_index("col")
    dp_count = lax.axis_size("dp")
    dp_place = lax.axis_index("dp")
    group_rows = block_input.shape[0]
    rows = group_rows // col_count
    lanes = mixer_vectors.shape[1]
    heads_here = lanes // HS
    feature_count = block_input.shape[1]
    width = feature_count * col_count
    first_row = col_place * rows
    reach = CONV - 1
    seg_row = segment_ids[0]
    seg_ext = jnp.concatenate(
        [jnp.full((reach,), -1, jnp.int32), seg_row, jnp.full((reach,), -2, jnp.int32)]
    )
    seg_here = lax.dynamic_slice_in_dim(seg_ext, first_row + reach, rows + reach)
    masks = []
    for shift in range(CONV):
        earlier = lax.dynamic_slice_in_dim(seg_ext, first_row + reach - shift, rows + reach)
        masks.append((earlier == seg_here).astype(f32))
    reset_rows = masks[1][:rows] < 0.5
    stream = block_input.astype(f32)
    branch_pre, normed_low, scale_rows = spread_product(
        block_input, branch_weights, False, 640, 2, norm_gains[0]
    )
    scale_one = scale_rows[0]
    contract_term = product_nt(output_cotangent, contract_weights).astype(bf16)
    contract_term, branch_pre = lax.optimization_barrier((contract_term, branch_pre))
    grad_activated = lax.psum_scatter(contract_term, "col", scatter_dimension=0, tiled=True)
    mixed = branch_pre[0]
    gelu_in = branch_pre[1]
    edge = from_behind(mixed[rows - reach :], "col", 1)
    extended = jnp.concatenate([edge, mixed], axis=0)
    windows = []
    conv_out = jnp.zeros((rows, lanes), f32) + mixer_vectors[CONV][None, :]
    for shift in range(CONV):
        window = extended[reach - shift : reach - shift + rows] * masks[shift][:rows, None]
        windows.append(window)
        conv_out = conv_out + mixer_vectors[shift][None, :] * window
    conv_low = conv_out.astype(bf16).reshape(rows, heads_here, HS)
    gate_pre = jnp.einsum(
        "thi,ghij->tghj", conv_low, gate_blocks, preferred_element_type=f32
    ).reshape(rows, 2, lanes)
    gate_pre = gate_pre + mixer_vectors[CONV + 1 : CONV + 3][None]

    def recurrence_terms(conv_values, gate_values, rate_values):
        input_gate = jax.nn.sigmoid(gate_values[:, 0])
        decay_gate = jax.nn.sigmoid(gate_values[:, 1])
        log_decay = -decay_scale * decay_gate * jax.nn.softplus(rate_values)[None, :]
        inject_scale = jnp.where(reset_rows[:, None], 1.0, jnp.sqrt(1.0 - jnp.exp(2.0 * log_decay)))
        decay_values = jnp.where(reset_rows[:, None], 0.0, jnp.exp(log_decay))
        return (decay_values, inject_scale * input_gate * conv_values)

    (decay, inject), pull_terms = jax.vjp(
        recurrence_terms, conv_out, gate_pre, mixer_vectors[CONV + 3]
    )
    local_a, local_b = linear_scan(decay, inject, False)
    identity = (jnp.ones((lanes,), f32), jnp.zeros((lanes,), f32))
    incoming = prefix((local_a[-1], local_b[-1]), "col", link, identity, False)
    carried = incoming[1]
    state = local_a * carried[None, :] + local_b
    gelu_out, pull_gelu = jax.vjp(gelu_tanh, gelu_in)
    hidden = (gelu_out * state).astype(bf16)
    hidden_all, middle, normed_two_low, scale_two = meet_product(
        hidden[None],
        output_weights,
        False,
        256,
        3,
        stream=block_input,
        gain=norm_gains[1],
    )
    expand_pre = spread_product(normed_two_low, expand_weights, False, 768, 4)

    def geglu(gate_values, up_values):
        return gelu_tanh(gate_values) * up_values

    activated, pull_geglu = jax.vjp(geglu, expand_pre[0], expand_pre[1])
    activated_low = activated.astype(bf16)
    activated_all, contract_grad = meet_gradient(activated_low[None], 640, 5, output_cotangent)
    cot_values = output_cotangent.astype(f32)
    grad_activated = grad_activated.astype(f32)
    grad_gate, grad_up = pull_geglu(grad_activated)
    grad_expand_low = jnp.stack([grad_gate, grad_up]).astype(bf16)
    grad_expand_low, contract_grad = lax.optimization_barrier((grad_expand_low, contract_grad))
    parts = dp_count if feature_count % (16 * dp_count) == 0 else 1
    grad_normed_two, expand_grad = meet_product(
        grad_expand_low, expand_weights, True, 768, 7, normed_two_low.T, "wide", parts
    )
    grad_middle_norm, gain_two_grad = norm_backward(
        middle, scale_two, norm_gains[1], grad_normed_two, width
    )
    grad_middle = cot_values + grad_middle_norm
    grad_branch_low = grad_middle.astype(bf16)
    output_grad = product_tn(hidden_all[0], grad_branch_low)
    grad_hidden = spread_product(grad_branch_low, output_weights, True, 256, 8)[0]
    grad_state = grad_hidden * gelu_out
    (grad_gelu_in,) = pull_gelu(grad_hidden * state)
    shifted_decay = jnp.concatenate([decay[1:], jnp.ones((1, lanes), f32)], axis=0)
    back_a, back_b = linear_scan(shifted_decay, grad_state, True)
    from_later = prefix((decay[0] * back_a[0], decay[0] * back_b[0]), "col", link, identity, True)
    grad_total = back_a * from_later[1][None, :] + back_b
    previous = jnp.concatenate([carried[None, :], state[:-1]], axis=0)
    grad_conv_direct, grad_gate_pre, grad_rate = pull_terms((grad_total * previous, grad_total))
    grad_gate_low = grad_gate_pre.astype(bf16)
    grad_gate_heads = grad_gate_low.reshape(rows, 2, heads_here, HS)
    grad_conv = grad_conv_direct + jnp.einsum(
        "tghj,ghij->thi", grad_gate_heads, gate_blocks, preferred_element_type=f32
    ).reshape(rows, lanes)
    parts = dp_count if feature_count % (16 * dp_count) == 0 else 1
    planes = dp_count == 4 and parts == 4 and 2 * feature_count <= lanes and group_rows <= lanes
    gate_bias_grad = jnp.sum(grad_gate_low.astype(f32), axis=0)
    after = from_behind(grad_conv[:reach], "col", -1)
    grad_conv_ext = jnp.concatenate([grad_conv, after], axis=0)
    grad_mixed = jnp.zeros((rows, lanes), f32)
    tap_grads = []
    for shift in range(CONV):
        masked = grad_conv_ext * masks[shift][:, None]
        grad_mixed = grad_mixed + mixer_vectors[shift][None, :] * masked[shift : shift + rows]
        tap_grads.append(jnp.sum(grad_conv * windows[shift], axis=0))
    grad_mixed, activated_all = lax.optimization_barrier((grad_mixed, activated_all))
    contracted_low = product(activated_all[0], contract_weights).astype(bf16)
    contracted = contracted_low.astype(f32) + lax.ppermute(
        contracted_low, "row", [(0, 1), (1, 0)]
    ).astype(f32)
    block_output = (middle + contracted).astype(bf16)
    vector_rows = tap_grads + [
        jnp.sum(grad_conv, axis=0),
        gate_bias_grad[0],
        gate_bias_grad[1],
        grad_rate,
    ]
    vectors_grad = jnp.stack(vector_rows)
    grad_branch_pre = jnp.stack([grad_mixed, grad_gelu_in]).astype(bf16)
    grad_normed_one, branch_grad = meet_product(
        grad_branch_pre, branch_weights, True, 640, 9, normed_low.T, "wide", parts
    )
    if planes:
        contract_sum = pair_sum(contract_grad.reshape((4, -1) + contract_grad.shape[1:]), 4)
        expand_grad, contract_sum = lax.optimization_barrier((expand_grad, contract_sum))
        expand_sum = pair_sum(expand_grad, 4)
        con_low = (momentum_rate * contract_momentum[0] + contract_sum).astype(bf16)
        weighted = grad_normed_one * norm_gains[0][None, :]
        inner_part = jnp.sum(stream * weighted, axis=1)
        gain_one_grad = jnp.sum(grad_normed_one * stream * scale_one[:, None], axis=0)
        col_part = jnp.concatenate(
            [
                vectors_grad,
                jnp.pad(inner_part, (0, lanes - group_rows))[None],
                jnp.zeros((7, lanes), f32),
            ]
        )
        gains_row = jnp.concatenate([gain_one_grad, gain_two_grad])
        dp_part = jnp.pad(gains_row[None], ((0, 7), (0, lanes - 2 * feature_count)))
        gates_part = gates_product(
            conv_low.reshape(rows, lanes), grad_gate_low[:, 0], grad_gate_low[:, 1]
        )
        piece_rows = branch_grad.shape[2]
        small_grad = jnp.concatenate(
            [
                branch_grad.reshape(4, 2 * piece_rows, lanes),
                output_grad.astype(bf16).reshape(4, piece_rows, lanes),
                gates_part.reshape(4, -1, lanes),
            ],
            axis=1,
        )
        con_low, expand_sum, col_part, dp_part, small_grad, block_output = (
            lax.optimization_barrier(
                (con_low, expand_sum, col_part, dp_part, small_grad, block_output)
            )
        )
        expand_low = (momentum_rate * expand_momentum[:, 0] + expand_sum).astype(bf16)
        small_grad, expand_sum = lax.optimization_barrier((small_grad, expand_sum))
        large, (expand_sum, contract_sum) = pieces_at_owner(
            expand_low[0], expand_low[1], con_low, (expand_sum, contract_sum)
        )
        small_sum = pair_sum(small_grad, 4)
        branch_sum = small_sum[: 2 * piece_rows].reshape(2, piece_rows, lanes)
        output_sum = small_sum[2 * piece_rows : 3 * piece_rows].reshape(output_momentum.shape[1:])
        branch_low = (momentum_rate * branch_momentum[:, 0] + branch_sum).astype(bf16)
        output_low = (momentum_rate * output_momentum[0] + output_sum).astype(bf16)
        expand_orth, con, branch_orth, out, gates_all, col_total, dp_total = finish_blocks(
            large,
            con_low.shape,
            branch_low[0],
            branch_low[1],
            output_low,
            small_sum[3 * piece_rows :],
            col_part,
            dp_part,
        )
        output_sum = output_sum.astype(f32)
        gates_total = gates_all.astype(f32)
        vectors_total = dp_total[:8]
        gains_total = dp_total[8, : 2 * feature_count].reshape(2, feature_count)
        inner = col_total[8, :group_rows]
        grad_stream_norm = (
            scale_one[:, None] * weighted
            - stream * (scale_one * scale_one * scale_one * inner / width)[:, None]
        )
    else:
        grad_stream_norm, gain_one_grad = norm_backward(
            stream, scale_one, norm_gains[0], grad_normed_one, width
        )
        vectors_total, gains_total = lax.psum(
            (lax.psum(vectors_grad, "col"), jnp.stack([gain_one_grad, gain_two_grad])), "dp"
        )
        gates_grad = jnp.einsum(
            "thi,tghj->ghij", conv_low, grad_gate_heads, preferred_element_type=f32
        ).astype(bf16)
        branch_sum = pair_sum(branch_grad, dp_count)
        expand_sum = pair_sum(expand_grad, dp_count)
        output_sum = dp_sum(output_grad)
        contract_sum = dp_sum(contract_grad)
        gates_total = lax.psum(gates_grad, ("dp", "col")).astype(f32)
    input_grad = (grad_middle + grad_stream_norm).astype(bf16)
    branch_sum = branch_sum.astype(f32)
    expand_sum = expand_sum.astype(f32)
    contract_sum = contract_sum.astype(f32)
    branch_moment = momentum_rate * branch_momentum[:, 0] + branch_sum
    expand_moment = momentum_rate * expand_momentum[:, 0] + expand_sum
    output_moment = momentum_rate * output_momentum[0] + output_sum
    contract_moment = momentum_rate * contract_momentum[0] + contract_sum
    if not planes:
        moments = (*branch_moment, output_moment, *expand_moment, contract_moment)
        lows = [moment.astype(bf16) for moment in moments]
        gathered = [lax.all_gather(low, "dp", axis=0, tiled=True) for low in lows]
        orth = owner_results(gathered, dp_place, dp_count)
        pieces = [
            lax.dynamic_slice_in_dim(
                owner_send(orth[number], number % dp_count),
                dp_place * lows[number].shape[0],
                lows[number].shape[0],
                0,
            )
            for number in range(6)
        ]
        branch_orth, expand_orth = jnp.stack(pieces[:2]), jnp.stack(pieces[3:5])
        out, con = pieces[2], pieces[5]

    def stepped(weight, orth, axis):
        count = orth.shape[axis]
        piece = lax.dynamic_slice_in_dim(weight, dp_place * count, count, axis).astype(f32)
        tall = max(1.0, weight.shape[axis] / weight.shape[axis + 1]) ** 0.5
        return piece - muon_rate * tall * orth.astype(f32)

    branch_new = stepped(branch_weights, branch_orth, 1)
    expand_new = stepped(expand_weights, expand_orth, 1)
    output_new = stepped(output_weights, out, 0)
    contract_new = stepped(contract_weights, con, 0)
    gates_moment = momentum_rate * gates_momentum + gates_total
    gate_sq = jnp.mean(gates_moment * gates_moment, axis=(2, 3), keepdims=True)
    gates_new = gate_blocks.astype(f32) - gate_rate * gates_moment * lax.rsqrt(gate_sq + eps_norm)
    vectors_moment, vectors_new = grouped_step(
        vectors_total, vectors_momentum, mixer_vectors, vector_rate
    )
    gains_moment, gains_new = grouped_step(gains_total, gains_momentum, norm_gains, vector_rate)
    return (
        block_output,
        input_grad,
        gains_total,
        branch_sum[:, None],
        vectors_total,
        gates_total,
        output_sum[None],
        expand_sum[:, None],
        contract_sum[None],
        gains_new,
        branch_new[:, None],
        vectors_new,
        gates_new,
        output_new[None],
        expand_new[:, None],
        contract_new[None],
        gains_moment,
        branch_moment[:, None],
        vectors_moment,
        gates_moment,
        output_moment[None],
        expand_moment[:, None],
        contract_moment[None],
    )


def solution(mesh):
    return jax.shard_map(
        shards,
        mesh=mesh,
        in_specs=(
            P("dp", "col"),
            P("dp", None),
            P("dp", "col"),
            P(None, "col"),
            P(None, "col", "row"),
            P(None, "row"),
            P(None, "row", None, None),
            P("row", "col"),
            P(None, "col", "row"),
            P("row", "col"),
            P(None, "col"),
            P(None, "col", "dp", "row"),
            P(None, "row"),
            P(None, "row", None, None),
            P("row", "dp", "col"),
            P(None, "col", "dp", "row"),
            P("row", "dp", "col"),
        ),
        out_specs=(
            P("dp", "col"),
            P("dp", "col"),
            P(None, "col"),
            P(None, "col", "dp", "row"),
            P(None, "row"),
            P(None, "row", None, None),
            P("row", "dp", "col"),
            P(None, "col", "dp", "row"),
            P("row", "dp", "col"),
            P(None, "col"),
            P(None, "col", "dp", "row"),
            P(None, "row"),
            P(None, "row", None, None),
            P("row", "dp", "col"),
            P(None, "col", "dp", "row"),
            P("row", "dp", "col"),
            P(None, "col"),
            P(None, "col", "dp", "row"),
            P(None, "row"),
            P(None, "row", None, None),
            P("row", "dp", "col"),
            P(None, "col", "dp", "row"),
            P("row", "dp", "col"),
        ),
        check_vma=False,
    )
```

```python
import functools

import jax
import jax.numpy as jnp
from jax import lax
from jax.experimental import pallas as pl
from jax.experimental.pallas import tpu as pltpu
from jax.sharding import PartitionSpec as P

CONV = 4
GROUP = 128
HS = 256


eps_norm = 1e-06
eps_frob = 1e-07
poly_first = 3.4445
poly_second = -4.775
poly_third = 2.0315
momentum_rate = 0.9
muon_rate = 0.1
gate_rate = 0.02
vector_rate = 0.3
decay_scale = 8.0


def broadcast(value, axis, source):
    kept = jnp.where(lax.axis_index(axis) == source, value, 0).astype(value.dtype)
    return lax.psum(kept, axis)


def from_behind(value, axis, steps):
    count = lax.axis_size(axis)
    initial, last = (max(0, -steps), min(count, count - steps))
    return lax.ppermute(value, axis, [(source, source + steps) for source in range(initial, last)])


def prefix(value, axis, combine, identity, reverse):
    count, here = (lax.axis_size(axis), lax.axis_index(axis))
    joined = lax.all_gather(jnp.stack(value), axis)
    everything = tuple(joined[:, k] for k in range(len(value)))
    start = jax.tree.map(
        lambda part, zero: jnp.broadcast_to(jnp.asarray(zero, part.dtype), part.shape),
        value,
        identity,
    )

    def lap(k, before):
        at = count - 1 - k if reverse else k
        reached = at > here if reverse else at < here
        new = combine(before, jax.tree.map(lambda part: part[at], everything))
        return jax.tree.map(lambda a, b: jnp.where(reached, a, b), new, before)

    return lax.fori_loop(0, count, lap, start)


def gelu_tanh(value):
    return jax.nn.gelu(value, approximate=True)


def product(left, right):
    return jnp.dot(left, right, preferred_element_type=jnp.float32)


def product_tn(left, right):
    return lax.dot_general(
        left, right, (((0,), (0,)), ((), ())), preferred_element_type=jnp.float32
    )


def product_nt(left, right):
    return lax.dot_general(
        left, right, (((1,), (1,)), ((), ())), preferred_element_type=jnp.float32
    )


def link(first, second):
    return (first[0] * second[0], second[0] * first[1] + second[1])


def scan_kernel(reverse, decay_ref, value_ref, prod_ref, sum_ref):
    rows, lanes = decay_ref.shape
    groups = rows // 8

    def lap(k, carry):
        base = pl.multiple_of((groups - 1 - k if reverse else k) * 8, 8)
        decay = decay_ref[pl.ds(base, 8), :]
        value = value_ref[pl.ds(base, 8), :]
        prod, total = carry
        prods, totals = [None] * 8, [None] * 8
        for j in range(7, -1, -1) if reverse else range(8):
            prod = decay[j : j + 1] * prod
            total = decay[j : j + 1] * total + value[j : j + 1]
            prods[j], totals[j] = prod, total
        prod_ref[pl.ds(base, 8), :] = jnp.concatenate(prods, axis=0)
        sum_ref[pl.ds(base, 8), :] = jnp.concatenate(totals, axis=0)
        return (prod, total)

    start = (jnp.ones((1, lanes), jnp.float32), jnp.zeros((1, lanes), jnp.float32))
    lax.fori_loop(0, groups, lap, start)


def linear_scan(decay, value, reverse):
    shape = jax.ShapeDtypeStruct(decay.shape, jnp.float32)
    return pl.pallas_call(
        functools.partial(scan_kernel, reverse),
        out_shape=(shape, shape),
        compiler_params=pltpu.CompilerParams(vmem_limit_bytes=16 * 1024 * 1024),
    )(decay, value)


MESH = pl.DeviceIdType.MESH
MIB = 1024 * 1024


def col_places():
    me = lax.axis_index("col")
    near_bit = lax.rem(me, 2)
    far_bit = lax.div(me, 2)
    return (me, near_bit, far_bit, me + 1 - 2 * near_bit, lax.rem(me + 2, 4))


def greet(axis_places):
    barrier = pltpu.get_barrier_semaphore()
    for axis, place in axis_places:
        pl.semaphore_signal(barrier, inc=1, device_id={axis: place}, device_id_type=MESH)
    pl.semaphore_wait(barrier, len(axis_places))


def dot_nn(left, right):
    return lax.dot_general(
        left, right, (((1,), (0,)), ((), ())), preferred_element_type=jnp.float32
    )


def dot_nt(left, right):
    return lax.dot_general(
        left, right, (((1,), (1,)), ((), ())), preferred_element_type=jnp.float32
    )


def columns_of(j, width, per):
    return (lax.div(j, per), pl.ds(pl.multiple_of(lax.rem(j, per) * width, width), width))


def share_parts(axis, buf, send_sem, recv_sem):
    me = lax.axis_index(axis)

    def copy(step):
        return pltpu.make_async_remote_copy(
            src_ref=buf.at[me],
            dst_ref=buf.at[me],
            send_sem=send_sem.at[step],
            recv_sem=recv_sem.at[step],
            device_id={axis: lax.rem(me + step, 4)},
            device_id_type=MESH,
        )

    def start(value):
        buf[me] = value
        for step in range(1, 4):
            copy(step).start()

    def arrive():
        for step in range(1, 4):
            copy(step).wait_recv()

    def finish():
        for step in range(1, 4):
            copy(step).wait_send()

    return (start, arrive, finish)


def col_peers():
    me = lax.axis_index("col")
    return [("col", lax.rem(me + step, 4)) for step in range(1, 4)]


def row_scales(values, share, buf):
    tokens, features = values.shape
    start, arrive, finish = share
    squares = jnp.sum(values * values, axis=1, keepdims=True)
    start(jnp.broadcast_to(squares, (tokens, 128)).T[:8])
    arrive()
    total = buf[0] + buf[1] + buf[2] + buf[3]
    scales = lax.rsqrt(total / (4 * features) + eps_norm)
    finish()
    return (scales, jnp.broadcast_to(scales[:1], (128, tokens)).T[:, :1])


def spread_kernel(
    flip, normed, *refs
):
    if normed:
        stream, gain, cot, w, side_w, out, low_out, scale_out, side_out = refs[:9]
        lhs, nbuf, side_buf, stage, nsend, nrecv, side_sem, stage_sem = refs[9:17]
        refs = refs[17:]
    else:
        lhs, w, out = refs[:3]
        refs = refs[3:]
    wbuf, send1, recv1, own, send2, recv2, wsem, s1s, s1r, s2s, s2r = refs
    chunks, rows, width = send2.shape
    per = out.shape[2] // width
    me, near_bit, far_bit, near, far = col_places()
    depth = lhs.shape[3]

    def w_copy(j):
        k, cols = columns_of(j, width, per)
        return pltpu.make_async_copy(
            w.at[cols, :] if flip else w.at[k, :, cols], wbuf.at[j], wsem.at[j]
        )

    def near_copy(j):
        return pltpu.make_async_remote_copy(
            src_ref=send1.at[j],
            dst_ref=recv1.at[j],
            send_sem=s1s.at[j],
            recv_sem=s1r.at[j],
            device_id={"col": near},
            device_id_type=MESH,
        )

    def far_copy(j):
        return pltpu.make_async_remote_copy(
            src_ref=send2.at[j],
            dst_ref=recv2.at[j],
            send_sem=s2s.at[j],
            recv_sem=s2r.at[j],
            device_id={"col": far},
            device_id_type=MESH,
        )

    def loop(count, act):
        def lap(j, carry):
            act(j)
            return carry

        lax.fori_loop(0, count, lap, 0)

    loop(chunks, lambda j: w_copy(j).start())
    if normed:
        span = side_buf.shape[1]
        side_chunks = side_buf.shape[0]

        def side_lines(j):
            return pl.ds(pl.multiple_of(j * span, span), span)

        def side_copy(j):
            return pltpu.make_async_copy(
                side_w.at[side_lines(j), :], side_buf.at[j], side_sem.at[j]
            )

        def stage_copy(j):
            return pltpu.make_async_copy(
                stage.at[j], side_out.at[:, side_lines(j)], stage_sem.at[j]
            )

        def side_part(j):
            side_copy(j).wait()
            stage[j] = dot_nt(cot[...], side_buf[j]).astype(jnp.bfloat16)
            stage_copy(j).start()

        loop(side_chunks, lambda j: side_copy(j).start())
        greet(col_peers())
        values = stream[...].astype(jnp.float32)
        scales, column = row_scales(values, share_parts("col", nbuf, nsend, nrecv), nbuf)
        scale_out[...] = scales
        low = (values * column * gain[...]).astype(jnp.bfloat16)
        low_out[...] = low
        lhs[...] = low.reshape(lhs.shape)
    else:
        greet((("col", near), ("col", far)))
    dot = dot_nt if flip else dot_nn

    def first(j):
        w_copy(j).wait()
        part = wbuf[j]
        theirs = dot(lhs[:, 1 - near_bit].reshape(2 * rows, depth), part)
        send1[j] = theirs.astype(jnp.bfloat16).reshape(2, rows, width)
        near_copy(j).start()
        mine = dot(lhs[:, near_bit].reshape(2 * rows, depth), part)
        own[j] = mine.reshape(2, rows, width)

    def second(j):
        near_copy(j).wait_recv()
        going = own[j, 1 - far_bit] + recv1[j, 1 - far_bit].astype(jnp.float32)
        send2[j] = going.astype(jnp.bfloat16)
        far_copy(j).start()
        own[j, far_bit] = own[j, far_bit] + recv1[j, far_bit].astype(jnp.float32)

    def third(j):
        far_copy(j).wait_recv()
        k, cols = columns_of(j, width, per)
        out[k, :, cols] = own[j, far_bit] + recv2[j].astype(jnp.float32)

    first(0)

    def both(j):
        first(j + 1)
        second(j)

    loop(chunks - 1, both)
    second(chunks - 1)
    if normed:
        loop(side_chunks, side_part)
    loop(chunks, third)
    if normed:
        loop(side_chunks, lambda j: stage_copy(j).wait())

    def drain(j):
        near_copy(j).wait_send()
        far_copy(j).wait_send()

    loop(chunks, drain)


def spread_product(lhs, w, flip, width, collective, gain=None, side=None):
    tokens, depth = lhs.shape
    rows = tokens // 4
    pairs = 1 if flip else w.shape[0]
    total = w.shape[0] if flip else w.shape[2]
    chunks = pairs * total // width
    tile = (width, depth) if flip else (depth, width)
    bf16, f32 = jnp.bfloat16, jnp.float32
    local = pl.BlockSpec(memory_space=pltpu.VMEM)
    shapes = [jax.ShapeDtypeStruct((pairs, rows, total), f32)]
    scratch = []
    anywhere = pl.BlockSpec(memory_space=pl.ANY)
    weights, remote_outs = [w], []
    if gain is None:
        inputs = [lhs.reshape(2, 2, rows, depth)]
    else:
        cot, side_w = side
        span = 768 if side_w.shape[0] % 768 == 0 else 256
        side_chunks = side_w.shape[0] // span
        inputs = [lhs, gain[None], cot]
        weights = [w, side_w]
        remote_outs = [jax.ShapeDtypeStruct((tokens, side_w.shape[0]), bf16)]
        shapes += [
            jax.ShapeDtypeStruct((tokens, depth), bf16),
            jax.ShapeDtypeStruct((8, tokens), f32),
        ]
        scratch = [pltpu.VMEM((2, 2, rows, depth), bf16), pltpu.VMEM((4, 8, tokens), f32)]
        scratch += [pltpu.VMEM((side_chunks, span, depth), bf16)]
        scratch += [pltpu.VMEM((side_chunks, tokens, span), bf16)]
        scratch += [pltpu.SemaphoreType.DMA((4,))] * 2
        scratch += [pltpu.SemaphoreType.DMA((side_chunks,))] * 2
    result = pl.pallas_call(
        functools.partial(spread_kernel, flip, gain is not None),
        out_shape=tuple(shapes + remote_outs),
        in_specs=[local] * len(inputs) + [anywhere] * len(weights),
        out_specs=[local] * len(shapes) + [anywhere] * len(remote_outs),
        scratch_shapes=scratch
        + [
            pltpu.VMEM((chunks,) + tile, bf16),
            pltpu.VMEM((chunks, 2, rows, width), bf16),
            pltpu.VMEM((chunks, 2, rows, width), bf16),
            pltpu.VMEM((chunks, 2, rows, width), f32),
            pltpu.VMEM((chunks, rows, width), bf16),
            pltpu.VMEM((chunks, rows, width), bf16),
        ]
        + [pltpu.SemaphoreType.DMA((chunks,))] * 5,
        compiler_params=pltpu.CompilerParams(
            collective_id=collective, has_side_effects=True, vmem_limit_bytes=56 * MIB
        ),
    )(*inputs, *weights)
    return result[0] if gain is None else result


def meet_kernel(flip, grad_mode, *refs):
    lone = grad_mode == "lone"
    if lone:
        piece, side, all_out, grad_out, buf, osem, ns, nr, fs, fr, rs, rr, stage, gsem = refs
    elif grad_mode:
        piece, w, side, prod, grad_out = refs[:5]
        refs = refs[5:]
    else:
        piece, w, stream, gain, all_out, prod, low_out, scale_out = refs[:8]
        nbuf, nsend, nrecv = refs[-3:]
        refs = refs[8:-3]
    if not lone:
        wbuf, buf, acc, sendx, recvx, wsem, osem, ns, nr, fs, fr, rs, rr, xs, xr = refs[:15]
    if grad_mode and not lone:
        stage, gsem = refs[15:]
    chunks, _, _, rows, width = buf.shape
    per = piece.shape[2] // width
    me, near_bit, far_bit, near, far = col_places()
    across = 1 - lax.axis_index("row")
    f32, bf16 = jnp.float32, jnp.bfloat16

    def w_copy(j):
        k, cols = columns_of(j, width, per)
        return pltpu.make_async_copy(
            w.at[k, :, cols] if flip else w.at[cols, :], wbuf.at[j], wsem.at[j]
        )

    def move(j, source, near_place, far_place, sems, target):
        return pltpu.make_async_remote_copy(
            src_ref=source,
            dst_ref=buf.at[j, far_place, near_place],
            send_sem=sems[0].at[j],
            recv_sem=sems[1].at[j],
            device_id={"col": target},
            device_id_type=MESH,
        )

    def piece_at(j):
        k, cols = columns_of(j, width, per)
        return piece.at[k, :, cols]

    def far_copy(j):
        return move(j, piece_at(j), near_bit, far_bit, (fs, fr), far)

    def near_copy(j):
        return move(j, piece_at(j), near_bit, far_bit, (ns, nr), near)

    def relay(j):
        return move(j, buf.at[j, 1 - far_bit, near_bit], near_bit, 1 - far_bit, (rs, rr), near)

    def out_copy(j):
        k, cols = columns_of(j, width, per)
        return pltpu.make_async_copy(buf.at[j], all_out.at[k, :, :, :, cols], osem.at[j])

    def cross(half):
        return pltpu.make_async_remote_copy(
            src_ref=sendx.at[half],
            dst_ref=recvx.at[half],
            send_sem=xs.at[half],
            recv_sem=xr.at[half],
            device_id={"row": across},
            device_id_type=MESH,
        )

    def loop(count, act):
        def lap(j, carry):
            act(j)
            return carry

        lax.fori_loop(0, count, lap, 0)

    if not lone:
        loop(chunks, lambda j: w_copy(j).start())
    if lone:
        greet((("col", near), ("col", far)))
    elif grad_mode:
        greet((("col", near), ("col", far), ("row", across)))
    else:
        greet(col_peers() + [("row", across)])

    def begin(j):
        far_copy(j).start()
        near_copy(j).start()
        k, cols = columns_of(j, width, per)
        buf[j, far_bit, near_bit] = piece[k, :, cols]

    loop(chunks, begin)
    if not lone:
        acc[...] = jnp.zeros_like(acc)
    dot = dot_nt if flip else dot_nn

    def add(j, half):
        both = buf[j, half].reshape(2 * rows, width)
        acc[half] = acc[half] + dot(both, wbuf[j])

    def here(j):
        near_copy(j).wait_recv()
        if not lone:
            w_copy(j).wait()
            add(j, far_bit)

    loop(chunks, here)
    if not lone:
        sendx[far_bit] = acc[far_bit].astype(bf16)
        cross(far_bit).start()

    def grad_copy(j):
        return grad_moves(j)

    if grad_mode == "wide":
        parts = grad_out.shape[0]

        def grad_moves(j):
            k, cols = columns_of(j, width, per)
            return pltpu.make_async_copy(
                stage.at[lax.rem(j, 2)], grad_out.at[:, k, :, cols], gsem.at[lax.rem(j, 2)]
            )

        def grad_part(j):
            block = buf[j].reshape(4 * rows, width)
            total = dot_nn(side[...], block).astype(bf16)
            stage[lax.rem(j, 2)] = total.reshape(stage.shape[1:])

    if lone:

        def grad_moves(j):
            return pltpu.make_async_copy(
                stage.at[lax.rem(j, 2)],
                grad_out.at[pl.ds(pl.multiple_of(j * width, width), width), :],
                gsem.at[lax.rem(j, 2)],
            )

        def grad_part(j):
            block = buf[j].reshape(4 * rows, width)
            stage[lax.rem(j, 2)] = dot_nn(block.T, side[...]).astype(bf16)

    def pass_on(j):
        far_copy(j).wait_recv()
        relay(j).start()

    def there(j):
        relay(j).wait_recv()
        if lone or not grad_mode:
            out_copy(j).start()
        if not lone:
            add(j, 1 - far_bit)
        if grad_mode:

            @pl.when(j >= 2)
            def _():
                grad_moves(j - 2).wait()

            grad_part(j)
            grad_moves(j).start()

    pass_on(0)

    def both(j):
        pass_on(j + 1)
        there(j)

    loop(chunks - 1, both)
    there(chunks - 1)
    if not lone:
        sendx[1 - far_bit] = acc[1 - far_bit].astype(bf16)
        cross(1 - far_bit).start()

        def settle(half):
            cross(half).wait_recv()
            prod[half] = sendx[half].astype(f32) + recvx[half].astype(f32)

        settle(far_bit)
        settle(1 - far_bit)
    if not grad_mode:
        values = prod[...].reshape(stream.shape) + stream[...].astype(f32)
        prod[...] = values.reshape(prod.shape)
        scales, column = row_scales(values, share_parts("col", nbuf, nsend, nrecv), nbuf)
        scale_out[...] = scales
        low_out[...] = (values * column * gain[...]).astype(bf16)

    def drain(j):
        near_copy(j).wait_send()
        far_copy(j).wait_send()
        relay(j).wait_send()
        if lone or not grad_mode:
            out_copy(j).wait()

    loop(chunks, drain)
    if not lone:
        cross(far_bit).wait_send()
        cross(1 - far_bit).wait_send()
    if grad_mode:
        for j in range(max(0, chunks - 2), chunks):
            grad_moves(j).wait()


def meet_gradient(piece, width, collective, side):
    pairs, rows, total = piece.shape
    chunks = pairs * total // width
    bf16 = jnp.bfloat16
    local = pl.BlockSpec(memory_space=pltpu.VMEM)
    anywhere = pl.BlockSpec(memory_space=pl.ANY)
    everything, gradient = pl.pallas_call(
        functools.partial(meet_kernel, False, "lone"),
        out_shape=(
            jax.ShapeDtypeStruct((pairs, 2, 2, rows, total), bf16),
            jax.ShapeDtypeStruct((total, side.shape[1]), bf16),
        ),
        in_specs=[local, local],
        out_specs=[anywhere, anywhere],
        scratch_shapes=[pltpu.VMEM((chunks, 2, 2, rows, width), bf16)]
        + [pltpu.SemaphoreType.DMA((chunks,))] * 7
        + [pltpu.VMEM((2, width, side.shape[1]), bf16), pltpu.SemaphoreType.DMA((2,))],
        compiler_params=pltpu.CompilerParams(
            collective_id=collective, has_side_effects=True, vmem_limit_bytes=40 * MIB
        ),
    )(piece, side)
    return (everything.reshape(pairs, 4 * rows, total), gradient)


def meet_product(piece, w, flip, width, collective, side=None, grad_mode=None, parts=1, stream=None, gain=None):
    pairs, rows, total = piece.shape
    features = w.shape[1]
    chunks = pairs * total // width
    tile = (features, width) if flip else (width, features)
    bf16, f32 = jnp.bfloat16, jnp.float32
    inputs, in_specs = (
        [piece, w],
        [pl.BlockSpec(memory_space=pltpu.VMEM), pl.BlockSpec(memory_space=pl.ANY)],
    )
    shapes = [jax.ShapeDtypeStruct((2, 2 * rows, features), f32)]
    out_specs = [pl.BlockSpec(memory_space=pltpu.VMEM)]
    scratch = [
        pltpu.VMEM((chunks,) + tile, bf16),
        pltpu.VMEM((chunks, 2, 2, rows, width), bf16),
        pltpu.VMEM((2, 2 * rows, features), f32),
        pltpu.VMEM((2, 2 * rows, features), bf16),
        pltpu.VMEM((2, 2 * rows, features), bf16),
    ]
    scratch += [pltpu.SemaphoreType.DMA((chunks,))] * 8 + [pltpu.SemaphoreType.DMA((2,))] * 2
    if grad_mode:
        inputs.append(side)
        in_specs.append(pl.BlockSpec(memory_space=pltpu.VMEM))
        out_specs.append(pl.BlockSpec(memory_space=pl.ANY))
        if grad_mode == "wide":
            shape = (parts, pairs, side.shape[0] // parts, total)
            stage = (2, parts, side.shape[0] // parts, width)
        else:
            shape = (total, side.shape[1])
            stage = (2, width, side.shape[1])
        shapes.append(jax.ShapeDtypeStruct(shape, bf16))
        scratch += [pltpu.VMEM(stage, bf16), pltpu.SemaphoreType.DMA((2,))]
    else:
        local = pl.BlockSpec(memory_space=pltpu.VMEM)
        inputs += [stream, gain[None]]
        in_specs += [local, local]
        shapes.insert(0, jax.ShapeDtypeStruct((pairs, 2, 2, rows, total), bf16))
        out_specs.insert(0, pl.BlockSpec(memory_space=pl.ANY))
        shapes.append(jax.ShapeDtypeStruct((4 * rows, features), bf16))
        shapes.append(jax.ShapeDtypeStruct((8, 4 * rows), f32))
        out_specs += [local, local]
        scratch += [pltpu.VMEM((4, 8, 4 * rows), f32)] + [pltpu.SemaphoreType.DMA((4,))] * 2
    result = pl.pallas_call(
        functools.partial(meet_kernel, flip, grad_mode),
        out_shape=tuple(shapes),
        in_specs=in_specs,
        out_specs=out_specs,
        scratch_shapes=scratch,
        compiler_params=pltpu.CompilerParams(
            collective_id=collective, has_side_effects=True, vmem_limit_bytes=56 * MIB
        ),
    )(*inputs)
    if grad_mode:
        return (result[0].reshape(4 * rows, features), result[1])
    return (
        result[0].reshape(pairs, 4 * rows, total),
        result[1].reshape(4 * rows, features),
        result[2],
        result[3][0],
    )


def block_steps(x, acc, gram, poly):
    side, total = x.shape
    step = 256
    count = total // step
    span = 1280 if total % 1280 == 0 else step
    f32, bf16 = jnp.float32, jnp.bfloat16

    def tile(k, size):
        return pl.ds(pl.multiple_of(k * size, size), size)

    def square(k, total):
        values = x[:, tile(k, step)].astype(f32)
        return total + jnp.sum(values * values, axis=0, keepdims=True)

    sums = lax.fori_loop(0, count, square, jnp.zeros((1, step), f32))
    norm = jnp.sqrt(jnp.sum(sums, axis=1, keepdims=True)) + eps_frob

    def divide(k, carry):
        x[:, tile(k, step)] = (x[:, tile(k, step)].astype(f32) / norm).astype(bf16)
        return carry

    lax.fori_loop(0, count, divide, 0)

    def lap(k, carry):
        acc[...] = jnp.zeros_like(acc)

        def add(j, inner):
            block = x[:, tile(j, span)]
            acc[:step, :step] = acc[:step, :step] + dot_nt(block[:step], block[:step])
            acc[step:, :] = acc[step:, :] + dot_nt(block[step:], block)
            return inner

        lax.fori_loop(0, total // span, add, 0)
        acc[:step, step:] = acc[step:, :step].T
        low = acc[...].astype(bf16)
        gram[...] = low
        square_gram = dot_nn(low, gram[...])
        poly[...] = (poly_second * low.astype(f32) + poly_third * square_gram).astype(bf16)

        def advance(j, inner):
            block = x[:, tile(j, span)]
            fresh = poly_first * block.astype(f32) + dot_nn(poly[...], block)
            x[:, tile(j, span)] = fresh.astype(bf16)
            return inner

        lax.fori_loop(0, total // span, advance, 0)
        return carry

    lax.fori_loop(0, 5, lap, 0)


def work_space(side):
    return [
        pltpu.VMEM((side, side), jnp.float32),
        pltpu.VMEM((side, side), jnp.bfloat16),
        pltpu.VMEM((side, side), jnp.bfloat16),
    ]


def gates_kernel(conv, first, second, out, full, came, send_sem, recv_sem):
    me = lax.axis_index("col")
    count = out.shape[0]
    greet([("col", lax.rem(me + step, 4)) for step in range(1, 4)])
    for k, grads in enumerate((first, second)):
        for head in range(conv.shape[1] // HS):
            columns = slice(head * HS, (head + 1) * HS)
            block = dot_nn(conv[:, columns].T, grads[:, columns])
            full[k * HS : (k + 1) * HS, columns] = block.astype(jnp.bfloat16)

    def part(place):
        return full.at[pl.ds(pl.multiple_of(place * count, count), count)]

    def copy(step):
        target = lax.rem(me + step, 4)
        return pltpu.make_async_remote_copy(
            src_ref=part(target),
            dst_ref=came.at[step - 1],
            send_sem=send_sem.at[step - 1],
            recv_sem=recv_sem.at[step - 1],
            device_id={"col": target},
            device_id_type=MESH,
        )

    for step in range(1, 4):
        copy(step).start()
    total = part(me)[...].astype(jnp.float32)
    for step in range(1, 4):
        copy(step).wait_recv()
        total = total + came[step - 1].astype(jnp.float32)
    out[...] = total.astype(jnp.bfloat16)
    for step in range(1, 4):
        copy(step).wait_send()


def gates_product(conv, first, second):
    lanes = conv.shape[1]
    count = 2 * HS // 4
    bf16 = jnp.bfloat16
    return pl.pallas_call(
        gates_kernel,
        out_shape=jax.ShapeDtypeStruct((count, lanes), bf16),
        in_specs=[pl.BlockSpec(memory_space=pltpu.VMEM)] * 3,
        out_specs=pl.BlockSpec(memory_space=pltpu.VMEM),
        scratch_shapes=[
            pltpu.VMEM((2 * HS, lanes), bf16),
            pltpu.VMEM((3, count, lanes), bf16),
            pltpu.SemaphoreType.DMA((3,)),
            pltpu.SemaphoreType.DMA((3,)),
        ],
        compiler_params=pltpu.CompilerParams(
            collective_id=12, has_side_effects=True, vmem_limit_bytes=16 * MIB
        ),
    )(conv, first, second)


def token_total(values):
    return lax.psum(values, "col")


def dp_sum(grad):
    low = grad.astype(jnp.bfloat16)
    return lax.psum_scatter(low, "dp", scatter_dimension=0, tiled=True).astype(jnp.float32)


def pair_sum(grad, dp_count):
    if grad.shape[0] == dp_count:
        return lax.psum_scatter(grad, "dp", scatter_dimension=0)
    return lax.psum_scatter(grad[0], "dp", scatter_dimension=1, tiled=True)


def owner_send(block, root):
    return broadcast(block, "dp", root)


def norm_backward(stream, scale, gain, grad_normed, width):
    weighted = grad_normed * gain[None, :]
    inner = token_total(jnp.sum(stream * weighted, axis=1))
    grad_stream = (
        scale[:, None] * weighted - stream * (scale * scale * scale * inner / width)[:, None]
    )
    grad_gain = jnp.sum(grad_normed * stream * scale[:, None], axis=0)
    return (grad_stream, grad_gain)


def orthogonalize(block):
    work = block
    values = work.astype(jnp.float32)
    work = (values / (jnp.sqrt(jnp.sum(values * values)) + eps_frob)).astype(jnp.bfloat16)
    for step in range(5):
        gram = product_nt(work, work).astype(jnp.bfloat16)
        poly = (poly_second * gram.astype(jnp.float32) + poly_third * product(gram, gram)).astype(
            jnp.bfloat16
        )
        work = (poly_first * work.astype(jnp.float32) + product(poly, work)).astype(jnp.bfloat16)
    return work


def owner_results(blocks, dp_place, dp_count):
    results = [None, None, None, None, None, None]
    for members in ((0, 1, 2), (3, 4, 5)):
        flipped = [blocks[number].shape[0] > blocks[number].shape[1] for number in members]
        wide = [
            blocks[number].T if turn else blocks[number] for number, turn in zip(members, flipped)
        ]
        chosen = wide[0]
        for number, candidate in zip(members[1:], wide[1:]):
            chosen = jnp.where(dp_place == number % dp_count, candidate, chosen)
        done = orthogonalize(chosen)
        for number, turn in zip(members, flipped):
            kept = jnp.where(dp_place == number % dp_count, done, jnp.zeros_like(done))
            results[number] = kept.T if turn else kept
    return results


def dp_moves(moves, sems):
    local_sem, send_sem, recv_sem = sems
    me = lax.axis_index("dp")

    def remote(k, sender, target):
        pairs, source, destination = moves[k]
        return pltpu.make_async_remote_copy(
            src_ref=source(sender, target),
            dst_ref=destination(sender, target),
            send_sem=send_sem.at[k, target],
            recv_sem=recv_sem.at[k, sender],
            device_id={"dp": target},
            device_id_type=MESH,
        )

    def local(k, place):
        pairs, source, destination = moves[k]
        return pltpu.make_async_copy(
            source(place, place), destination(place, place), local_sem.at[k]
        )

    def each(chosen, act):
        for k in chosen:
            for sender, target in moves[k][0]:
                act(k, sender, target)

    def start_one(k, sender, target):
        @pl.when(me == sender)
        def _():
            if sender == target:
                local(k, sender).start()
            else:
                remote(k, sender, target).start()

    def arrive_one(k, sender, target):
        @pl.when(me == target)
        def _():
            if sender == target:
                local(k, sender).wait()
            else:
                remote(k, sender, target).wait_recv()

    def sent_one(k, sender, target):
        if sender != target:

            @pl.when(me == sender)
            def _():
                remote(k, sender, target).wait_send()

    return (
        lambda *chosen: each(chosen, start_one),
        lambda *chosen: each(chosen, arrive_one),
        lambda *chosen: each(chosen, sent_one),
    )


def rows_at(ref, place):
    def pick(sender, target):
        index = sender if place == "sender" else target
        count = ref.shape[0] // 4
        return ref.at[pl.ds(index * count, count)]

    return pick


def entry(ref, place):
    return lambda sender, target: ref.at[sender if place == "sender" else target]


def whole(ref):
    return lambda sender, target: ref


def to_owner(owner):
    return [(sender, owner) for sender in ((owner + step) % 4 for step in range(4))]


def from_owner(owner):
    return [(owner, target) for target in ((owner + step) % 4 for step in range(4))]


SMALL_OWNER, CON_OWNER, GATE_OWNER, UP_OWNER = (2, 1, 3, 0)


def beside(block, rows):
    return jnp.concatenate(
        [block[k * rows : (k + 1) * rows] for k in range(block.shape[0] // rows)], axis=1
    )


def below(block, columns):
    return jnp.concatenate(
        [block[:, k * columns : (k + 1) * columns] for k in range(block.shape[1] // columns)]
    )


def pieces_at_owner(e0, e1, packed, later):
    me = lax.axis_index("dp")

    def piece_for(owner):
        return jnp.where(owner == GATE_OWNER, e0, jnp.where(owner == UP_OWNER, e1, packed))

    leaving = [piece_for(lax.rem(me + step, 4)) for step in range(4)]
    leaving, later = lax.optimization_barrier((leaving, later))
    pieces = leaving[:1]
    for step in range(1, 4):
        pairs = [(sender, (sender + step) % 4) for sender in range(4)]
        pairs = [pair for pair in pairs if pair[1] != SMALL_OWNER]
        pieces.append(lax.ppermute(leaving[step], "dp", pairs))
    return (pieces, later)


def tail_kernel(*refs):
    large, (b0, b1, out) = refs[:4], refs[4:7]
    gates_piece, col_part, dp_part = refs[7:10]
    expand_o, con_o, branch_o, out_o, gates_o, col_o, dp_o = refs[10:17]
    x, packed, pieces, first, second, third, out_v, acc, gram, poly, load_sem = refs[17:28]
    col_buf, dp_buf, gates_dp, gates_col = refs[28:32]
    shares = [
        share_parts("col", col_buf, *refs[32:34]),
        share_parts("dp", dp_buf, *refs[34:36]),
        share_parts("dp", gates_dp, *refs[36:38]),
        share_parts("col", gates_col, *refs[38:40]),
    ]
    sems = refs[40:]
    place = lax.axis_index("col")
    me = lax.axis_index("dp")
    small = out.shape[0]
    width = pieces.shape[1]
    side = x.shape[0]
    rows = side // 4
    moves = [
        (to_owner(SMALL_OWNER), whole(b0), rows_at(first, "sender")),
        (to_owner(SMALL_OWNER), whole(b1), rows_at(second, "sender")),
        (to_owner(SMALL_OWNER), whole(out), entry(out_v, "sender")),
        (from_owner(GATE_OWNER), rows_at(x, "target"), whole(expand_o.at[0])),
        (from_owner(UP_OWNER), rows_at(x, "target"), whole(expand_o.at[1])),
        (from_owner(CON_OWNER), entry(pieces, "target"), whole(con_o)),
        (from_owner(SMALL_OWNER), rows_at(first, "target"), whole(branch_o.at[0])),
        (from_owner(SMALL_OWNER), rows_at(second, "target"), whole(branch_o.at[1])),
        (from_owner(SMALL_OWNER), entry(out_v, "target"), whole(out_o)),
    ]
    start, arrive, sent = dp_moves(moves, sems)
    greet(
        [("dp", lax.rem(me + step, 4)) for step in range(1, 4)]
        + [("col", lax.rem(place + step, 4)) for step in range(1, 4)]
    )
    shares[0][0](col_part[...])
    shares[2][0](gates_piece[...])
    start(0, 1, 2)
    shares[0][1]()
    summed = col_buf[0] + col_buf[1] + col_buf[2] + col_buf[3]
    col_o[...] = summed
    shares[1][0](jnp.concatenate([summed[:8], dp_part[...]], axis=0))
    shares[2][1]()
    shares[3][0](gates_dp[...].reshape(gates_col.shape[1:]))

    def load(owner, target):
        copies = [
            pltpu.make_async_copy(large[step], target((owner - step) % 4), load_sem.at[step])
            for step in range(4)
        ]
        for copy in copies:
            copy.start()
        for copy in copies:
            copy.wait()

    @pl.when(me == CON_OWNER)
    def _():
        load(CON_OWNER, lambda j: packed.at[j])
        for j in range(4):
            for k in range(width // rows):
                first_column = j * width + k * rows
                x[:, first_column : first_column + rows] = packed[j, :, k * side : (k + 1) * side].T

    @pl.when(me == GATE_OWNER)
    def _():
        load(GATE_OWNER, lambda j: x.at[pl.ds(j * rows, rows)])

    @pl.when(me == UP_OWNER)
    def _():
        load(UP_OWNER, lambda j: x.at[pl.ds(j * rows, rows)])

    @pl.when(me != SMALL_OWNER)
    def _():
        block_steps(x, acc, gram, poly)

    @pl.when(me == CON_OWNER)
    def _():
        for j in range(4):
            pieces[j] = x[:, j * width : (j + 1) * width].T

    start(3, 4, 5)
    for k, part in enumerate((first, second, third)):
        arrive(k)

        @pl.when(me == SMALL_OWNER)
        def _():
            if k == 2:
                for j in range(4):
                    part[:, j * small : (j + 1) * small] = out_v[j].T
            block_steps(part, acc, gram, poly)
            if k == 2:
                for j in range(4):
                    out_v[j] = part[:, j * small : (j + 1) * small].T

        start(6 + k)
    shares[1][1]()
    dp_o[...] = dp_buf[0] + dp_buf[1] + dp_buf[2] + dp_buf[3]
    shares[3][1]()
    half = gates_col.shape[1]
    for k in range(2):
        for head in range(gates_o.shape[1]):
            columns = slice(head * HS, (head + 1) * HS)
            for j in range(HS // half):
                lines = slice(j * half, (j + 1) * half)
                gates_o[k, head, lines, :] = gates_col[k * (HS // half) + j][:, columns]
    arrive(6, 7, 8, 3, 4, 5)
    sent(0, 1, 2, 3, 4, 5, 6, 7, 8)
    for share in shares:
        share[2]()


def finish_blocks(large, con_shape, b0, b1, out, gates_piece, col_part, dp_part):
    piece = large[0].shape
    rows, total = piece
    side = 4 * rows
    f32, bf16 = jnp.float32, jnp.bfloat16
    shape = jax.ShapeDtypeStruct
    small = pltpu.VMEM((side, b0.shape[1]), bf16)
    quarter = (4 * gates_piece.shape[0], gates_piece.shape[1])
    anywhere = pl.BlockSpec(memory_space=pl.ANY)
    local = pl.BlockSpec(memory_space=pltpu.VMEM)
    sems = pltpu.SemaphoreType.DMA
    shapes = [shape(s, bf16) for s in ((2,) + piece, con_shape, (2,) + b0.shape, out.shape)]
    shapes += [shape((2, quarter[1] // HS, HS, HS), bf16), shape(col_part.shape, f32)]
    shapes += [shape(col_part.shape, f32)]
    return pl.pallas_call(
        tail_kernel,
        out_shape=tuple(shapes),
        in_specs=[anywhere] * 7 + [local] * 3,
        out_specs=[anywhere] * 4 + [local] * 3,
        scratch_shapes=[
            pltpu.VMEM((side, total), bf16),
            pltpu.VMEM((4,) + piece, bf16),
            pltpu.VMEM((4,) + con_shape, bf16),
            small,
            small,
            small,
            pltpu.VMEM((4,) + out.shape, bf16),
        ]
        + work_space(side)
        + [sems((4,))]
        + [
            pltpu.VMEM((4,) + col_part.shape, f32),
            pltpu.VMEM((4,) + col_part.shape, f32),
            pltpu.VMEM((4,) + gates_piece.shape, bf16),
            pltpu.VMEM((4,) + quarter, bf16),
        ]
        + [sems((4,))] * 8
        + [sems((9,)), sems((9, 4)), sems((9, 4))],
        compiler_params=pltpu.CompilerParams(
            collective_id=0, has_side_effects=True, vmem_limit_bytes=40 * MIB
        ),
    )(*large, b0, b1, out, gates_piece, col_part, dp_part)


def grouped_step(grad, moment, weight, rate):
    new_moment = momentum_rate * moment + grad
    rows, cols = new_moment.shape
    grouped = new_moment.reshape(rows, cols // GROUP, GROUP)
    norm_sq = jnp.mean(grouped * grouped, axis=2, keepdims=True)
    update = (grouped * lax.rsqrt(norm_sq + eps_norm)).reshape(rows, cols)
    return (new_moment, weight - rate * update)


def shards(
    block_input,
    segment_ids,
    output_cotangent,
    norm_gains,
    branch_weights,
    mixer_vectors,
    gate_blocks,
    output_weights,
    expand_weights,
    contract_weights,
    gains_momentum,
    branch_momentum,
    vectors_momentum,
    gates_momentum,
    output_momentum,
    expand_momentum,
    contract_momentum,
):
    f32 = jnp.float32
    bf16 = jnp.bfloat16
    col_count = lax.axis_size("col")
    col_place = lax.axis_index("col")
    dp_count = lax.axis_size("dp")
    dp_place = lax.axis_index("dp")
    group_rows = block_input.shape[0]
    rows = group_rows // col_count
    lanes = mixer_vectors.shape[1]
    heads_here = lanes // HS
    feature_count = block_input.shape[1]
    width = feature_count * col_count
    first_row = col_place * rows
    reach = CONV - 1
    seg_row = segment_ids[0]
    seg_ext = jnp.concatenate(
        [jnp.full((reach,), -1, jnp.int32), seg_row, jnp.full((reach,), -2, jnp.int32)]
    )
    seg_here = lax.dynamic_slice_in_dim(seg_ext, first_row + reach, rows + reach)
    masks = []
    for shift in range(CONV):
        earlier = lax.dynamic_slice_in_dim(seg_ext, first_row + reach - shift, rows + reach)
        masks.append((earlier == seg_here).astype(f32))
    reset_rows = masks[1][:rows] < 0.5
    stream = block_input.astype(f32)
    branch_pre, normed_low, scale_rows, contract_term = spread_product(
        block_input,
        branch_weights,
        False,
        640,
        2,
        norm_gains[0],
        (output_cotangent, contract_weights),
    )
    scale_one = scale_rows[0]
    grad_activated = lax.psum_scatter(contract_term, "col", scatter_dimension=0, tiled=True)
    mixed = branch_pre[0]
    gelu_in = branch_pre[1]
    edge = from_behind(mixed[rows - reach :], "col", 1)
    extended = jnp.concatenate([edge, mixed], axis=0)
    windows = []
    conv_out = jnp.zeros((rows, lanes), f32) + mixer_vectors[CONV][None, :]
    for shift in range(CONV):
        window = extended[reach - shift : reach - shift + rows] * masks[shift][:rows, None]
        windows.append(window)
        conv_out = conv_out + mixer_vectors[shift][None, :] * window
    conv_low = conv_out.astype(bf16).reshape(rows, heads_here, HS)
    gate_pre = jnp.einsum(
        "thi,ghij->tghj", conv_low, gate_blocks, preferred_element_type=f32
    ).reshape(rows, 2, lanes)
    gate_pre = gate_pre + mixer_vectors[CONV + 1 : CONV + 3][None]

    def recurrence_terms(conv_values, gate_values, rate_values):
        input_gate = jax.nn.sigmoid(gate_values[:, 0])
        decay_gate = jax.nn.sigmoid(gate_values[:, 1])
        log_decay = -decay_scale * decay_gate * jax.nn.softplus(rate_values)[None, :]
        inject_scale = jnp.where(reset_rows[:, None], 1.0, jnp.sqrt(1.0 - jnp.exp(2.0 * log_decay)))
        decay_values = jnp.where(reset_rows[:, None], 0.0, jnp.exp(log_decay))
        return (decay_values, inject_scale * input_gate * conv_values)

    (decay, inject), pull_terms = jax.vjp(
        recurrence_terms, conv_out, gate_pre, mixer_vectors[CONV + 3]
    )
    local_a, local_b = linear_scan(decay, inject, False)
    identity = (jnp.ones((lanes,), f32), jnp.zeros((lanes,), f32))
    incoming = prefix((local_a[-1], local_b[-1]), "col", link, identity, False)
    carried = incoming[1]
    state = local_a * carried[None, :] + local_b
    gelu_out, pull_gelu = jax.vjp(gelu_tanh, gelu_in)
    hidden = (gelu_out * state).astype(bf16)
    hidden_all, middle, normed_two_low, scale_two = meet_product(
        hidden[None],
        output_weights,
        False,
        256,
        3,
        stream=block_input,
        gain=norm_gains[1],
    )
    expand_pre = spread_product(normed_two_low, expand_weights, False, 768, 4)

    def geglu(gate_values, up_values):
        return gelu_tanh(gate_values) * up_values

    activated, pull_geglu = jax.vjp(geglu, expand_pre[0], expand_pre[1])
    activated_low = activated.astype(bf16)
    activated_all, contract_grad = meet_gradient(activated_low[None], 640, 5, output_cotangent)
    cot_values = output_cotangent.astype(f32)
    grad_activated = grad_activated.astype(f32)
    grad_gate, grad_up = pull_geglu(grad_activated)
    grad_expand_low = jnp.stack([grad_gate, grad_up]).astype(bf16)
    grad_expand_low, contract_grad = lax.optimization_barrier((grad_expand_low, contract_grad))
    parts = dp_count if feature_count % (16 * dp_count) == 0 else 1
    grad_normed_two, expand_grad = meet_product(
        grad_expand_low, expand_weights, True, 768, 7, normed_two_low.T, "wide", parts
    )
    grad_middle_norm, gain_two_grad = norm_backward(
        middle, scale_two, norm_gains[1], grad_normed_two, width
    )
    grad_middle = cot_values + grad_middle_norm
    grad_branch_low = grad_middle.astype(bf16)
    output_grad = product_tn(hidden_all[0], grad_branch_low)
    grad_hidden = spread_product(grad_branch_low, output_weights, True, 256, 8)[0]
    grad_state = grad_hidden * gelu_out
    (grad_gelu_in,) = pull_gelu(grad_hidden * state)
    shifted_decay = jnp.concatenate([decay[1:], jnp.ones((1, lanes), f32)], axis=0)
    back_a, back_b = linear_scan(shifted_decay, grad_state, True)
    from_later = prefix((decay[0] * back_a[0], decay[0] * back_b[0]), "col", link, identity, True)
    grad_total = back_a * from_later[1][None, :] + back_b
    previous = jnp.concatenate([carried[None, :], state[:-1]], axis=0)
    grad_conv_direct, grad_gate_pre, grad_rate = pull_terms((grad_total * previous, grad_total))
    grad_gate_low = grad_gate_pre.astype(bf16)
    grad_gate_heads = grad_gate_low.reshape(rows, 2, heads_here, HS)
    grad_conv = grad_conv_direct + jnp.einsum(
        "tghj,ghij->thi", grad_gate_heads, gate_blocks, preferred_element_type=f32
    ).reshape(rows, lanes)
    parts = dp_count if feature_count % (16 * dp_count) == 0 else 1
    planes = dp_count == 4 and parts == 4 and 2 * feature_count <= lanes and group_rows <= lanes
    gate_bias_grad = jnp.sum(grad_gate_low.astype(f32), axis=0)
    after = from_behind(grad_conv[:reach], "col", -1)
    grad_conv_ext = jnp.concatenate([grad_conv, after], axis=0)
    grad_mixed = jnp.zeros((rows, lanes), f32)
    tap_grads = []
    for shift in range(CONV):
        masked = grad_conv_ext * masks[shift][:, None]
        grad_mixed = grad_mixed + mixer_vectors[shift][None, :] * masked[shift : shift + rows]
        tap_grads.append(jnp.sum(grad_conv * windows[shift], axis=0))
    grad_mixed, activated_all = lax.optimization_barrier((grad_mixed, activated_all))
    contracted_low = product(activated_all[0], contract_weights).astype(bf16)
    contracted = contracted_low.astype(f32) + lax.ppermute(
        contracted_low, "row", [(0, 1), (1, 0)]
    ).astype(f32)
    block_output = (middle + contracted).astype(bf16)
    vector_rows = tap_grads + [
        jnp.sum(grad_conv, axis=0),
        gate_bias_grad[0],
        gate_bias_grad[1],
        grad_rate,
    ]
    vectors_grad = jnp.stack(vector_rows)
    grad_branch_pre = jnp.stack([grad_mixed, grad_gelu_in]).astype(bf16)
    grad_normed_one, branch_grad = meet_product(
        grad_branch_pre, branch_weights, True, 640, 9, normed_low.T, "wide", parts
    )
    if planes:
        contract_sum = pair_sum(contract_grad.reshape((4, -1) + contract_grad.shape[1:]), 4)
        expand_grad, contract_sum = lax.optimization_barrier((expand_grad, contract_sum))
        expand_sum = pair_sum(expand_grad, 4)
        con_low = (momentum_rate * contract_momentum[0] + contract_sum).astype(bf16)
        con_low = beside(con_low, expand_momentum.shape[2])
        weighted = grad_normed_one * norm_gains[0][None, :]
        inner_part = jnp.sum(stream * weighted, axis=1)
        gain_one_grad = jnp.sum(grad_normed_one * stream * scale_one[:, None], axis=0)
        col_part = jnp.concatenate(
            [
                vectors_grad,
                jnp.pad(inner_part, (0, lanes - group_rows))[None],
                jnp.zeros((7, lanes), f32),
            ]
        )
        gains_row = jnp.concatenate([gain_one_grad, gain_two_grad])
        dp_part = jnp.pad(gains_row[None], ((0, 7), (0, lanes - 2 * feature_count)))
        gates_part = gates_product(
            conv_low.reshape(rows, lanes), grad_gate_low[:, 0], grad_gate_low[:, 1]
        )
        piece_rows = branch_grad.shape[2]
        small_grad = jnp.concatenate(
            [
                branch_grad.reshape(4, 2 * piece_rows, lanes),
                jnp.stack([beside(part, piece_rows) for part in jnp.split(output_grad.astype(bf16), 4)]),
                gates_part.reshape(4, -1, lanes),
            ],
            axis=1,
        )
        con_low, expand_sum, col_part, dp_part, small_grad, block_output = (
            lax.optimization_barrier(
                (con_low, expand_sum, col_part, dp_part, small_grad, block_output)
            )
        )
        expand_low = (momentum_rate * expand_momentum[:, 0] + expand_sum).astype(bf16)
        small_grad, expand_sum = lax.optimization_barrier((small_grad, expand_sum))
        large, (expand_sum, contract_sum) = pieces_at_owner(
            expand_low[0], expand_low[1], con_low, (expand_sum, contract_sum)
        )
        small_sum = pair_sum(small_grad, 4)
        branch_sum = small_sum[: 2 * piece_rows].reshape(2, piece_rows, lanes)
        output_sum = below(small_sum[2 * piece_rows : 3 * piece_rows], output_momentum.shape[2])
        branch_low = (momentum_rate * branch_momentum[:, 0] + branch_sum).astype(bf16)
        output_low = (momentum_rate * output_momentum[0] + output_sum).astype(bf16)
        expand_orth, con, branch_orth, out, gates_all, col_total, dp_total = finish_blocks(
            large,
            contract_momentum.shape[1:],
            branch_low[0],
            branch_low[1],
            output_low,
            small_sum[3 * piece_rows :],
            col_part,
            dp_part,
        )
        output_sum = output_sum.astype(f32)
        gates_total = gates_all.astype(f32)
        vectors_total = dp_total[:8]
        gains_total = dp_total[8, : 2 * feature_count].reshape(2, feature_count)
        inner = col_total[8, :group_rows]
        grad_stream_norm = (
            scale_one[:, None] * weighted
            - stream * (scale_one * scale_one * scale_one * inner / width)[:, None]
        )
    else:
        grad_stream_norm, gain_one_grad = norm_backward(
            stream, scale_one, norm_gains[0], grad_normed_one, width
        )
        vectors_total, gains_total = lax.psum(
            (lax.psum(vectors_grad, "col"), jnp.stack([gain_one_grad, gain_two_grad])), "dp"
        )
        gates_grad = jnp.einsum(
            "thi,tghj->ghij", conv_low, grad_gate_heads, preferred_element_type=f32
        ).astype(bf16)
        branch_sum = pair_sum(branch_grad, dp_count)
        expand_sum = pair_sum(expand_grad, dp_count)
        output_sum = dp_sum(output_grad)
        contract_sum = dp_sum(contract_grad)
        gates_total = lax.psum(gates_grad, ("dp", "col")).astype(f32)
    input_grad = (grad_middle + grad_stream_norm).astype(bf16)
    branch_sum = branch_sum.astype(f32)
    expand_sum = expand_sum.astype(f32)
    contract_sum = contract_sum.astype(f32)
    branch_moment = momentum_rate * branch_momentum[:, 0] + branch_sum
    expand_moment = momentum_rate * expand_momentum[:, 0] + expand_sum
    output_moment = momentum_rate * output_momentum[0] + output_sum
    contract_moment = momentum_rate * contract_momentum[0] + contract_sum
    if not planes:
        moments = (*branch_moment, output_moment, *expand_moment, contract_moment)
        lows = [moment.astype(bf16) for moment in moments]
        gathered = [lax.all_gather(low, "dp", axis=0, tiled=True) for low in lows]
        orth = owner_results(gathered, dp_place, dp_count)
        pieces = [
            lax.dynamic_slice_in_dim(
                owner_send(orth[number], number % dp_count),
                dp_place * lows[number].shape[0],
                lows[number].shape[0],
                0,
            )
            for number in range(6)
        ]
        branch_orth, expand_orth = jnp.stack(pieces[:2]), jnp.stack(pieces[3:5])
        out, con = pieces[2], pieces[5]

    def stepped(weight, orth, axis):
        count = orth.shape[axis]
        piece = lax.dynamic_slice_in_dim(weight, dp_place * count, count, axis).astype(f32)
        tall = max(1.0, weight.shape[axis] / weight.shape[axis + 1]) ** 0.5
        return piece - muon_rate * tall * orth.astype(f32)

    branch_new = stepped(branch_weights, branch_orth, 1)
    expand_new = stepped(expand_weights, expand_orth, 1)
    output_new = stepped(output_weights, out, 0)
    contract_new = stepped(contract_weights, con, 0)
    gates_moment = momentum_rate * gates_momentum + gates_total
    gate_sq = jnp.mean(gates_moment * gates_moment, axis=(2, 3), keepdims=True)
    gates_new = gate_blocks.astype(f32) - gate_rate * gates_moment * lax.rsqrt(gate_sq + eps_norm)
    vectors_moment, vectors_new = grouped_step(
        vectors_total, vectors_momentum, mixer_vectors, vector_rate
    )
    gains_moment, gains_new = grouped_step(gains_total, gains_momentum, norm_gains, vector_rate)
    return (
        block_output,
        input_grad,
        gains_total,
        branch_sum[:, None],
        vectors_total,
        gates_total,
        output_sum[None],
        expand_sum[:, None],
        contract_sum[None],
        gains_new,
        branch_new[:, None],
        vectors_new,
        gates_new,
        output_new[None],
        expand_new[:, None],
        contract_new[None],
        gains_moment,
        branch_moment[:, None],
        vectors_moment,
        gates_moment,
        output_moment[None],
        expand_moment[:, None],
        contract_moment[None],
    )


def solution(mesh):
    return jax.shard_map(
        shards,
        mesh=mesh,
        in_specs=(
            P("dp", "col"),
            P("dp", None),
            P("dp", "col"),
            P(None, "col"),
            P(None, "col", "row"),
            P(None, "row"),
            P(None, "row", None, None),
            P("row", "col"),
            P(None, "col", "row"),
            P("row", "col"),
            P(None, "col"),
            P(None, "col", "dp", "row"),
            P(None, "row"),
            P(None, "row", None, None),
            P("row", "dp", "col"),
            P(None, "col", "dp", "row"),
            P("row", "dp", "col"),
        ),
        out_specs=(
            P("dp", "col"),
            P("dp", "col"),
            P(None, "col"),
            P(None, "col", "dp", "row"),
            P(None, "row"),
            P(None, "row", None, None),
            P("row", "dp", "col"),
            P(None, "col", "dp", "row"),
            P("row", "dp", "col"),
            P(None, "col"),
            P(None, "col", "dp", "row"),
            P(None, "row"),
            P(None, "row", None, None),
            P("row", "dp", "col"),
            P(None, "col", "dp", "row"),
            P("row", "dp", "col"),
            P(None, "col"),
            P(None, "col", "dp", "row"),
            P(None, "row"),
            P(None, "row", None, None),
            P("row", "dp", "col"),
            P(None, "col", "dp", "row"),
            P("row", "dp", "col"),
        ),
        check_vma=False,
    )
```

```python
import functools

import jax
import jax.numpy as jnp
from jax import lax
from jax.experimental import pallas as pl
from jax.experimental.pallas import tpu as pltpu
from jax.sharding import PartitionSpec as P

CONV = 4
GROUP = 128
HS = 256


eps_norm = 1e-06
eps_frob = 1e-07
poly_first = 3.4445
poly_second = -4.775
poly_third = 2.0315
momentum_rate = 0.9
muon_rate = 0.1
gate_rate = 0.02
vector_rate = 0.3
decay_scale = 8.0


def broadcast(value, axis, source):
    kept = jnp.where(lax.axis_index(axis) == source, value, 0).astype(value.dtype)
    return lax.psum(kept, axis)


def from_behind(value, axis, steps):
    count = lax.axis_size(axis)
    initial, last = (max(0, -steps), min(count, count - steps))
    return lax.ppermute(value, axis, [(source, source + steps) for source in range(initial, last)])


def prefix(value, axis, combine, identity, reverse):
    count, here = (lax.axis_size(axis), lax.axis_index(axis))
    joined = lax.all_gather(jnp.stack(value), axis)
    everything = tuple(joined[:, k] for k in range(len(value)))
    start = jax.tree.map(
        lambda part, zero: jnp.broadcast_to(jnp.asarray(zero, part.dtype), part.shape),
        value,
        identity,
    )

    def lap(k, before):
        at = count - 1 - k if reverse else k
        reached = at > here if reverse else at < here
        new = combine(before, jax.tree.map(lambda part: part[at], everything))
        return jax.tree.map(lambda a, b: jnp.where(reached, a, b), new, before)

    return lax.fori_loop(0, count, lap, start)


def gelu_tanh(value):
    return jax.nn.gelu(value, approximate=True)


def product(left, right):
    return jnp.dot(left, right, preferred_element_type=jnp.float32)


def product_tn(left, right):
    return lax.dot_general(
        left, right, (((0,), (0,)), ((), ())), preferred_element_type=jnp.float32
    )


def product_nt(left, right):
    return lax.dot_general(
        left, right, (((1,), (1,)), ((), ())), preferred_element_type=jnp.float32
    )


def link(first, second):
    return (first[0] * second[0], second[0] * first[1] + second[1])


def scan_kernel(reverse, decay_ref, value_ref, prod_ref, sum_ref):
    rows, lanes = decay_ref.shape
    groups = rows // 8

    def lap(k, carry):
        base = pl.multiple_of((groups - 1 - k if reverse else k) * 8, 8)
        decay = decay_ref[pl.ds(base, 8), :]
        value = value_ref[pl.ds(base, 8), :]
        prod, total = carry
        prods, totals = [None] * 8, [None] * 8
        for j in range(7, -1, -1) if reverse else range(8):
            prod = decay[j : j + 1] * prod
            total = decay[j : j + 1] * total + value[j : j + 1]
            prods[j], totals[j] = prod, total
        prod_ref[pl.ds(base, 8), :] = jnp.concatenate(prods, axis=0)
        sum_ref[pl.ds(base, 8), :] = jnp.concatenate(totals, axis=0)
        return (prod, total)

    start = (jnp.ones((1, lanes), jnp.float32), jnp.zeros((1, lanes), jnp.float32))
    lax.fori_loop(0, groups, lap, start)


def linear_scan(decay, value, reverse):
    shape = jax.ShapeDtypeStruct(decay.shape, jnp.float32)
    return pl.pallas_call(
        functools.partial(scan_kernel, reverse),
        out_shape=(shape, shape),
        compiler_params=pltpu.CompilerParams(vmem_limit_bytes=16 * 1024 * 1024),
    )(decay, value)


MESH = pl.DeviceIdType.MESH
MIB = 1024 * 1024


def col_places():
    me = lax.axis_index("col")
    near_bit = lax.rem(me, 2)
    far_bit = lax.div(me, 2)
    return (me, near_bit, far_bit, me + 1 - 2 * near_bit, lax.rem(me + 2, 4))


def greet(axis_places):
    barrier = pltpu.get_barrier_semaphore()
    for axis, place in axis_places:
        pl.semaphore_signal(barrier, inc=1, device_id={axis: place}, device_id_type=MESH)
    pl.semaphore_wait(barrier, len(axis_places))


def dot_nn(left, right):
    return lax.dot_general(
        left, right, (((1,), (0,)), ((), ())), preferred_element_type=jnp.float32
    )


def dot_nt(left, right):
    return lax.dot_general(
        left, right, (((1,), (1,)), ((), ())), preferred_element_type=jnp.float32
    )


def columns_of(j, width, per):
    return (lax.div(j, per), pl.ds(pl.multiple_of(lax.rem(j, per) * width, width), width))


def share_parts(axis, buf, send_sem, recv_sem):
    me = lax.axis_index(axis)

    def copy(step):
        return pltpu.make_async_remote_copy(
            src_ref=buf.at[me],
            dst_ref=buf.at[me],
            send_sem=send_sem.at[step],
            recv_sem=recv_sem.at[step],
            device_id={axis: lax.rem(me + step, 4)},
            device_id_type=MESH,
        )

    def start(value):
        buf[me] = value
        for step in range(1, 4):
            copy(step).start()

    def arrive():
        for step in range(1, 4):
            copy(step).wait_recv()

    def finish():
        for step in range(1, 4):
            copy(step).wait_send()

    return (start, arrive, finish)


def col_peers():
    me = lax.axis_index("col")
    return [("col", lax.rem(me + step, 4)) for step in range(1, 4)]


def row_scales(values, share, buf):
    tokens, features = values.shape
    start, arrive, finish = share
    squares = jnp.sum(values * values, axis=1, keepdims=True)
    start(jnp.broadcast_to(squares, (tokens, 128)).T[:8])
    arrive()
    total = buf[0] + buf[1] + buf[2] + buf[3]
    scales = lax.rsqrt(total / (4 * features) + eps_norm)
    finish()
    return (scales, jnp.broadcast_to(scales[:1], (128, tokens)).T[:, :1])


def spread_kernel(
    flip, normed, *refs
):
    if normed:
        stream, gain, cot, w, side_w, out, low_out, scale_out, side_out = refs[:9]
        lhs, nbuf, side_buf, stage, nsend, nrecv, side_sem, stage_sem = refs[9:17]
        refs = refs[17:]
    else:
        lhs, w, out = refs[:3]
        refs = refs[3:]
    wbuf, send1, recv1, own, send2, recv2, wsem, s1s, s1r, s2s, s2r = refs
    chunks, rows, width = send2.shape
    per = out.shape[2] // width
    me, near_bit, far_bit, near, far = col_places()
    depth = lhs.shape[3]

    def w_copy(j):
        k, cols = columns_of(j, width, per)
        return pltpu.make_async_copy(
            w.at[cols, :] if flip else w.at[k, :, cols], wbuf.at[j], wsem.at[j]
        )

    def near_copy(j):
        return pltpu.make_async_remote_copy(
            src_ref=send1.at[j],
            dst_ref=recv1.at[j],
            send_sem=s1s.at[j],
            recv_sem=s1r.at[j],
            device_id={"col": near},
            device_id_type=MESH,
        )

    def far_copy(j):
        return pltpu.make_async_remote_copy(
            src_ref=send2.at[j],
            dst_ref=recv2.at[j],
            send_sem=s2s.at[j],
            recv_sem=s2r.at[j],
            device_id={"col": far},
            device_id_type=MESH,
        )

    def loop(count, act):
        def lap(j, carry):
            act(j)
            return carry

        lax.fori_loop(0, count, lap, 0)

    loop(chunks, lambda j: w_copy(j).start())
    if normed:
        span = side_buf.shape[1]
        side_chunks = side_buf.shape[0]

        def side_lines(j):
            return pl.ds(pl.multiple_of(j * span, span), span)

        def side_copy(j):
            return pltpu.make_async_copy(
                side_w.at[side_lines(j), :], side_buf.at[j], side_sem.at[j]
            )

        def stage_copy(j):
            return pltpu.make_async_copy(
                stage.at[j], side_out.at[:, side_lines(j)], stage_sem.at[j]
            )

        def side_part(j):
            side_copy(j).wait()
            stage[j] = dot_nt(cot[...], side_buf[j]).astype(jnp.bfloat16)
            stage_copy(j).start()

        loop(side_chunks, lambda j: side_copy(j).start())
        greet(col_peers())
        values = stream[...].astype(jnp.float32)
        scales, column = row_scales(values, share_parts("col", nbuf, nsend, nrecv), nbuf)
        scale_out[...] = scales
        low = (values * column * gain[...]).astype(jnp.bfloat16)
        low_out[...] = low
        lhs[...] = low.reshape(lhs.shape)
    else:
        greet((("col", near), ("col", far)))
    dot = dot_nt if flip else dot_nn

    def first(j):
        w_copy(j).wait()
        part = wbuf[j]
        theirs = dot(lhs[:, 1 - near_bit].reshape(2 * rows, depth), part)
        send1[j] = theirs.astype(jnp.bfloat16).reshape(2, rows, width)
        near_copy(j).start()
        mine = dot(lhs[:, near_bit].reshape(2 * rows, depth), part)
        own[j] = mine.reshape(2, rows, width)

    def second(j):
        near_copy(j).wait_recv()
        going = own[j, 1 - far_bit] + recv1[j, 1 - far_bit].astype(jnp.float32)
        send2[j] = going.astype(jnp.bfloat16)
        far_copy(j).start()
        own[j, far_bit] = own[j, far_bit] + recv1[j, far_bit].astype(jnp.float32)

    def third(j):
        far_copy(j).wait_recv()
        k, cols = columns_of(j, width, per)
        out[k, :, cols] = own[j, far_bit] + recv2[j].astype(jnp.float32)

    first(0)

    def both(j):
        first(j + 1)
        second(j)

    loop(chunks - 1, both)
    second(chunks - 1)
    if normed:
        loop(side_chunks, side_part)
    loop(chunks, third)
    if normed:
        loop(side_chunks, lambda j: stage_copy(j).wait())

    def drain(j):
        near_copy(j).wait_send()
        far_copy(j).wait_send()

    loop(chunks, drain)


def spread_product(lhs, w, flip, width, collective, gain=None, side=None):
    tokens, depth = lhs.shape
    rows = tokens // 4
    pairs = 1 if flip else w.shape[0]
    total = w.shape[0] if flip else w.shape[2]
    chunks = pairs * total // width
    tile = (width, depth) if flip else (depth, width)
    bf16, f32 = jnp.bfloat16, jnp.float32
    local = pl.BlockSpec(memory_space=pltpu.VMEM)
    shapes = [jax.ShapeDtypeStruct((pairs, rows, total), f32)]
    scratch = []
    anywhere = pl.BlockSpec(memory_space=pl.ANY)
    weights, remote_outs = [w], []
    if gain is None:
        inputs = [lhs.reshape(2, 2, rows, depth)]
    else:
        cot, side_w = side
        span = 768 if side_w.shape[0] % 768 == 0 else 256
        side_chunks = side_w.shape[0] // span
        inputs = [lhs, gain[None], cot]
        weights = [w, side_w]
        remote_outs = [jax.ShapeDtypeStruct((tokens, side_w.shape[0]), bf16)]
        shapes += [
            jax.ShapeDtypeStruct((tokens, depth), bf16),
            jax.ShapeDtypeStruct((8, tokens), f32),
        ]
        scratch = [pltpu.VMEM((2, 2, rows, depth), bf16), pltpu.VMEM((4, 8, tokens), f32)]
        scratch += [pltpu.VMEM((side_chunks, span, depth), bf16)]
        scratch += [pltpu.VMEM((side_chunks, tokens, span), bf16)]
        scratch += [pltpu.SemaphoreType.DMA((4,))] * 2
        scratch += [pltpu.SemaphoreType.DMA((side_chunks,))] * 2
    result = pl.pallas_call(
        functools.partial(spread_kernel, flip, gain is not None),
        out_shape=tuple(shapes + remote_outs),
        in_specs=[local] * len(inputs) + [anywhere] * len(weights),
        out_specs=[local] * len(shapes) + [anywhere] * len(remote_outs),
        scratch_shapes=scratch
        + [
            pltpu.VMEM((chunks,) + tile, bf16),
            pltpu.VMEM((chunks, 2, rows, width), bf16),
            pltpu.VMEM((chunks, 2, rows, width), bf16),
            pltpu.VMEM((chunks, 2, rows, width), f32),
            pltpu.VMEM((chunks, rows, width), bf16),
            pltpu.VMEM((chunks, rows, width), bf16),
        ]
        + [pltpu.SemaphoreType.DMA((chunks,))] * 5,
        compiler_params=pltpu.CompilerParams(
            collective_id=collective, has_side_effects=True, vmem_limit_bytes=56 * MIB
        ),
    )(*inputs, *weights)
    return result[0] if gain is None else result


def meet_kernel(flip, grad_mode, *refs):
    lone = grad_mode == "lone"
    if lone:
        piece, side, all_out, grad_out, buf, osem, ns, nr, fs, fr, rs, rr, stage, gsem = refs
    elif grad_mode:
        piece, w, side, prod, grad_out = refs[:5]
        refs = refs[5:]
    else:
        piece, w, stream, gain, all_out, prod, low_out, scale_out = refs[:8]
        nbuf, nsend, nrecv = refs[-3:]
        refs = refs[8:-3]
    if not lone:
        wbuf, buf, acc, sendx, recvx, wsem, osem, ns, nr, fs, fr, rs, rr, xs, xr = refs[:15]
    if grad_mode and not lone:
        stage, gsem = refs[15:]
    chunks, _, _, rows, width = buf.shape
    per = piece.shape[2] // width
    me, near_bit, far_bit, near, far = col_places()
    across = 1 - lax.axis_index("row")
    f32, bf16 = jnp.float32, jnp.bfloat16

    def w_copy(j):
        k, cols = columns_of(j, width, per)
        return pltpu.make_async_copy(
            w.at[k, :, cols] if flip else w.at[cols, :], wbuf.at[j], wsem.at[j]
        )

    def move(j, source, near_place, far_place, sems, target):
        return pltpu.make_async_remote_copy(
            src_ref=source,
            dst_ref=buf.at[j, far_place, near_place],
            send_sem=sems[0].at[j],
            recv_sem=sems[1].at[j],
            device_id={"col": target},
            device_id_type=MESH,
        )

    def piece_at(j):
        k, cols = columns_of(j, width, per)
        return piece.at[k, :, cols]

    def far_copy(j):
        return move(j, piece_at(j), near_bit, far_bit, (fs, fr), far)

    def near_copy(j):
        return move(j, piece_at(j), near_bit, far_bit, (ns, nr), near)

    def relay(j):
        return move(j, buf.at[j, 1 - far_bit, near_bit], near_bit, 1 - far_bit, (rs, rr), near)

    def out_copy(j):
        k, cols = columns_of(j, width, per)
        return pltpu.make_async_copy(buf.at[j], all_out.at[k, :, :, :, cols], osem.at[j])

    def cross(half):
        return pltpu.make_async_remote_copy(
            src_ref=sendx.at[half],
            dst_ref=recvx.at[half],
            send_sem=xs.at[half],
            recv_sem=xr.at[half],
            device_id={"row": across},
            device_id_type=MESH,
        )

    def loop(count, act):
        def lap(j, carry):
            act(j)
            return carry

        lax.fori_loop(0, count, lap, 0)

    if not lone:
        loop(chunks, lambda j: w_copy(j).start())
    if lone:
        greet((("col", near), ("col", far)))
    elif grad_mode:
        greet((("col", near), ("col", far), ("row", across)))
    else:
        greet(col_peers() + [("row", across)])

    def begin(j):
        far_copy(j).start()
        near_copy(j).start()
        k, cols = columns_of(j, width, per)
        buf[j, far_bit, near_bit] = piece[k, :, cols]

    loop(chunks, begin)
    if not lone:
        acc[...] = jnp.zeros_like(acc)
    dot = dot_nt if flip else dot_nn

    def add(j, half):
        both = buf[j, half].reshape(2 * rows, width)
        acc[half] = acc[half] + dot(both, wbuf[j])

    def here(j):
        near_copy(j).wait_recv()
        if not lone:
            w_copy(j).wait()
            add(j, far_bit)

    loop(chunks, here)
    if not lone:
        sendx[far_bit] = acc[far_bit].astype(bf16)
        cross(far_bit).start()

    def grad_copy(j):
        return grad_moves(j)

    if grad_mode == "wide":
        parts = grad_out.shape[0]

        def grad_moves(j):
            k, cols = columns_of(j, width, per)
            return pltpu.make_async_copy(
                stage.at[lax.rem(j, 2)], grad_out.at[:, k, :, cols], gsem.at[lax.rem(j, 2)]
            )

        def grad_part(j):
            block = buf[j].reshape(4 * rows, width)
            total = dot_nn(side[...], block).astype(bf16)
            stage[lax.rem(j, 2)] = total.reshape(stage.shape[1:])

    if lone:

        def grad_moves(j):
            return pltpu.make_async_copy(
                stage.at[lax.rem(j, 2)],
                grad_out.at[pl.ds(pl.multiple_of(j * width, width), width), :],
                gsem.at[lax.rem(j, 2)],
            )

        def grad_part(j):
            block = buf[j].reshape(4 * rows, width)
            stage[lax.rem(j, 2)] = dot_nn(block.T, side[...]).astype(bf16)

    def pass_on(j):
        far_copy(j).wait_recv()
        relay(j).start()

    def there(j):
        relay(j).wait_recv()
        if lone or not grad_mode:
            out_copy(j).start()
        if not lone:
            add(j, 1 - far_bit)
        if grad_mode:

            @pl.when(j >= 2)
            def _():
                grad_moves(j - 2).wait()

            grad_part(j)
            grad_moves(j).start()

    pass_on(0)

    def both(j):
        pass_on(j + 1)
        there(j)

    loop(chunks - 1, both)
    there(chunks - 1)
    if not lone:
        sendx[1 - far_bit] = acc[1 - far_bit].astype(bf16)
        cross(1 - far_bit).start()

        def settle(half):
            cross(half).wait_recv()
            prod[half] = sendx[half].astype(f32) + recvx[half].astype(f32)

        settle(far_bit)
        settle(1 - far_bit)
    if not grad_mode:
        values = prod[...].reshape(stream.shape) + stream[...].astype(f32)
        prod[...] = values.reshape(prod.shape)
        scales, column = row_scales(values, share_parts("col", nbuf, nsend, nrecv), nbuf)
        scale_out[...] = scales
        low_out[...] = (values * column * gain[...]).astype(bf16)

    def drain(j):
        near_copy(j).wait_send()
        far_copy(j).wait_send()
        relay(j).wait_send()
        if lone or not grad_mode:
            out_copy(j).wait()

    loop(chunks, drain)
    if not lone:
        cross(far_bit).wait_send()
        cross(1 - far_bit).wait_send()
    if grad_mode:
        for j in range(max(0, chunks - 2), chunks):
            grad_moves(j).wait()


def meet_gradient(piece, width, collective, side):
    pairs, rows, total = piece.shape
    chunks = pairs * total // width
    bf16 = jnp.bfloat16
    local = pl.BlockSpec(memory_space=pltpu.VMEM)
    anywhere = pl.BlockSpec(memory_space=pl.ANY)
    everything, gradient = pl.pallas_call(
        functools.partial(meet_kernel, False, "lone"),
        out_shape=(
            jax.ShapeDtypeStruct((pairs, 2, 2, rows, total), bf16),
            jax.ShapeDtypeStruct((total, side.shape[1]), bf16),
        ),
        in_specs=[local, local],
        out_specs=[anywhere, anywhere],
        scratch_shapes=[pltpu.VMEM((chunks, 2, 2, rows, width), bf16)]
        + [pltpu.SemaphoreType.DMA((chunks,))] * 7
        + [pltpu.VMEM((2, width, side.shape[1]), bf16), pltpu.SemaphoreType.DMA((2,))],
        compiler_params=pltpu.CompilerParams(
            collective_id=collective, has_side_effects=True, vmem_limit_bytes=40 * MIB
        ),
    )(piece, side)
    return (everything.reshape(pairs, 4 * rows, total), gradient)


def meet_product(piece, w, flip, width, collective, side=None, grad_mode=None, parts=1, stream=None, gain=None):
    pairs, rows, total = piece.shape
    features = w.shape[1]
    chunks = pairs * total // width
    tile = (features, width) if flip else (width, features)
    bf16, f32 = jnp.bfloat16, jnp.float32
    inputs, in_specs = (
        [piece, w],
        [pl.BlockSpec(memory_space=pltpu.VMEM), pl.BlockSpec(memory_space=pl.ANY)],
    )
    shapes = [jax.ShapeDtypeStruct((2, 2 * rows, features), f32)]
    out_specs = [pl.BlockSpec(memory_space=pltpu.VMEM)]
    scratch = [
        pltpu.VMEM((chunks,) + tile, bf16),
        pltpu.VMEM((chunks, 2, 2, rows, width), bf16),
        pltpu.VMEM((2, 2 * rows, features), f32),
        pltpu.VMEM((2, 2 * rows, features), bf16),
        pltpu.VMEM((2, 2 * rows, features), bf16),
    ]
    scratch += [pltpu.SemaphoreType.DMA((chunks,))] * 8 + [pltpu.SemaphoreType.DMA((2,))] * 2
    if grad_mode:
        inputs.append(side)
        in_specs.append(pl.BlockSpec(memory_space=pltpu.VMEM))
        out_specs.append(pl.BlockSpec(memory_space=pl.ANY))
        if grad_mode == "wide":
            shape = (parts, pairs, side.shape[0] // parts, total)
            stage = (2, parts, side.shape[0] // parts, width)
        else:
            shape = (total, side.shape[1])
            stage = (2, width, side.shape[1])
        shapes.append(jax.ShapeDtypeStruct(shape, bf16))
        scratch += [pltpu.VMEM(stage, bf16), pltpu.SemaphoreType.DMA((2,))]
    else:
        local = pl.BlockSpec(memory_space=pltpu.VMEM)
        inputs += [stream, gain[None]]
        in_specs += [local, local]
        shapes.insert(0, jax.ShapeDtypeStruct((pairs, 2, 2, rows, total), bf16))
        out_specs.insert(0, pl.BlockSpec(memory_space=pl.ANY))
        shapes.append(jax.ShapeDtypeStruct((4 * rows, features), bf16))
        shapes.append(jax.ShapeDtypeStruct((8, 4 * rows), f32))
        out_specs += [local, local]
        scratch += [pltpu.VMEM((4, 8, 4 * rows), f32)] + [pltpu.SemaphoreType.DMA((4,))] * 2
    result = pl.pallas_call(
        functools.partial(meet_kernel, flip, grad_mode),
        out_shape=tuple(shapes),
        in_specs=in_specs,
        out_specs=out_specs,
        scratch_shapes=scratch,
        compiler_params=pltpu.CompilerParams(
            collective_id=collective, has_side_effects=True, vmem_limit_bytes=56 * MIB
        ),
    )(*inputs)
    if grad_mode:
        return (result[0].reshape(4 * rows, features), result[1])
    return (
        result[0].reshape(pairs, 4 * rows, total),
        result[1].reshape(4 * rows, features),
        result[2],
        result[3][0],
    )


def block_steps(x, acc, gram, poly):
    side, total = x.shape
    step = 256
    count = total // step
    span = 1280 if total % 1280 == 0 else step
    f32, bf16 = jnp.float32, jnp.bfloat16

    def tile(k, size):
        return pl.ds(pl.multiple_of(k * size, size), size)

    def square(k, total):
        values = x[:, tile(k, step)].astype(f32)
        return total + jnp.sum(values * values, axis=0, keepdims=True)

    sums = lax.fori_loop(0, count, square, jnp.zeros((1, step), f32))
    norm = jnp.sqrt(jnp.sum(sums, axis=1, keepdims=True)) + eps_frob

    def divide(k, carry):
        x[:, tile(k, step)] = (x[:, tile(k, step)].astype(f32) / norm).astype(bf16)
        return carry

    lax.fori_loop(0, count, divide, 0)

    def lap(k, carry):
        acc[...] = jnp.zeros_like(acc)

        def add(j, inner):
            block = x[:, tile(j, span)]
            acc[:step, :step] = acc[:step, :step] + dot_nt(block[:step], block[:step])
            acc[step:, :] = acc[step:, :] + dot_nt(block[step:], block)
            return inner

        lax.fori_loop(0, total // span, add, 0)
        acc[:step, step:] = acc[step:, :step].T
        low = acc[...].astype(bf16)
        gram[...] = low
        square_gram = dot_nn(low, gram[...])
        poly[...] = (poly_second * low.astype(f32) + poly_third * square_gram).astype(bf16)

        def advance(j, inner):
            block = x[:, tile(j, span)]
            fresh = poly_first * block.astype(f32) + dot_nn(poly[...], block)
            x[:, tile(j, span)] = fresh.astype(bf16)
            return inner

        lax.fori_loop(0, total // span, advance, 0)
        return carry

    lax.fori_loop(0, 5, lap, 0)


def work_space(side):
    return [
        pltpu.VMEM((side, side), jnp.float32),
        pltpu.VMEM((side, side), jnp.bfloat16),
        pltpu.VMEM((side, side), jnp.bfloat16),
    ]


def gates_kernel(conv, first, second, out, full, came, send_sem, recv_sem):
    me = lax.axis_index("col")
    count = out.shape[0]
    greet([("col", lax.rem(me + step, 4)) for step in range(1, 4)])
    for k, grads in enumerate((first, second)):
        for head in range(conv.shape[1] // HS):
            columns = slice(head * HS, (head + 1) * HS)
            block = dot_nn(conv[:, columns].T, grads[:, columns])
            full[k * HS : (k + 1) * HS, columns] = block.astype(jnp.bfloat16)

    def part(place):
        return full.at[pl.ds(pl.multiple_of(place * count, count), count)]

    def copy(step):
        target = lax.rem(me + step, 4)
        return pltpu.make_async_remote_copy(
            src_ref=part(target),
            dst_ref=came.at[step - 1],
            send_sem=send_sem.at[step - 1],
            recv_sem=recv_sem.at[step - 1],
            device_id={"col": target},
            device_id_type=MESH,
        )

    for step in range(1, 4):
        copy(step).start()
    total = part(me)[...].astype(jnp.float32)
    for step in range(1, 4):
        copy(step).wait_recv()
        total = total + came[step - 1].astype(jnp.float32)
    out[...] = total.astype(jnp.bfloat16)
    for step in range(1, 4):
        copy(step).wait_send()


def gates_product(conv, first, second):
    lanes = conv.shape[1]
    count = 2 * HS // 4
    bf16 = jnp.bfloat16
    return pl.pallas_call(
        gates_kernel,
        out_shape=jax.ShapeDtypeStruct((count, lanes), bf16),
        in_specs=[pl.BlockSpec(memory_space=pltpu.VMEM)] * 3,
        out_specs=pl.BlockSpec(memory_space=pltpu.VMEM),
        scratch_shapes=[
            pltpu.VMEM((2 * HS, lanes), bf16),
            pltpu.VMEM((3, count, lanes), bf16),
            pltpu.SemaphoreType.DMA((3,)),
            pltpu.SemaphoreType.DMA((3,)),
        ],
        compiler_params=pltpu.CompilerParams(
            collective_id=12, has_side_effects=True, vmem_limit_bytes=16 * MIB
        ),
    )(conv, first, second)


def token_total(values):
    return lax.psum(values, "col")


def dp_sum(grad):
    low = grad.astype(jnp.bfloat16)
    return lax.psum_scatter(low, "dp", scatter_dimension=0, tiled=True).astype(jnp.float32)


def pair_sum(grad, dp_count):
    if grad.shape[0] == dp_count:
        return lax.psum_scatter(grad, "dp", scatter_dimension=0)
    return lax.psum_scatter(grad[0], "dp", scatter_dimension=1, tiled=True)


def owner_send(block, root):
    return broadcast(block, "dp", root)


def norm_backward(stream, scale, gain, grad_normed, width):
    weighted = grad_normed * gain[None, :]
    inner = token_total(jnp.sum(stream * weighted, axis=1))
    grad_stream = (
        scale[:, None] * weighted - stream * (scale * scale * scale * inner / width)[:, None]
    )
    grad_gain = jnp.sum(grad_normed * stream * scale[:, None], axis=0)
    return (grad_stream, grad_gain)


def orthogonalize(block):
    work = block
    values = work.astype(jnp.float32)
    work = (values / (jnp.sqrt(jnp.sum(values * values)) + eps_frob)).astype(jnp.bfloat16)
    for step in range(5):
        gram = product_nt(work, work).astype(jnp.bfloat16)
        poly = (poly_second * gram.astype(jnp.float32) + poly_third * product(gram, gram)).astype(
            jnp.bfloat16
        )
        work = (poly_first * work.astype(jnp.float32) + product(poly, work)).astype(jnp.bfloat16)
    return work


def owner_results(blocks, dp_place, dp_count):
    results = [None, None, None, None, None, None]
    for members in ((0, 1, 2), (3, 4, 5)):
        flipped = [blocks[number].shape[0] > blocks[number].shape[1] for number in members]
        wide = [
            blocks[number].T if turn else blocks[number] for number, turn in zip(members, flipped)
        ]
        chosen = wide[0]
        for number, candidate in zip(members[1:], wide[1:]):
            chosen = jnp.where(dp_place == number % dp_count, candidate, chosen)
        done = orthogonalize(chosen)
        for number, turn in zip(members, flipped):
            kept = jnp.where(dp_place == number % dp_count, done, jnp.zeros_like(done))
            results[number] = kept.T if turn else kept
    return results


def dp_moves(moves, sems):
    local_sem, send_sem, recv_sem = sems
    me = lax.axis_index("dp")

    def remote(k, sender, target):
        pairs, source, destination = moves[k]
        return pltpu.make_async_remote_copy(
            src_ref=source(sender, target),
            dst_ref=destination(sender, target),
            send_sem=send_sem.at[k, target],
            recv_sem=recv_sem.at[k, sender],
            device_id={"dp": target},
            device_id_type=MESH,
        )

    def local(k, place):
        pairs, source, destination = moves[k]
        return pltpu.make_async_copy(
            source(place, place), destination(place, place), local_sem.at[k]
        )

    def each(chosen, act):
        for k in chosen:
            for sender, target in moves[k][0]:
                act(k, sender, target)

    def start_one(k, sender, target):
        @pl.when(me == sender)
        def _():
            if sender == target:
                local(k, sender).start()
            else:
                remote(k, sender, target).start()

    def arrive_one(k, sender, target):
        @pl.when(me == target)
        def _():
            if sender == target:
                local(k, sender).wait()
            else:
                remote(k, sender, target).wait_recv()

    def sent_one(k, sender, target):
        if sender != target:

            @pl.when(me == sender)
            def _():
                remote(k, sender, target).wait_send()

    return (
        lambda *chosen: each(chosen, start_one),
        lambda *chosen: each(chosen, arrive_one),
        lambda *chosen: each(chosen, sent_one),
    )


def rows_at(ref, place):
    def pick(sender, target):
        index = sender if place == "sender" else target
        count = ref.shape[0] // 4
        return ref.at[pl.ds(index * count, count)]

    return pick


def entry(ref, place):
    return lambda sender, target: ref.at[sender if place == "sender" else target]


def whole(ref):
    return lambda sender, target: ref


def to_owner(owner):
    return [(sender, owner) for sender in ((owner + step) % 4 for step in range(4))]


def from_owner(owner):
    return [(owner, target) for target in ((owner + step) % 4 for step in range(4))]


SMALL_OWNER, CON_OWNER, GATE_OWNER, UP_OWNER = (2, 1, 3, 0)


def beside(block, rows):
    return jnp.concatenate(
        [block[k * rows : (k + 1) * rows] for k in range(block.shape[0] // rows)], axis=1
    )


def below(block, columns):
    return jnp.concatenate(
        [block[:, k * columns : (k + 1) * columns] for k in range(block.shape[1] // columns)]
    )


def pieces_at_owner(e0, e1, packed, later):
    me = lax.axis_index("dp")

    def piece_for(owner):
        return jnp.where(owner == GATE_OWNER, e0, jnp.where(owner == UP_OWNER, e1, packed))

    leaving = [piece_for(lax.rem(me + step, 4)) for step in range(4)]
    leaving, later = lax.optimization_barrier((leaving, later))
    pieces = leaving[:1]
    for step in range(1, 4):
        pairs = [(sender, (sender + step) % 4) for sender in range(4)]
        pairs = [pair for pair in pairs if pair[1] != SMALL_OWNER]
        pieces.append(lax.ppermute(leaving[step], "dp", pairs))
    return (pieces, later)


def tail_kernel(*refs):
    large, (b0, b1, out) = refs[:4], refs[4:7]
    gates_piece, col_part, dp_part = refs[7:10]
    expand_o, con_o, branch_o, out_o, gates_o, col_o, dp_o = refs[10:17]
    x, packed, pieces, first, second, third, out_v, acc, gram, poly, load_sem = refs[17:28]
    col_buf, dp_buf, gates_dp, gates_col = refs[28:32]
    shares = [
        share_parts("col", col_buf, *refs[32:34]),
        share_parts("dp", dp_buf, *refs[34:36]),
        share_parts("dp", gates_dp, *refs[36:38]),
        share_parts("col", gates_col, *refs[38:40]),
    ]
    sems = refs[40:]
    place = lax.axis_index("col")
    me = lax.axis_index("dp")
    small = out.shape[0]
    width = pieces.shape[1]
    side = x.shape[0]
    rows = side // 4
    moves = [
        (to_owner(SMALL_OWNER), whole(b0), rows_at(first, "sender")),
        (to_owner(SMALL_OWNER), whole(b1), rows_at(second, "sender")),
        (to_owner(SMALL_OWNER), whole(out), entry(out_v, "sender")),
        (from_owner(GATE_OWNER), rows_at(x, "target"), whole(expand_o.at[0])),
        (from_owner(UP_OWNER), rows_at(x, "target"), whole(expand_o.at[1])),
        (from_owner(CON_OWNER), entry(pieces, "target"), whole(con_o)),
        (from_owner(SMALL_OWNER), rows_at(first, "target"), whole(branch_o.at[0])),
        (from_owner(SMALL_OWNER), rows_at(second, "target"), whole(branch_o.at[1])),
        (from_owner(SMALL_OWNER), entry(out_v, "target"), whole(out_o)),
    ]
    start, arrive, sent = dp_moves(moves, sems)
    greet(
        [("dp", lax.rem(me + step, 4)) for step in range(1, 4)]
        + [("col", lax.rem(place + step, 4)) for step in range(1, 4)]
    )
    def loads(owner, target):
        return [
            pltpu.make_async_copy(large[step], target((owner - step) % 4), load_sem.at[step])
            for step in range(4)
        ]

    for owner in (CON_OWNER, GATE_OWNER, UP_OWNER):

        @pl.when(me == owner)
        def _():
            if owner == CON_OWNER:
                copies = loads(owner, lambda j: packed.at[j])
            else:
                copies = loads(owner, lambda j: x.at[pl.ds(j * rows, rows)])
            for copy in copies:
                copy.start()

    shares[0][0](col_part[...])
    shares[2][0](gates_piece[...])
    start(0, 1, 2)
    shares[0][1]()
    summed = col_buf[0] + col_buf[1] + col_buf[2] + col_buf[3]
    col_o[...] = summed
    shares[1][0](jnp.concatenate([summed[:8], dp_part[...]], axis=0))
    shares[2][1]()
    shares[3][0](gates_dp[...].reshape(gates_col.shape[1:]))

    @pl.when(me == CON_OWNER)
    def _():
        for copy in loads(CON_OWNER, lambda j: packed.at[j]):
            copy.wait()
        for j in range(4):
            for k in range(width // rows):
                first_column = j * width + k * rows
                x[:, first_column : first_column + rows] = packed[j, :, k * side : (k + 1) * side].T

    for owner in (GATE_OWNER, UP_OWNER):

        @pl.when(me == owner)
        def _():
            for copy in loads(owner, lambda j: x.at[pl.ds(j * rows, rows)]):
                copy.wait()

    @pl.when(me != SMALL_OWNER)
    def _():
        block_steps(x, acc, gram, poly)

    @pl.when(me == CON_OWNER)
    def _():
        for j in range(4):
            pieces[j] = x[:, j * width : (j + 1) * width].T

    start(3, 4, 5)
    for k, part in enumerate((first, second, third)):
        arrive(k)

        @pl.when(me == SMALL_OWNER)
        def _():
            if k == 2:
                for j in range(4):
                    part[:, j * small : (j + 1) * small] = out_v[j].T
            block_steps(part, acc, gram, poly)
            if k == 2:
                for j in range(4):
                    out_v[j] = part[:, j * small : (j + 1) * small].T

        start(6 + k)
    shares[1][1]()
    dp_o[...] = dp_buf[0] + dp_buf[1] + dp_buf[2] + dp_buf[3]
    shares[3][1]()
    half = gates_col.shape[1]
    for k in range(2):
        for head in range(gates_o.shape[1]):
            columns = slice(head * HS, (head + 1) * HS)
            for j in range(HS // half):
                lines = slice(j * half, (j + 1) * half)
                gates_o[k, head, lines, :] = gates_col[k * (HS // half) + j][:, columns]
    arrive(6, 7, 8, 3, 4, 5)
    sent(0, 1, 2, 3, 4, 5, 6, 7, 8)
    for share in shares:
        share[2]()


def finish_blocks(large, con_shape, b0, b1, out, gates_piece, col_part, dp_part):
    piece = large[0].shape
    rows, total = piece
    side = 4 * rows
    f32, bf16 = jnp.float32, jnp.bfloat16
    shape = jax.ShapeDtypeStruct
    small = pltpu.VMEM((side, b0.shape[1]), bf16)
    quarter = (4 * gates_piece.shape[0], gates_piece.shape[1])
    anywhere = pl.BlockSpec(memory_space=pl.ANY)
    local = pl.BlockSpec(memory_space=pltpu.VMEM)
    sems = pltpu.SemaphoreType.DMA
    shapes = [shape(s, bf16) for s in ((2,) + piece, con_shape, (2,) + b0.shape, out.shape)]
    shapes += [shape((2, quarter[1] // HS, HS, HS), bf16), shape(col_part.shape, f32)]
    shapes += [shape(col_part.shape, f32)]
    return pl.pallas_call(
        tail_kernel,
        out_shape=tuple(shapes),
        in_specs=[anywhere] * 7 + [local] * 3,
        out_specs=[anywhere] * 4 + [local] * 3,
        scratch_shapes=[
            pltpu.VMEM((side, total), bf16),
            pltpu.VMEM((4,) + piece, bf16),
            pltpu.VMEM((4,) + con_shape, bf16),
            small,
            small,
            small,
            pltpu.VMEM((4,) + out.shape, bf16),
        ]
        + work_space(side)
        + [sems((4,))]
        + [
            pltpu.VMEM((4,) + col_part.shape, f32),
            pltpu.VMEM((4,) + col_part.shape, f32),
            pltpu.VMEM((4,) + gates_piece.shape, bf16),
            pltpu.VMEM((4,) + quarter, bf16),
        ]
        + [sems((4,))] * 8
        + [sems((9,)), sems((9, 4)), sems((9, 4))],
        compiler_params=pltpu.CompilerParams(
            collective_id=0, has_side_effects=True, vmem_limit_bytes=40 * MIB
        ),
    )(*large, b0, b1, out, gates_piece, col_part, dp_part)


def grouped_step(grad, moment, weight, rate):
    new_moment = momentum_rate * moment + grad
    rows, cols = new_moment.shape
    grouped = new_moment.reshape(rows, cols // GROUP, GROUP)
    norm_sq = jnp.mean(grouped * grouped, axis=2, keepdims=True)
    update = (grouped * lax.rsqrt(norm_sq + eps_norm)).reshape(rows, cols)
    return (new_moment, weight - rate * update)


def shards(
    block_input,
    segment_ids,
    output_cotangent,
    norm_gains,
    branch_weights,
    mixer_vectors,
    gate_blocks,
    output_weights,
    expand_weights,
    contract_weights,
    gains_momentum,
    branch_momentum,
    vectors_momentum,
    gates_momentum,
    output_momentum,
    expand_momentum,
    contract_momentum,
):
    f32 = jnp.float32
    bf16 = jnp.bfloat16
    col_count = lax.axis_size("col")
    col_place = lax.axis_index("col")
    dp_count = lax.axis_size("dp")
    dp_place = lax.axis_index("dp")
    group_rows = block_input.shape[0]
    rows = group_rows // col_count
    lanes = mixer_vectors.shape[1]
    heads_here = lanes // HS
    feature_count = block_input.shape[1]
    width = feature_count * col_count
    first_row = col_place * rows
    reach = CONV - 1
    seg_row = segment_ids[0]
    seg_ext = jnp.concatenate(
        [jnp.full((reach,), -1, jnp.int32), seg_row, jnp.full((reach,), -2, jnp.int32)]
    )
    seg_here = lax.dynamic_slice_in_dim(seg_ext, first_row + reach, rows + reach)
    masks = []
    for shift in range(CONV):
        earlier = lax.dynamic_slice_in_dim(seg_ext, first_row + reach - shift, rows + reach)
        masks.append((earlier == seg_here).astype(f32))
    reset_rows = masks[1][:rows] < 0.5
    stream = block_input.astype(f32)
    branch_pre, normed_low, scale_rows, contract_term = spread_product(
        block_input,
        branch_weights,
        False,
        640,
        2,
        norm_gains[0],
        (output_cotangent, contract_weights),
    )
    scale_one = scale_rows[0]
    grad_activated = lax.psum_scatter(contract_term, "col", scatter_dimension=0, tiled=True)
    mixed = branch_pre[0]
    gelu_in = branch_pre[1]
    edge = from_behind(mixed[rows - reach :], "col", 1)
    extended = jnp.concatenate([edge, mixed], axis=0)
    windows = []
    conv_out = jnp.zeros((rows, lanes), f32) + mixer_vectors[CONV][None, :]
    for shift in range(CONV):
        window = extended[reach - shift : reach - shift + rows] * masks[shift][:rows, None]
        windows.append(window)
        conv_out = conv_out + mixer_vectors[shift][None, :] * window
    conv_low = conv_out.astype(bf16).reshape(rows, heads_here, HS)
    gate_pre = jnp.einsum(
        "thi,ghij->tghj", conv_low, gate_blocks, preferred_element_type=f32
    ).reshape(rows, 2, lanes)
    gate_pre = gate_pre + mixer_vectors[CONV + 1 : CONV + 3][None]

    def recurrence_terms(conv_values, gate_values, rate_values):
        input_gate = jax.nn.sigmoid(gate_values[:, 0])
        decay_gate = jax.nn.sigmoid(gate_values[:, 1])
        log_decay = -decay_scale * decay_gate * jax.nn.softplus(rate_values)[None, :]
        inject_scale = jnp.where(reset_rows[:, None], 1.0, jnp.sqrt(1.0 - jnp.exp(2.0 * log_decay)))
        decay_values = jnp.where(reset_rows[:, None], 0.0, jnp.exp(log_decay))
        return (decay_values, inject_scale * input_gate * conv_values)

    (decay, inject), pull_terms = jax.vjp(
        recurrence_terms, conv_out, gate_pre, mixer_vectors[CONV + 3]
    )
    local_a, local_b = linear_scan(decay, inject, False)
    identity = (jnp.ones((lanes,), f32), jnp.zeros((lanes,), f32))
    incoming = prefix((local_a[-1], local_b[-1]), "col", link, identity, False)
    carried = incoming[1]
    state = local_a * carried[None, :] + local_b
    gelu_out, pull_gelu = jax.vjp(gelu_tanh, gelu_in)
    hidden = (gelu_out * state).astype(bf16)
    hidden_all, middle, normed_two_low, scale_two = meet_product(
        hidden[None],
        output_weights,
        False,
        256,
        3,
        stream=block_input,
        gain=norm_gains[1],
    )
    expand_pre = spread_product(normed_two_low, expand_weights, False, 768, 4)

    def geglu(gate_values, up_values):
        return gelu_tanh(gate_values) * up_values

    activated, pull_geglu = jax.vjp(geglu, expand_pre[0], expand_pre[1])
    activated_low = activated.astype(bf16)
    activated_low, grad_activated = lax.optimization_barrier((activated_low, grad_activated))
    activated_all, contract_grad = meet_gradient(activated_low[None], 640, 5, output_cotangent)
    cot_values = output_cotangent.astype(f32)
    grad_activated, contract_grad = lax.optimization_barrier((grad_activated, contract_grad))
    grad_gate, grad_up = pull_geglu(grad_activated.astype(f32))
    grad_expand_low = jnp.stack([grad_gate, grad_up]).astype(bf16)
    grad_expand_low, contract_grad = lax.optimization_barrier((grad_expand_low, contract_grad))
    parts = dp_count if feature_count % (16 * dp_count) == 0 else 1
    grad_normed_two, expand_grad = meet_product(
        grad_expand_low, expand_weights, True, 768, 7, normed_two_low.T, "wide", parts
    )
    grad_middle_norm, gain_two_grad = norm_backward(
        middle, scale_two, norm_gains[1], grad_normed_two, width
    )
    grad_middle = cot_values + grad_middle_norm
    grad_branch_low = grad_middle.astype(bf16)
    output_grad = product_tn(hidden_all[0], grad_branch_low)
    grad_hidden = spread_product(grad_branch_low, output_weights, True, 256, 8)[0]
    grad_state = grad_hidden * gelu_out
    (grad_gelu_in,) = pull_gelu(grad_hidden * state)
    shifted_decay = jnp.concatenate([decay[1:], jnp.ones((1, lanes), f32)], axis=0)
    back_a, back_b = linear_scan(shifted_decay, grad_state, True)
    from_later = prefix((decay[0] * back_a[0], decay[0] * back_b[0]), "col", link, identity, True)
    grad_total = back_a * from_later[1][None, :] + back_b
    previous = jnp.concatenate([carried[None, :], state[:-1]], axis=0)
    grad_conv_direct, grad_gate_pre, grad_rate = pull_terms((grad_total * previous, grad_total))
    grad_gate_low = grad_gate_pre.astype(bf16)
    grad_gate_heads = grad_gate_low.reshape(rows, 2, heads_here, HS)
    grad_conv = grad_conv_direct + jnp.einsum(
        "tghj,ghij->thi", grad_gate_heads, gate_blocks, preferred_element_type=f32
    ).reshape(rows, lanes)
    parts = dp_count if feature_count % (16 * dp_count) == 0 else 1
    planes = dp_count == 4 and parts == 4 and 2 * feature_count <= lanes and group_rows <= lanes
    gate_bias_grad = jnp.sum(grad_gate_low.astype(f32), axis=0)
    after = from_behind(grad_conv[:reach], "col", -1)
    grad_conv_ext = jnp.concatenate([grad_conv, after], axis=0)
    grad_mixed = jnp.zeros((rows, lanes), f32)
    tap_grads = []
    for shift in range(CONV):
        masked = grad_conv_ext * masks[shift][:, None]
        grad_mixed = grad_mixed + mixer_vectors[shift][None, :] * masked[shift : shift + rows]
        tap_grads.append(jnp.sum(grad_conv * windows[shift], axis=0))
    grad_mixed, activated_all = lax.optimization_barrier((grad_mixed, activated_all))
    contracted_low = product(activated_all[0], contract_weights).astype(bf16)
    contracted = contracted_low.astype(f32) + lax.ppermute(
        contracted_low, "row", [(0, 1), (1, 0)]
    ).astype(f32)
    block_output = (middle + contracted).astype(bf16)
    vector_rows = tap_grads + [
        jnp.sum(grad_conv, axis=0),
        gate_bias_grad[0],
        gate_bias_grad[1],
        grad_rate,
    ]
    vectors_grad = jnp.stack(vector_rows)
    grad_branch_pre = jnp.stack([grad_mixed, grad_gelu_in]).astype(bf16)
    grad_normed_one, branch_grad = meet_product(
        grad_branch_pre, branch_weights, True, 640, 9, normed_low.T, "wide", parts
    )
    if planes:
        contract_sum = pair_sum(contract_grad.reshape((4, -1) + contract_grad.shape[1:]), 4)
        expand_grad, contract_sum = lax.optimization_barrier((expand_grad, contract_sum))
        expand_sum = pair_sum(expand_grad, 4)
        con_low = (momentum_rate * contract_momentum[0] + contract_sum).astype(bf16)
        con_low = beside(con_low, expand_momentum.shape[2])
        weighted = grad_normed_one * norm_gains[0][None, :]
        inner_part = jnp.sum(stream * weighted, axis=1)
        gain_one_grad = jnp.sum(grad_normed_one * stream * scale_one[:, None], axis=0)
        col_part = jnp.concatenate(
            [
                vectors_grad,
                jnp.pad(inner_part, (0, lanes - group_rows))[None],
                jnp.zeros((7, lanes), f32),
            ]
        )
        gains_row = jnp.concatenate([gain_one_grad, gain_two_grad])
        dp_part = jnp.pad(gains_row[None], ((0, 7), (0, lanes - 2 * feature_count)))
        gates_part = gates_product(
            conv_low.reshape(rows, lanes), grad_gate_low[:, 0], grad_gate_low[:, 1]
        )
        piece_rows = branch_grad.shape[2]
        small_grad = jnp.concatenate(
            [
                branch_grad.reshape(4, 2 * piece_rows, lanes),
                jnp.stack([beside(part, piece_rows) for part in jnp.split(output_grad.astype(bf16), 4)]),
                gates_part.reshape(4, -1, lanes),
            ],
            axis=1,
        )
        con_low, expand_sum, col_part, dp_part, small_grad, block_output = (
            lax.optimization_barrier(
                (con_low, expand_sum, col_part, dp_part, small_grad, block_output)
            )
        )
        expand_low = (momentum_rate * expand_momentum[:, 0] + expand_sum).astype(bf16)
        small_grad, expand_sum = lax.optimization_barrier((small_grad, expand_sum))
        large, (expand_sum, contract_sum) = pieces_at_owner(
            expand_low[0], expand_low[1], con_low, (expand_sum, contract_sum)
        )
        small_sum = pair_sum(small_grad, 4)
        branch_sum = small_sum[: 2 * piece_rows].reshape(2, piece_rows, lanes)
        output_sum = below(small_sum[2 * piece_rows : 3 * piece_rows], output_momentum.shape[2])
        branch_low = (momentum_rate * branch_momentum[:, 0] + branch_sum).astype(bf16)
        output_low = (momentum_rate * output_momentum[0] + output_sum).astype(bf16)
        expand_orth, con, branch_orth, out, gates_all, col_total, dp_total = finish_blocks(
            large,
            contract_momentum.shape[1:],
            branch_low[0],
            branch_low[1],
            output_low,
            small_sum[3 * piece_rows :],
            col_part,
            dp_part,
        )
        output_sum = output_sum.astype(f32)
        gates_total = gates_all.astype(f32)
        vectors_total = dp_total[:8]
        gains_total = dp_total[8, : 2 * feature_count].reshape(2, feature_count)
        inner = col_total[8, :group_rows]
        grad_stream_norm = (
            scale_one[:, None] * weighted
            - stream * (scale_one * scale_one * scale_one * inner / width)[:, None]
        )
    else:
        grad_stream_norm, gain_one_grad = norm_backward(
            stream, scale_one, norm_gains[0], grad_normed_one, width
        )
        vectors_total, gains_total = lax.psum(
            (lax.psum(vectors_grad, "col"), jnp.stack([gain_one_grad, gain_two_grad])), "dp"
        )
        gates_grad = jnp.einsum(
            "thi,tghj->ghij", conv_low, grad_gate_heads, preferred_element_type=f32
        ).astype(bf16)
        branch_sum = pair_sum(branch_grad, dp_count)
        expand_sum = pair_sum(expand_grad, dp_count)
        output_sum = dp_sum(output_grad)
        contract_sum = dp_sum(contract_grad)
        gates_total = lax.psum(gates_grad, ("dp", "col")).astype(f32)
    input_grad = (grad_middle + grad_stream_norm).astype(bf16)
    branch_sum = branch_sum.astype(f32)
    expand_sum = expand_sum.astype(f32)
    contract_sum = contract_sum.astype(f32)
    branch_moment = momentum_rate * branch_momentum[:, 0] + branch_sum
    expand_moment = momentum_rate * expand_momentum[:, 0] + expand_sum
    output_moment = momentum_rate * output_momentum[0] + output_sum
    contract_moment = momentum_rate * contract_momentum[0] + contract_sum
    if not planes:
        moments = (*branch_moment, output_moment, *expand_moment, contract_moment)
        lows = [moment.astype(bf16) for moment in moments]
        gathered = [lax.all_gather(low, "dp", axis=0, tiled=True) for low in lows]
        orth = owner_results(gathered, dp_place, dp_count)
        pieces = [
            lax.dynamic_slice_in_dim(
                owner_send(orth[number], number % dp_count),
                dp_place * lows[number].shape[0],
                lows[number].shape[0],
                0,
            )
            for number in range(6)
        ]
        branch_orth, expand_orth = jnp.stack(pieces[:2]), jnp.stack(pieces[3:5])
        out, con = pieces[2], pieces[5]

    def stepped(weight, orth, axis):
        count = orth.shape[axis]
        piece = lax.dynamic_slice_in_dim(weight, dp_place * count, count, axis).astype(f32)
        tall = max(1.0, weight.shape[axis] / weight.shape[axis + 1]) ** 0.5
        return piece - muon_rate * tall * orth.astype(f32)

    branch_new = stepped(branch_weights, branch_orth, 1)
    expand_new = stepped(expand_weights, expand_orth, 1)
    output_new = stepped(output_weights, out, 0)
    contract_new = stepped(contract_weights, con, 0)
    gates_moment = momentum_rate * gates_momentum + gates_total
    gate_sq = jnp.mean(gates_moment * gates_moment, axis=(2, 3), keepdims=True)
    gates_new = gate_blocks.astype(f32) - gate_rate * gates_moment * lax.rsqrt(gate_sq + eps_norm)
    vectors_moment, vectors_new = grouped_step(
        vectors_total, vectors_momentum, mixer_vectors, vector_rate
    )
    gains_moment, gains_new = grouped_step(gains_total, gains_momentum, norm_gains, vector_rate)
    return (
        block_output,
        input_grad,
        gains_total,
        branch_sum[:, None],
        vectors_total,
        gates_total,
        output_sum[None],
        expand_sum[:, None],
        contract_sum[None],
        gains_new,
        branch_new[:, None],
        vectors_new,
        gates_new,
        output_new[None],
        expand_new[:, None],
        contract_new[None],
        gains_moment,
        branch_moment[:, None],
        vectors_moment,
        gates_moment,
        output_moment[None],
        expand_moment[:, None],
        contract_moment[None],
    )


def solution(mesh):
    return jax.shard_map(
        shards,
        mesh=mesh,
        in_specs=(
            P("dp", "col"),
            P("dp", None),
            P("dp", "col"),
            P(None, "col"),
            P(None, "col", "row"),
            P(None, "row"),
            P(None, "row", None, None),
            P("row", "col"),
            P(None, "col", "row"),
            P("row", "col"),
            P(None, "col"),
            P(None, "col", "dp", "row"),
            P(None, "row"),
            P(None, "row", None, None),
            P("row", "dp", "col"),
            P(None, "col", "dp", "row"),
            P("row", "dp", "col"),
        ),
        out_specs=(
            P("dp", "col"),
            P("dp", "col"),
            P(None, "col"),
            P(None, "col", "dp", "row"),
            P(None, "row"),
            P(None, "row", None, None),
            P("row", "dp", "col"),
            P(None, "col", "dp", "row"),
            P("row", "dp", "col"),
            P(None, "col"),
            P(None, "col", "dp", "row"),
            P(None, "row"),
            P(None, "row", None, None),
            P("row", "dp", "col"),
            P(None, "col", "dp", "row"),
            P("row", "dp", "col"),
            P(None, "col"),
            P(None, "col", "dp", "row"),
            P(None, "row"),
            P(None, "row", None, None),
            P("row", "dp", "col"),
            P(None, "col", "dp", "row"),
            P("row", "dp", "col"),
        ),
        check_vma=False,
    )
```

```python
import functools

import jax
import jax.numpy as jnp
from jax import lax
from jax.experimental import pallas as pl
from jax.experimental.pallas import tpu as pltpu
from jax.sharding import PartitionSpec as P

CONV = 4
GROUP = 128
HS = 256


eps_norm = 1e-06
eps_frob = 1e-07
poly_first = 3.4445
poly_second = -4.775
poly_third = 2.0315
momentum_rate = 0.9
muon_rate = 0.1
gate_rate = 0.02
vector_rate = 0.3
decay_scale = 8.0


def broadcast(value, axis, source):
    kept = jnp.where(lax.axis_index(axis) == source, value, 0).astype(value.dtype)
    return lax.psum(kept, axis)


def from_behind(value, axis, steps):
    count = lax.axis_size(axis)
    initial, last = (max(0, -steps), min(count, count - steps))
    return lax.ppermute(value, axis, [(source, source + steps) for source in range(initial, last)])


def prefix(value, axis, combine, identity, reverse):
    count, here = (lax.axis_size(axis), lax.axis_index(axis))
    joined = lax.all_gather(jnp.stack(value), axis)
    everything = tuple(joined[:, k] for k in range(len(value)))
    start = jax.tree.map(
        lambda part, zero: jnp.broadcast_to(jnp.asarray(zero, part.dtype), part.shape),
        value,
        identity,
    )

    def lap(k, before):
        at = count - 1 - k if reverse else k
        reached = at > here if reverse else at < here
        new = combine(before, jax.tree.map(lambda part: part[at], everything))
        return jax.tree.map(lambda a, b: jnp.where(reached, a, b), new, before)

    return lax.fori_loop(0, count, lap, start)


def gelu_tanh(value):
    return jax.nn.gelu(value, approximate=True)


def product(left, right):
    return jnp.dot(left, right, preferred_element_type=jnp.float32)


def product_tn(left, right):
    return lax.dot_general(
        left, right, (((0,), (0,)), ((), ())), preferred_element_type=jnp.float32
    )


def product_nt(left, right):
    return lax.dot_general(
        left, right, (((1,), (1,)), ((), ())), preferred_element_type=jnp.float32
    )


def link(first, second):
    return (first[0] * second[0], second[0] * first[1] + second[1])


def scan_kernel(reverse, decay_ref, value_ref, prod_ref, sum_ref):
    rows, lanes = decay_ref.shape
    groups = rows // 8

    def lap(k, carry):
        base = pl.multiple_of((groups - 1 - k if reverse else k) * 8, 8)
        decay = decay_ref[pl.ds(base, 8), :]
        value = value_ref[pl.ds(base, 8), :]
        prod, total = carry
        prods, totals = [None] * 8, [None] * 8
        for j in range(7, -1, -1) if reverse else range(8):
            prod = decay[j : j + 1] * prod
            total = decay[j : j + 1] * total + value[j : j + 1]
            prods[j], totals[j] = prod, total
        prod_ref[pl.ds(base, 8), :] = jnp.concatenate(prods, axis=0)
        sum_ref[pl.ds(base, 8), :] = jnp.concatenate(totals, axis=0)
        return (prod, total)

    start = (jnp.ones((1, lanes), jnp.float32), jnp.zeros((1, lanes), jnp.float32))
    lax.fori_loop(0, groups, lap, start)


def linear_scan(decay, value, reverse):
    shape = jax.ShapeDtypeStruct(decay.shape, jnp.float32)
    return pl.pallas_call(
        functools.partial(scan_kernel, reverse),
        out_shape=(shape, shape),
        compiler_params=pltpu.CompilerParams(vmem_limit_bytes=16 * 1024 * 1024),
    )(decay, value)


MESH = pl.DeviceIdType.MESH
MIB = 1024 * 1024


def col_places():
    me = lax.axis_index("col")
    near_bit = lax.rem(me, 2)
    far_bit = lax.div(me, 2)
    return (me, near_bit, far_bit, me + 1 - 2 * near_bit, lax.rem(me + 2, 4))


def greet(axis_places):
    barrier = pltpu.get_barrier_semaphore()
    for axis, place in axis_places:
        pl.semaphore_signal(barrier, inc=1, device_id={axis: place}, device_id_type=MESH)
    pl.semaphore_wait(barrier, len(axis_places))


def dot_nn(left, right):
    return lax.dot_general(
        left, right, (((1,), (0,)), ((), ())), preferred_element_type=jnp.float32
    )


def dot_nt(left, right):
    return lax.dot_general(
        left, right, (((1,), (1,)), ((), ())), preferred_element_type=jnp.float32
    )


def columns_of(j, width, per):
    return (lax.div(j, per), pl.ds(pl.multiple_of(lax.rem(j, per) * width, width), width))


def share_parts(axis, buf, send_sem, recv_sem):
    me = lax.axis_index(axis)

    def copy(step):
        return pltpu.make_async_remote_copy(
            src_ref=buf.at[me],
            dst_ref=buf.at[me],
            send_sem=send_sem.at[step],
            recv_sem=recv_sem.at[step],
            device_id={axis: lax.rem(me + step, 4)},
            device_id_type=MESH,
        )

    def start(value):
        buf[me] = value
        for step in range(1, 4):
            copy(step).start()

    def arrive():
        for step in range(1, 4):
            copy(step).wait_recv()

    def finish():
        for step in range(1, 4):
            copy(step).wait_send()

    return (start, arrive, finish)


def col_peers():
    me = lax.axis_index("col")
    return [("col", lax.rem(me + step, 4)) for step in range(1, 4)]


def row_scales(values, share, buf):
    tokens, features = values.shape
    start, arrive, finish = share
    squares = jnp.sum(values * values, axis=1, keepdims=True)
    start(jnp.broadcast_to(squares, (tokens, 128)).T[:8])
    arrive()
    total = buf[0] + buf[1] + buf[2] + buf[3]
    scales = lax.rsqrt(total / (4 * features) + eps_norm)
    finish()
    return (scales, jnp.broadcast_to(scales[:1], (128, tokens)).T[:, :1])


def spread_kernel(
    flip, normed, *refs
):
    if normed:
        stream, gain, cot, w, side_w, out, low_out, scale_out, side_out = refs[:9]
        lhs, nbuf, side_buf, stage, nsend, nrecv, side_sem, stage_sem = refs[9:17]
        refs = refs[17:]
    else:
        lhs, w, out = refs[:3]
        refs = refs[3:]
    wbuf, send1, recv1, own, send2, recv2, wsem, s1s, s1r, s2s, s2r = refs
    chunks, rows, width = send2.shape
    per = out.shape[2] // width
    me, near_bit, far_bit, near, far = col_places()
    depth = lhs.shape[3]

    def w_copy(j):
        k, cols = columns_of(j, width, per)
        return pltpu.make_async_copy(
            w.at[cols, :] if flip else w.at[k, :, cols], wbuf.at[j], wsem.at[j]
        )

    def near_copy(j):
        return pltpu.make_async_remote_copy(
            src_ref=send1.at[j],
            dst_ref=recv1.at[j],
            send_sem=s1s.at[j],
            recv_sem=s1r.at[j],
            device_id={"col": near},
            device_id_type=MESH,
        )

    def far_copy(j):
        return pltpu.make_async_remote_copy(
            src_ref=send2.at[j],
            dst_ref=recv2.at[j],
            send_sem=s2s.at[j],
            recv_sem=s2r.at[j],
            device_id={"col": far},
            device_id_type=MESH,
        )

    def loop(count, act):
        def lap(j, carry):
            act(j)
            return carry

        lax.fori_loop(0, count, lap, 0)

    loop(chunks, lambda j: w_copy(j).start())
    if normed:
        span = side_buf.shape[1]
        side_chunks = side_buf.shape[0]

        def side_lines(j):
            return pl.ds(pl.multiple_of(j * span, span), span)

        def side_copy(j):
            return pltpu.make_async_copy(
                side_w.at[side_lines(j), :], side_buf.at[j], side_sem.at[j]
            )

        def stage_copy(j):
            return pltpu.make_async_copy(
                stage.at[j], side_out.at[:, side_lines(j)], stage_sem.at[j]
            )

        def side_part(j):
            side_copy(j).wait()
            stage[j] = dot_nt(cot[...], side_buf[j]).astype(jnp.bfloat16)
            stage_copy(j).start()

        loop(side_chunks, lambda j: side_copy(j).start())
        greet(col_peers())
        values = stream[...].astype(jnp.float32)
        scales, column = row_scales(values, share_parts("col", nbuf, nsend, nrecv), nbuf)
        scale_out[...] = scales
        low = (values * column * gain[...]).astype(jnp.bfloat16)
        low_out[...] = low
        lhs[...] = low.reshape(lhs.shape)
    else:
        greet((("col", near), ("col", far)))
    dot = dot_nt if flip else dot_nn

    def first(j):
        w_copy(j).wait()
        part = wbuf[j]
        theirs = dot(lhs[:, 1 - near_bit].reshape(2 * rows, depth), part)
        send1[j] = theirs.astype(jnp.bfloat16).reshape(2, rows, width)
        near_copy(j).start()
        mine = dot(lhs[:, near_bit].reshape(2 * rows, depth), part)
        own[j] = mine.reshape(2, rows, width)

    def second(j):
        near_copy(j).wait_recv()
        going = own[j, 1 - far_bit] + recv1[j, 1 - far_bit].astype(jnp.float32)
        send2[j] = going.astype(jnp.bfloat16)
        far_copy(j).start()
        own[j, far_bit] = own[j, far_bit] + recv1[j, far_bit].astype(jnp.float32)

    def third(j):
        far_copy(j).wait_recv()
        k, cols = columns_of(j, width, per)
        out[k, :, cols] = own[j, far_bit] + recv2[j].astype(jnp.float32)

    first(0)

    def both(j):
        first(j + 1)
        second(j)

    loop(chunks - 1, both)
    second(chunks - 1)
    if normed:
        loop(side_chunks, side_part)
    loop(chunks, third)
    if normed:
        loop(side_chunks, lambda j: stage_copy(j).wait())

    def drain(j):
        near_copy(j).wait_send()
        far_copy(j).wait_send()

    loop(chunks, drain)


def spread_product(lhs, w, flip, width, collective, gain=None, side=None):
    tokens, depth = lhs.shape
    rows = tokens // 4
    pairs = 1 if flip else w.shape[0]
    total = w.shape[0] if flip else w.shape[2]
    chunks = pairs * total // width
    tile = (width, depth) if flip else (depth, width)
    bf16, f32 = jnp.bfloat16, jnp.float32
    local = pl.BlockSpec(memory_space=pltpu.VMEM)
    shapes = [jax.ShapeDtypeStruct((pairs, rows, total), f32)]
    scratch = []
    anywhere = pl.BlockSpec(memory_space=pl.ANY)
    weights, remote_outs = [w], []
    if gain is None:
        inputs = [lhs.reshape(2, 2, rows, depth)]
    else:
        cot, side_w = side
        span = 768 if side_w.shape[0] % 768 == 0 else 256
        side_chunks = side_w.shape[0] // span
        inputs = [lhs, gain[None], cot]
        weights = [w, side_w]
        remote_outs = [jax.ShapeDtypeStruct((tokens, side_w.shape[0]), bf16)]
        shapes += [
            jax.ShapeDtypeStruct((tokens, depth), bf16),
            jax.ShapeDtypeStruct((8, tokens), f32),
        ]
        scratch = [pltpu.VMEM((2, 2, rows, depth), bf16), pltpu.VMEM((4, 8, tokens), f32)]
        scratch += [pltpu.VMEM((side_chunks, span, depth), bf16)]
        scratch += [pltpu.VMEM((side_chunks, tokens, span), bf16)]
        scratch += [pltpu.SemaphoreType.DMA((4,))] * 2
        scratch += [pltpu.SemaphoreType.DMA((side_chunks,))] * 2
    result = pl.pallas_call(
        functools.partial(spread_kernel, flip, gain is not None),
        out_shape=tuple(shapes + remote_outs),
        in_specs=[local] * len(inputs) + [anywhere] * len(weights),
        out_specs=[local] * len(shapes) + [anywhere] * len(remote_outs),
        scratch_shapes=scratch
        + [
            pltpu.VMEM((chunks,) + tile, bf16),
            pltpu.VMEM((chunks, 2, rows, width), bf16),
            pltpu.VMEM((chunks, 2, rows, width), bf16),
            pltpu.VMEM((chunks, 2, rows, width), f32),
            pltpu.VMEM((chunks, rows, width), bf16),
            pltpu.VMEM((chunks, rows, width), bf16),
        ]
        + [pltpu.SemaphoreType.DMA((chunks,))] * 5,
        compiler_params=pltpu.CompilerParams(
            collective_id=collective, has_side_effects=True, vmem_limit_bytes=56 * MIB
        ),
    )(*inputs, *weights)
    return result[0] if gain is None else result


def meet_kernel(flip, grad_mode, *refs):
    lone = grad_mode == "lone"
    if lone:
        piece, side, all_out, grad_out, buf, osem, ns, nr, fs, fr, rs, rr, stage, gsem = refs
    elif grad_mode:
        piece, w, side, prod, grad_out = refs[:5]
        refs = refs[5:]
    else:
        piece, w, stream, gain, all_out, prod, low_out, scale_out = refs[:8]
        nbuf, nsend, nrecv = refs[-3:]
        refs = refs[8:-3]
    if not lone:
        wbuf, buf, acc, sendx, recvx, wsem, osem, ns, nr, fs, fr, rs, rr, xs, xr = refs[:15]
    if grad_mode and not lone:
        stage, gsem = refs[15:]
    chunks, _, _, rows, width = buf.shape
    per = piece.shape[2] // width
    me, near_bit, far_bit, near, far = col_places()
    across = 1 - lax.axis_index("row")
    f32, bf16 = jnp.float32, jnp.bfloat16

    def w_copy(j):
        k, cols = columns_of(j, width, per)
        return pltpu.make_async_copy(
            w.at[k, :, cols] if flip else w.at[cols, :], wbuf.at[j], wsem.at[j]
        )

    def move(j, source, near_place, far_place, sems, target):
        return pltpu.make_async_remote_copy(
            src_ref=source,
            dst_ref=buf.at[j, far_place, near_place],
            send_sem=sems[0].at[j],
            recv_sem=sems[1].at[j],
            device_id={"col": target},
            device_id_type=MESH,
        )

    def piece_at(j):
        k, cols = columns_of(j, width, per)
        return piece.at[k, :, cols]

    def far_copy(j):
        return move(j, piece_at(j), near_bit, far_bit, (fs, fr), far)

    def near_copy(j):
        return move(j, piece_at(j), near_bit, far_bit, (ns, nr), near)

    def relay(j):
        return move(j, buf.at[j, 1 - far_bit, near_bit], near_bit, 1 - far_bit, (rs, rr), near)

    def out_copy(j):
        k, cols = columns_of(j, width, per)
        return pltpu.make_async_copy(buf.at[j], all_out.at[k, :, :, :, cols], osem.at[j])

    def cross(half):
        return pltpu.make_async_remote_copy(
            src_ref=sendx.at[half],
            dst_ref=recvx.at[half],
            send_sem=xs.at[half],
            recv_sem=xr.at[half],
            device_id={"row": across},
            device_id_type=MESH,
        )

    def loop(count, act):
        def lap(j, carry):
            act(j)
            return carry

        lax.fori_loop(0, count, lap, 0)

    if not lone:
        loop(chunks, lambda j: w_copy(j).start())
    if lone:
        greet((("col", near), ("col", far)))
    elif grad_mode:
        greet((("col", near), ("col", far), ("row", across)))
    else:
        greet(col_peers() + [("row", across)])

    def begin(j):
        far_copy(j).start()
        near_copy(j).start()
        k, cols = columns_of(j, width, per)
        buf[j, far_bit, near_bit] = piece[k, :, cols]

    loop(chunks, begin)
    if not lone:
        acc[...] = jnp.zeros_like(acc)
    dot = dot_nt if flip else dot_nn

    def add(j, half):
        both = buf[j, half].reshape(2 * rows, width)
        acc[half] = acc[half] + dot(both, wbuf[j])

    def here(j):
        near_copy(j).wait_recv()
        if not lone:
            w_copy(j).wait()
            add(j, far_bit)

    loop(chunks, here)
    if not lone:
        sendx[far_bit] = acc[far_bit].astype(bf16)
        cross(far_bit).start()

    def grad_copy(j):
        return grad_moves(j)

    if grad_mode == "wide":
        parts = grad_out.shape[0]

        def grad_moves(j):
            k, cols = columns_of(j, width, per)
            return pltpu.make_async_copy(
                stage.at[lax.rem(j, 2)], grad_out.at[:, k, :, cols], gsem.at[lax.rem(j, 2)]
            )

        def grad_part(j):
            block = buf[j].reshape(4 * rows, width)
            total = dot_nn(side[...], block).astype(bf16)
            stage[lax.rem(j, 2)] = total.reshape(stage.shape[1:])

    if lone:

        def grad_moves(j):
            return pltpu.make_async_copy(
                stage.at[lax.rem(j, 2)],
                grad_out.at[pl.ds(pl.multiple_of(j * width, width), width), :],
                gsem.at[lax.rem(j, 2)],
            )

        def grad_part(j):
            block = buf[j].reshape(4 * rows, width)
            stage[lax.rem(j, 2)] = dot_nn(block.T, side[...]).astype(bf16)

    def pass_on(j):
        far_copy(j).wait_recv()
        relay(j).start()

    def there(j):
        relay(j).wait_recv()
        if lone or not grad_mode:
            out_copy(j).start()
        if not lone:
            add(j, 1 - far_bit)
        if grad_mode:

            @pl.when(j >= 2)
            def _():
                grad_moves(j - 2).wait()

            grad_part(j)
            grad_moves(j).start()

    pass_on(0)

    def both(j):
        pass_on(j + 1)
        there(j)

    loop(chunks - 1, both)
    there(chunks - 1)
    if not lone:
        sendx[1 - far_bit] = acc[1 - far_bit].astype(bf16)
        cross(1 - far_bit).start()

        def settle(half):
            cross(half).wait_recv()
            prod[half] = sendx[half].astype(f32) + recvx[half].astype(f32)

        settle(far_bit)
        settle(1 - far_bit)
    if not grad_mode:
        values = prod[...].reshape(stream.shape) + stream[...].astype(f32)
        prod[...] = values.reshape(prod.shape)
        scales, column = row_scales(values, share_parts("col", nbuf, nsend, nrecv), nbuf)
        scale_out[...] = scales
        low_out[...] = (values * column * gain[...]).astype(bf16)

    def drain(j):
        near_copy(j).wait_send()
        far_copy(j).wait_send()
        relay(j).wait_send()
        if lone or not grad_mode:
            out_copy(j).wait()

    loop(chunks, drain)
    if not lone:
        cross(far_bit).wait_send()
        cross(1 - far_bit).wait_send()
    if grad_mode:
        for j in range(max(0, chunks - 2), chunks):
            grad_moves(j).wait()


def meet_gradient(piece, width, collective, side):
    pairs, rows, total = piece.shape
    chunks = pairs * total // width
    bf16 = jnp.bfloat16
    local = pl.BlockSpec(memory_space=pltpu.VMEM)
    anywhere = pl.BlockSpec(memory_space=pl.ANY)
    everything, gradient = pl.pallas_call(
        functools.partial(meet_kernel, False, "lone"),
        out_shape=(
            jax.ShapeDtypeStruct((pairs, 2, 2, rows, total), bf16),
            jax.ShapeDtypeStruct((total, side.shape[1]), bf16),
        ),
        in_specs=[local, local],
        out_specs=[anywhere, anywhere],
        scratch_shapes=[pltpu.VMEM((chunks, 2, 2, rows, width), bf16)]
        + [pltpu.SemaphoreType.DMA((chunks,))] * 7
        + [pltpu.VMEM((2, width, side.shape[1]), bf16), pltpu.SemaphoreType.DMA((2,))],
        compiler_params=pltpu.CompilerParams(
            collective_id=collective, has_side_effects=True, vmem_limit_bytes=40 * MIB
        ),
    )(piece, side)
    return (everything.reshape(pairs, 4 * rows, total), gradient)


def meet_product(piece, w, flip, width, collective, side=None, grad_mode=None, parts=1, stream=None, gain=None):
    pairs, rows, total = piece.shape
    features = w.shape[1]
    chunks = pairs * total // width
    tile = (features, width) if flip else (width, features)
    bf16, f32 = jnp.bfloat16, jnp.float32
    inputs, in_specs = (
        [piece, w],
        [pl.BlockSpec(memory_space=pltpu.VMEM), pl.BlockSpec(memory_space=pl.ANY)],
    )
    shapes = [jax.ShapeDtypeStruct((2, 2 * rows, features), f32)]
    out_specs = [pl.BlockSpec(memory_space=pltpu.VMEM)]
    scratch = [
        pltpu.VMEM((chunks,) + tile, bf16),
        pltpu.VMEM((chunks, 2, 2, rows, width), bf16),
        pltpu.VMEM((2, 2 * rows, features), f32),
        pltpu.VMEM((2, 2 * rows, features), bf16),
        pltpu.VMEM((2, 2 * rows, features), bf16),
    ]
    scratch += [pltpu.SemaphoreType.DMA((chunks,))] * 8 + [pltpu.SemaphoreType.DMA((2,))] * 2
    if grad_mode:
        inputs.append(side)
        in_specs.append(pl.BlockSpec(memory_space=pltpu.VMEM))
        out_specs.append(pl.BlockSpec(memory_space=pl.ANY))
        if grad_mode == "wide":
            shape = (parts, pairs, side.shape[0] // parts, total)
            stage = (2, parts, side.shape[0] // parts, width)
        else:
            shape = (total, side.shape[1])
            stage = (2, width, side.shape[1])
        shapes.append(jax.ShapeDtypeStruct(shape, bf16))
        scratch += [pltpu.VMEM(stage, bf16), pltpu.SemaphoreType.DMA((2,))]
    else:
        local = pl.BlockSpec(memory_space=pltpu.VMEM)
        inputs += [stream, gain[None]]
        in_specs += [local, local]
        shapes.insert(0, jax.ShapeDtypeStruct((pairs, 2, 2, rows, total), bf16))
        out_specs.insert(0, pl.BlockSpec(memory_space=pl.ANY))
        shapes.append(jax.ShapeDtypeStruct((4 * rows, features), bf16))
        shapes.append(jax.ShapeDtypeStruct((8, 4 * rows), f32))
        out_specs += [local, local]
        scratch += [pltpu.VMEM((4, 8, 4 * rows), f32)] + [pltpu.SemaphoreType.DMA((4,))] * 2
    result = pl.pallas_call(
        functools.partial(meet_kernel, flip, grad_mode),
        out_shape=tuple(shapes),
        in_specs=in_specs,
        out_specs=out_specs,
        scratch_shapes=scratch,
        compiler_params=pltpu.CompilerParams(
            collective_id=collective, has_side_effects=True, vmem_limit_bytes=56 * MIB
        ),
    )(*inputs)
    if grad_mode:
        return (result[0].reshape(4 * rows, features), result[1])
    return (
        result[0].reshape(pairs, 4 * rows, total),
        result[1].reshape(4 * rows, features),
        result[2],
        result[3][0],
    )


def block_steps(x, acc, gram, poly):
    side, total = x.shape
    step = 256
    count = total // step
    span = 1280 if total % 1280 == 0 else step
    f32, bf16 = jnp.float32, jnp.bfloat16

    def tile(k, size):
        return pl.ds(pl.multiple_of(k * size, size), size)

    def square(k, total):
        values = x[:, tile(k, step)].astype(f32)
        return total + jnp.sum(values * values, axis=0, keepdims=True)

    sums = lax.fori_loop(0, count, square, jnp.zeros((1, step), f32))
    norm = jnp.sqrt(jnp.sum(sums, axis=1, keepdims=True)) + eps_frob

    def divide(k, carry):
        x[:, tile(k, step)] = (x[:, tile(k, step)].astype(f32) / norm).astype(bf16)
        return carry

    lax.fori_loop(0, count, divide, 0)

    def lap(k, carry):
        acc[...] = jnp.zeros_like(acc)

        def add(j, inner):
            block = x[:, tile(j, span)]
            acc[:step, :step] = acc[:step, :step] + dot_nt(block[:step], block[:step])
            acc[step:, :] = acc[step:, :] + dot_nt(block[step:], block)
            return inner

        lax.fori_loop(0, total // span, add, 0)
        acc[:step, step:] = acc[step:, :step].T
        low = acc[...].astype(bf16)
        gram[...] = low
        square_gram = dot_nn(low, gram[...])
        poly[...] = (poly_second * low.astype(f32) + poly_third * square_gram).astype(bf16)

        def advance(j, inner):
            block = x[:, tile(j, span)]
            fresh = poly_first * block.astype(f32) + dot_nn(poly[...], block)
            x[:, tile(j, span)] = fresh.astype(bf16)
            return inner

        lax.fori_loop(0, total // span, advance, 0)
        return carry

    lax.fori_loop(0, 5, lap, 0)


def work_space(side):
    return [
        pltpu.VMEM((side, side), jnp.float32),
        pltpu.VMEM((side, side), jnp.bfloat16),
        pltpu.VMEM((side, side), jnp.bfloat16),
    ]


def gates_kernel(conv, first, second, out, full, came, send_sem, recv_sem):
    me = lax.axis_index("col")
    count = out.shape[0]
    greet([("col", lax.rem(me + step, 4)) for step in range(1, 4)])
    for k, grads in enumerate((first, second)):
        for head in range(conv.shape[1] // HS):
            columns = slice(head * HS, (head + 1) * HS)
            block = dot_nn(conv[:, columns].T, grads[:, columns])
            full[k * HS : (k + 1) * HS, columns] = block.astype(jnp.bfloat16)

    def part(place):
        return full.at[pl.ds(pl.multiple_of(place * count, count), count)]

    def copy(step):
        target = lax.rem(me + step, 4)
        return pltpu.make_async_remote_copy(
            src_ref=part(target),
            dst_ref=came.at[step - 1],
            send_sem=send_sem.at[step - 1],
            recv_sem=recv_sem.at[step - 1],
            device_id={"col": target},
            device_id_type=MESH,
        )

    for step in range(1, 4):
        copy(step).start()
    total = part(me)[...].astype(jnp.float32)
    for step in range(1, 4):
        copy(step).wait_recv()
        total = total + came[step - 1].astype(jnp.float32)
    out[...] = total.astype(jnp.bfloat16)
    for step in range(1, 4):
        copy(step).wait_send()


def gates_product(conv, first, second):
    lanes = conv.shape[1]
    count = 2 * HS // 4
    bf16 = jnp.bfloat16
    return pl.pallas_call(
        gates_kernel,
        out_shape=jax.ShapeDtypeStruct((count, lanes), bf16),
        in_specs=[pl.BlockSpec(memory_space=pltpu.VMEM)] * 3,
        out_specs=pl.BlockSpec(memory_space=pltpu.VMEM),
        scratch_shapes=[
            pltpu.VMEM((2 * HS, lanes), bf16),
            pltpu.VMEM((3, count, lanes), bf16),
            pltpu.SemaphoreType.DMA((3,)),
            pltpu.SemaphoreType.DMA((3,)),
        ],
        compiler_params=pltpu.CompilerParams(
            collective_id=12, has_side_effects=True, vmem_limit_bytes=16 * MIB
        ),
    )(conv, first, second)


def token_total(values):
    return lax.psum(values, "col")


def dp_sum(grad):
    low = grad.astype(jnp.bfloat16)
    return lax.psum_scatter(low, "dp", scatter_dimension=0, tiled=True).astype(jnp.float32)


def pair_sum(grad, dp_count):
    if grad.shape[0] == dp_count:
        return lax.psum_scatter(grad, "dp", scatter_dimension=0)
    return lax.psum_scatter(grad[0], "dp", scatter_dimension=1, tiled=True)


def owner_send(block, root):
    return broadcast(block, "dp", root)


def norm_backward(stream, scale, gain, grad_normed, width):
    weighted = grad_normed * gain[None, :]
    inner = token_total(jnp.sum(stream * weighted, axis=1))
    grad_stream = (
        scale[:, None] * weighted - stream * (scale * scale * scale * inner / width)[:, None]
    )
    grad_gain = jnp.sum(grad_normed * stream * scale[:, None], axis=0)
    return (grad_stream, grad_gain)


def orthogonalize(block):
    work = block
    values = work.astype(jnp.float32)
    work = (values / (jnp.sqrt(jnp.sum(values * values)) + eps_frob)).astype(jnp.bfloat16)
    for step in range(5):
        gram = product_nt(work, work).astype(jnp.bfloat16)
        poly = (poly_second * gram.astype(jnp.float32) + poly_third * product(gram, gram)).astype(
            jnp.bfloat16
        )
        work = (poly_first * work.astype(jnp.float32) + product(poly, work)).astype(jnp.bfloat16)
    return work


def owner_results(blocks, dp_place, dp_count):
    results = [None, None, None, None, None, None]
    for members in ((0, 1, 2), (3, 4, 5)):
        flipped = [blocks[number].shape[0] > blocks[number].shape[1] for number in members]
        wide = [
            blocks[number].T if turn else blocks[number] for number, turn in zip(members, flipped)
        ]
        chosen = wide[0]
        for number, candidate in zip(members[1:], wide[1:]):
            chosen = jnp.where(dp_place == number % dp_count, candidate, chosen)
        done = orthogonalize(chosen)
        for number, turn in zip(members, flipped):
            kept = jnp.where(dp_place == number % dp_count, done, jnp.zeros_like(done))
            results[number] = kept.T if turn else kept
    return results


def dp_moves(moves, sems):
    local_sem, send_sem, recv_sem = sems
    me = lax.axis_index("dp")

    def remote(k, sender, target):
        pairs, source, destination = moves[k]
        return pltpu.make_async_remote_copy(
            src_ref=source(sender, target),
            dst_ref=destination(sender, target),
            send_sem=send_sem.at[k, target],
            recv_sem=recv_sem.at[k, sender],
            device_id={"dp": target},
            device_id_type=MESH,
        )

    def local(k, place):
        pairs, source, destination = moves[k]
        return pltpu.make_async_copy(
            source(place, place), destination(place, place), local_sem.at[k]
        )

    def each(chosen, act):
        for k in chosen:
            for sender, target in moves[k][0]:
                act(k, sender, target)

    def start_one(k, sender, target):
        @pl.when(me == sender)
        def _():
            if sender == target:
                local(k, sender).start()
            else:
                remote(k, sender, target).start()

    def arrive_one(k, sender, target):
        @pl.when(me == target)
        def _():
            if sender == target:
                local(k, sender).wait()
            else:
                remote(k, sender, target).wait_recv()

    def sent_one(k, sender, target):
        if sender != target:

            @pl.when(me == sender)
            def _():
                remote(k, sender, target).wait_send()

    return (
        lambda *chosen: each(chosen, start_one),
        lambda *chosen: each(chosen, arrive_one),
        lambda *chosen: each(chosen, sent_one),
    )


def rows_at(ref, place):
    def pick(sender, target):
        index = sender if place == "sender" else target
        count = ref.shape[0] // 4
        return ref.at[pl.ds(index * count, count)]

    return pick


def entry(ref, place):
    return lambda sender, target: ref.at[sender if place == "sender" else target]


def whole(ref):
    return lambda sender, target: ref


def to_owner(owner):
    return [(sender, owner) for sender in ((owner + step) % 4 for step in range(4))]


def from_owner(owner):
    return [(owner, target) for target in ((owner + step) % 4 for step in range(4))]


SMALL_OWNER, CON_OWNER, GATE_OWNER, UP_OWNER = (2, 1, 3, 0)


def beside(block, rows):
    return jnp.concatenate(
        [block[k * rows : (k + 1) * rows] for k in range(block.shape[0] // rows)], axis=1
    )


def below(block, columns):
    return jnp.concatenate(
        [block[:, k * columns : (k + 1) * columns] for k in range(block.shape[1] // columns)]
    )


def pieces_at_owner(e0, e1, packed, later):
    me = lax.axis_index("dp")

    def piece_for(owner):
        return jnp.where(owner == GATE_OWNER, e0, jnp.where(owner == UP_OWNER, e1, packed))

    leaving = [piece_for(lax.rem(me + step, 4)) for step in range(4)]
    leaving, later = lax.optimization_barrier((leaving, later))
    pieces = leaving[:1]
    for step in range(1, 4):
        pairs = [(sender, (sender + step) % 4) for sender in range(4)]
        pairs = [pair for pair in pairs if pair[1] != SMALL_OWNER]
        pieces.append(lax.ppermute(leaving[step], "dp", pairs))
    return (pieces, later)


def tail_kernel(*refs):
    large, (b0, b1, out) = refs[:4], refs[4:7]
    gates_piece, col_part, dp_part = refs[7:10]
    expand_o, con_o, branch_o, out_o, gates_o, col_o, dp_o = refs[10:17]
    x, packed, pieces, first, second, third, out_v, acc, gram, poly, load_sem = refs[17:28]
    col_buf, dp_buf, gates_dp, gates_col = refs[28:32]
    shares = [
        share_parts("col", col_buf, *refs[32:34]),
        share_parts("dp", dp_buf, *refs[34:36]),
        share_parts("dp", gates_dp, *refs[36:38]),
        share_parts("col", gates_col, *refs[38:40]),
    ]
    sems = refs[40:]
    place = lax.axis_index("col")
    me = lax.axis_index("dp")
    small = out.shape[0]
    width = pieces.shape[2]
    side = x.shape[0]
    rows = side // 4
    moves = [
        (to_owner(SMALL_OWNER), whole(b0), rows_at(first, "sender")),
        (to_owner(SMALL_OWNER), whole(b1), rows_at(second, "sender")),
        (to_owner(SMALL_OWNER), whole(out), entry(out_v, "sender")),
        (from_owner(GATE_OWNER), rows_at(x, "target"), whole(expand_o.at[0])),
        (from_owner(UP_OWNER), rows_at(x, "target"), whole(expand_o.at[1])),
        (from_owner(CON_OWNER), entry(pieces, "target"), whole(con_o)),
        (from_owner(SMALL_OWNER), rows_at(first, "target"), whole(branch_o.at[0])),
        (from_owner(SMALL_OWNER), rows_at(second, "target"), whole(branch_o.at[1])),
        (from_owner(SMALL_OWNER), entry(out_v, "target"), whole(out_o)),
    ]
    start, arrive, sent = dp_moves(moves, sems)
    greet(
        [("dp", lax.rem(me + step, 4)) for step in range(1, 4)]
        + [("col", lax.rem(place + step, 4)) for step in range(1, 4)]
    )
    shares[0][0](col_part[...])
    shares[2][0](gates_piece[...])
    start(0, 1, 2)
    shares[0][1]()
    summed = col_buf[0] + col_buf[1] + col_buf[2] + col_buf[3]
    col_o[...] = summed
    shares[1][0](jnp.concatenate([summed[:8], dp_part[...]], axis=0))
    shares[2][1]()
    shares[3][0](gates_dp[...].reshape(gates_col.shape[1:]))

    def load(owner, target):
        copies = [
            pltpu.make_async_copy(large[step], target((owner - step) % 4), load_sem.at[step])
            for step in range(4)
        ]
        for copy in copies:
            copy.start()
        for copy in copies:
            copy.wait()

    @pl.when(me == CON_OWNER)
    def _():
        load(CON_OWNER, lambda j: packed.at[j])
        for j in range(4):
            for k in range(4):
                part = packed[j, :, k * width : (k + 1) * width]
                x[k * rows : (k + 1) * rows, j * width : (j + 1) * width] = part

    @pl.when(me == GATE_OWNER)
    def _():
        load(GATE_OWNER, lambda j: x.at[pl.ds(j * rows, rows)])

    @pl.when(me == UP_OWNER)
    def _():
        load(UP_OWNER, lambda j: x.at[pl.ds(j * rows, rows)])

    @pl.when(me != SMALL_OWNER)
    def _():
        block_steps(x, acc, gram, poly)

    @pl.when(me == CON_OWNER)
    def _():
        for j in range(4):
            pieces[j] = x[:, j * width : (j + 1) * width]

    start(3, 4, 5)
    for k, part in enumerate((first, second, third)):
        arrive(k)

        @pl.when(me == SMALL_OWNER)
        def _():
            if k == 2:
                for j in range(4):
                    part[:, j * small : (j + 1) * small] = out_v[j].T
            block_steps(part, acc, gram, poly)
            if k == 2:
                for j in range(4):
                    out_v[j] = part[:, j * small : (j + 1) * small].T

        start(6 + k)
    shares[1][1]()
    dp_o[...] = dp_buf[0] + dp_buf[1] + dp_buf[2] + dp_buf[3]
    shares[3][1]()
    half = gates_col.shape[1]
    for k in range(2):
        for head in range(gates_o.shape[1]):
            columns = slice(head * HS, (head + 1) * HS)
            for j in range(HS // half):
                lines = slice(j * half, (j + 1) * half)
                gates_o[k, head, lines, :] = gates_col[k * (HS // half) + j][:, columns]
    arrive(6, 7, 8, 3, 4, 5)
    sent(0, 1, 2, 3, 4, 5, 6, 7, 8)
    for share in shares:
        share[2]()


def finish_blocks(large, con_shape, b0, b1, out, gates_piece, col_part, dp_part):
    piece = large[0].shape
    rows, total = piece
    side = 4 * rows
    f32, bf16 = jnp.float32, jnp.bfloat16
    shape = jax.ShapeDtypeStruct
    small = pltpu.VMEM((side, b0.shape[1]), bf16)
    quarter = (4 * gates_piece.shape[0], gates_piece.shape[1])
    anywhere = pl.BlockSpec(memory_space=pl.ANY)
    local = pl.BlockSpec(memory_space=pltpu.VMEM)
    sems = pltpu.SemaphoreType.DMA
    shapes = [shape(s, bf16) for s in ((2,) + piece, con_shape, (2,) + b0.shape, out.shape)]
    shapes += [shape((2, quarter[1] // HS, HS, HS), bf16), shape(col_part.shape, f32)]
    shapes += [shape(col_part.shape, f32)]
    return pl.pallas_call(
        tail_kernel,
        out_shape=tuple(shapes),
        in_specs=[anywhere] * 7 + [local] * 3,
        out_specs=[anywhere] * 4 + [local] * 3,
        scratch_shapes=[
            pltpu.VMEM((side, total), bf16),
            pltpu.VMEM((4,) + piece, bf16),
            pltpu.VMEM((4,) + con_shape, bf16),
            small,
            small,
            small,
            pltpu.VMEM((4,) + out.shape, bf16),
        ]
        + work_space(side)
        + [sems((4,))]
        + [
            pltpu.VMEM((4,) + col_part.shape, f32),
            pltpu.VMEM((4,) + col_part.shape, f32),
            pltpu.VMEM((4,) + gates_piece.shape, bf16),
            pltpu.VMEM((4,) + quarter, bf16),
        ]
        + [sems((4,))] * 8
        + [sems((9,)), sems((9, 4)), sems((9, 4))],
        compiler_params=pltpu.CompilerParams(
            collective_id=0, has_side_effects=True, vmem_limit_bytes=40 * MIB
        ),
    )(*large, b0, b1, out, gates_piece, col_part, dp_part)


def grouped_step(grad, moment, weight, rate):
    new_moment = momentum_rate * moment + grad
    rows, cols = new_moment.shape
    grouped = new_moment.reshape(rows, cols // GROUP, GROUP)
    norm_sq = jnp.mean(grouped * grouped, axis=2, keepdims=True)
    update = (grouped * lax.rsqrt(norm_sq + eps_norm)).reshape(rows, cols)
    return (new_moment, weight - rate * update)


def shards(
    block_input,
    segment_ids,
    output_cotangent,
    norm_gains,
    branch_weights,
    mixer_vectors,
    gate_blocks,
    output_weights,
    expand_weights,
    contract_weights,
    gains_momentum,
    branch_momentum,
    vectors_momentum,
    gates_momentum,
    output_momentum,
    expand_momentum,
    contract_momentum,
):
    f32 = jnp.float32
    bf16 = jnp.bfloat16
    col_count = lax.axis_size("col")
    col_place = lax.axis_index("col")
    dp_count = lax.axis_size("dp")
    dp_place = lax.axis_index("dp")
    group_rows = block_input.shape[0]
    rows = group_rows // col_count
    lanes = mixer_vectors.shape[1]
    heads_here = lanes // HS
    feature_count = block_input.shape[1]
    width = feature_count * col_count
    first_row = col_place * rows
    reach = CONV - 1
    seg_row = segment_ids[0]
    seg_ext = jnp.concatenate(
        [jnp.full((reach,), -1, jnp.int32), seg_row, jnp.full((reach,), -2, jnp.int32)]
    )
    seg_here = lax.dynamic_slice_in_dim(seg_ext, first_row + reach, rows + reach)
    masks = []
    for shift in range(CONV):
        earlier = lax.dynamic_slice_in_dim(seg_ext, first_row + reach - shift, rows + reach)
        masks.append((earlier == seg_here).astype(f32))
    reset_rows = masks[1][:rows] < 0.5
    stream = block_input.astype(f32)
    branch_pre, normed_low, scale_rows, contract_term = spread_product(
        block_input,
        branch_weights,
        False,
        640,
        2,
        norm_gains[0],
        (output_cotangent, contract_weights),
    )
    scale_one = scale_rows[0]
    grad_activated = lax.psum_scatter(contract_term, "col", scatter_dimension=0, tiled=True)
    mixed = branch_pre[0]
    gelu_in = branch_pre[1]
    edge = from_behind(mixed[rows - reach :], "col", 1)
    extended = jnp.concatenate([edge, mixed], axis=0)
    windows = []
    conv_out = jnp.zeros((rows, lanes), f32) + mixer_vectors[CONV][None, :]
    for shift in range(CONV):
        window = extended[reach - shift : reach - shift + rows] * masks[shift][:rows, None]
        windows.append(window)
        conv_out = conv_out + mixer_vectors[shift][None, :] * window
    conv_low = conv_out.astype(bf16).reshape(rows, heads_here, HS)
    gate_pre = jnp.einsum(
        "thi,ghij->tghj", conv_low, gate_blocks, preferred_element_type=f32
    ).reshape(rows, 2, lanes)
    gate_pre = gate_pre + mixer_vectors[CONV + 1 : CONV + 3][None]

    def recurrence_terms(conv_values, gate_values, rate_values):
        input_gate = jax.nn.sigmoid(gate_values[:, 0])
        decay_gate = jax.nn.sigmoid(gate_values[:, 1])
        log_decay = -decay_scale * decay_gate * jax.nn.softplus(rate_values)[None, :]
        inject_scale = jnp.where(reset_rows[:, None], 1.0, jnp.sqrt(1.0 - jnp.exp(2.0 * log_decay)))
        decay_values = jnp.where(reset_rows[:, None], 0.0, jnp.exp(log_decay))
        return (decay_values, inject_scale * input_gate * conv_values)

    (decay, inject), pull_terms = jax.vjp(
        recurrence_terms, conv_out, gate_pre, mixer_vectors[CONV + 3]
    )
    local_a, local_b = linear_scan(decay, inject, False)
    identity = (jnp.ones((lanes,), f32), jnp.zeros((lanes,), f32))
    incoming = prefix((local_a[-1], local_b[-1]), "col", link, identity, False)
    carried = incoming[1]
    state = local_a * carried[None, :] + local_b
    gelu_out, pull_gelu = jax.vjp(gelu_tanh, gelu_in)
    hidden = (gelu_out * state).astype(bf16)
    hidden_all, middle, normed_two_low, scale_two = meet_product(
        hidden[None],
        output_weights,
        False,
        256,
        3,
        stream=block_input,
        gain=norm_gains[1],
    )
    expand_pre = spread_product(normed_two_low, expand_weights, False, 768, 4)

    def geglu(gate_values, up_values):
        return gelu_tanh(gate_values) * up_values

    activated, pull_geglu = jax.vjp(geglu, expand_pre[0], expand_pre[1])
    activated_low = activated.astype(bf16)
    activated_all, contract_grad = meet_gradient(activated_low[None], 640, 5, output_cotangent)
    cot_values = output_cotangent.astype(f32)
    grad_activated = grad_activated.astype(f32)
    grad_gate, grad_up = pull_geglu(grad_activated)
    grad_expand_low = jnp.stack([grad_gate, grad_up]).astype(bf16)
    grad_expand_low, contract_grad = lax.optimization_barrier((grad_expand_low, contract_grad))
    parts = dp_count if feature_count % (16 * dp_count) == 0 else 1
    grad_normed_two, expand_grad = meet_product(
        grad_expand_low, expand_weights, True, 768, 7, normed_two_low.T, "wide", parts
    )
    grad_middle_norm, gain_two_grad = norm_backward(
        middle, scale_two, norm_gains[1], grad_normed_two, width
    )
    grad_middle = cot_values + grad_middle_norm
    grad_branch_low = grad_middle.astype(bf16)
    output_grad = product_tn(hidden_all[0], grad_branch_low)
    grad_hidden = spread_product(grad_branch_low, output_weights, True, 256, 8)[0]
    grad_state = grad_hidden * gelu_out
    (grad_gelu_in,) = pull_gelu(grad_hidden * state)
    shifted_decay = jnp.concatenate([decay[1:], jnp.ones((1, lanes), f32)], axis=0)
    back_a, back_b = linear_scan(shifted_decay, grad_state, True)
    from_later = prefix((decay[0] * back_a[0], decay[0] * back_b[0]), "col", link, identity, True)
    grad_total = back_a * from_later[1][None, :] + back_b
    previous = jnp.concatenate([carried[None, :], state[:-1]], axis=0)
    grad_conv_direct, grad_gate_pre, grad_rate = pull_terms((grad_total * previous, grad_total))
    grad_gate_low = grad_gate_pre.astype(bf16)
    grad_gate_heads = grad_gate_low.reshape(rows, 2, heads_here, HS)
    grad_conv = grad_conv_direct + jnp.einsum(
        "tghj,ghij->thi", grad_gate_heads, gate_blocks, preferred_element_type=f32
    ).reshape(rows, lanes)
    parts = dp_count if feature_count % (16 * dp_count) == 0 else 1
    planes = dp_count == 4 and parts == 4 and 2 * feature_count <= lanes and group_rows <= lanes
    gate_bias_grad = jnp.sum(grad_gate_low.astype(f32), axis=0)
    after = from_behind(grad_conv[:reach], "col", -1)
    grad_conv_ext = jnp.concatenate([grad_conv, after], axis=0)
    grad_mixed = jnp.zeros((rows, lanes), f32)
    tap_grads = []
    for shift in range(CONV):
        masked = grad_conv_ext * masks[shift][:, None]
        grad_mixed = grad_mixed + mixer_vectors[shift][None, :] * masked[shift : shift + rows]
        tap_grads.append(jnp.sum(grad_conv * windows[shift], axis=0))
    grad_mixed, activated_all = lax.optimization_barrier((grad_mixed, activated_all))
    contracted_low = product(activated_all[0], contract_weights).astype(bf16)
    contracted = contracted_low.astype(f32) + lax.ppermute(
        contracted_low, "row", [(0, 1), (1, 0)]
    ).astype(f32)
    block_output = (middle + contracted).astype(bf16)
    vector_rows = tap_grads + [
        jnp.sum(grad_conv, axis=0),
        gate_bias_grad[0],
        gate_bias_grad[1],
        grad_rate,
    ]
    vectors_grad = jnp.stack(vector_rows)
    grad_branch_pre = jnp.stack([grad_mixed, grad_gelu_in]).astype(bf16)
    grad_normed_one, branch_grad = meet_product(
        grad_branch_pre, branch_weights, True, 640, 9, normed_low.T, "wide", parts
    )
    if planes:
        contract_sum = pair_sum(contract_grad.reshape((4, -1) + contract_grad.shape[1:]), 4)
        expand_grad, contract_sum = lax.optimization_barrier((expand_grad, contract_sum))
        expand_sum = pair_sum(expand_grad, 4)
        con_low = (momentum_rate * contract_momentum[0] + contract_sum).astype(bf16)
        con_low = beside(con_low.T, expand_momentum.shape[2])
        weighted = grad_normed_one * norm_gains[0][None, :]
        inner_part = jnp.sum(stream * weighted, axis=1)
        gain_one_grad = jnp.sum(grad_normed_one * stream * scale_one[:, None], axis=0)
        col_part = jnp.concatenate(
            [
                vectors_grad,
                jnp.pad(inner_part, (0, lanes - group_rows))[None],
                jnp.zeros((7, lanes), f32),
            ]
        )
        gains_row = jnp.concatenate([gain_one_grad, gain_two_grad])
        dp_part = jnp.pad(gains_row[None], ((0, 7), (0, lanes - 2 * feature_count)))
        gates_part = gates_product(
            conv_low.reshape(rows, lanes), grad_gate_low[:, 0], grad_gate_low[:, 1]
        )
        piece_rows = branch_grad.shape[2]
        small_grad = jnp.concatenate(
            [
                branch_grad.reshape(4, 2 * piece_rows, lanes),
                jnp.stack([beside(part, piece_rows) for part in jnp.split(output_grad.astype(bf16), 4)]),
                gates_part.reshape(4, -1, lanes),
            ],
            axis=1,
        )
        con_low, expand_sum, col_part, dp_part, small_grad, block_output = (
            lax.optimization_barrier(
                (con_low, expand_sum, col_part, dp_part, small_grad, block_output)
            )
        )
        expand_low = (momentum_rate * expand_momentum[:, 0] + expand_sum).astype(bf16)
        small_grad, expand_sum = lax.optimization_barrier((small_grad, expand_sum))
        large, (expand_sum, contract_sum) = pieces_at_owner(
            expand_low[0], expand_low[1], con_low, (expand_sum, contract_sum)
        )
        small_sum = pair_sum(small_grad, 4)
        branch_sum = small_sum[: 2 * piece_rows].reshape(2, piece_rows, lanes)
        output_sum = below(small_sum[2 * piece_rows : 3 * piece_rows], output_momentum.shape[2])
        branch_low = (momentum_rate * branch_momentum[:, 0] + branch_sum).astype(bf16)
        output_low = (momentum_rate * output_momentum[0] + output_sum).astype(bf16)
        expand_orth, con, branch_orth, out, gates_all, col_total, dp_total = finish_blocks(
            large,
            contract_momentum.shape[:0:-1],
            branch_low[0],
            branch_low[1],
            output_low,
            small_sum[3 * piece_rows :],
            col_part,
            dp_part,
        )
        output_sum = output_sum.astype(f32)
        con = con.T
        gates_total = gates_all.astype(f32)
        vectors_total = dp_total[:8]
        gains_total = dp_total[8, : 2 * feature_count].reshape(2, feature_count)
        inner = col_total[8, :group_rows]
        grad_stream_norm = (
            scale_one[:, None] * weighted
            - stream * (scale_one * scale_one * scale_one * inner / width)[:, None]
        )
    else:
        grad_stream_norm, gain_one_grad = norm_backward(
            stream, scale_one, norm_gains[0], grad_normed_one, width
        )
        vectors_total, gains_total = lax.psum(
            (lax.psum(vectors_grad, "col"), jnp.stack([gain_one_grad, gain_two_grad])), "dp"
        )
        gates_grad = jnp.einsum(
            "thi,tghj->ghij", conv_low, grad_gate_heads, preferred_element_type=f32
        ).astype(bf16)
        branch_sum = pair_sum(branch_grad, dp_count)
        expand_sum = pair_sum(expand_grad, dp_count)
        output_sum = dp_sum(output_grad)
        contract_sum = dp_sum(contract_grad)
        gates_total = lax.psum(gates_grad, ("dp", "col")).astype(f32)
    input_grad = (grad_middle + grad_stream_norm).astype(bf16)
    branch_sum = branch_sum.astype(f32)
    expand_sum = expand_sum.astype(f32)
    contract_sum = contract_sum.astype(f32)
    branch_moment = momentum_rate * branch_momentum[:, 0] + branch_sum
    expand_moment = momentum_rate * expand_momentum[:, 0] + expand_sum
    output_moment = momentum_rate * output_momentum[0] + output_sum
    contract_moment = momentum_rate * contract_momentum[0] + contract_sum
    if not planes:
        moments = (*branch_moment, output_moment, *expand_moment, contract_moment)
        lows = [moment.astype(bf16) for moment in moments]
        gathered = [lax.all_gather(low, "dp", axis=0, tiled=True) for low in lows]
        orth = owner_results(gathered, dp_place, dp_count)
        pieces = [
            lax.dynamic_slice_in_dim(
                owner_send(orth[number], number % dp_count),
                dp_place * lows[number].shape[0],
                lows[number].shape[0],
                0,
            )
            for number in range(6)
        ]
        branch_orth, expand_orth = jnp.stack(pieces[:2]), jnp.stack(pieces[3:5])
        out, con = pieces[2], pieces[5]

    def stepped(weight, orth, axis):
        count = orth.shape[axis]
        piece = lax.dynamic_slice_in_dim(weight, dp_place * count, count, axis).astype(f32)
        tall = max(1.0, weight.shape[axis] / weight.shape[axis + 1]) ** 0.5
        return piece - muon_rate * tall * orth.astype(f32)

    branch_new = stepped(branch_weights, branch_orth, 1)
    expand_new = stepped(expand_weights, expand_orth, 1)
    output_new = stepped(output_weights, out, 0)
    contract_new = stepped(contract_weights, con, 0)
    gates_moment = momentum_rate * gates_momentum + gates_total
    gate_sq = jnp.mean(gates_moment * gates_moment, axis=(2, 3), keepdims=True)
    gates_new = gate_blocks.astype(f32) - gate_rate * gates_moment * lax.rsqrt(gate_sq + eps_norm)
    vectors_moment, vectors_new = grouped_step(
        vectors_total, vectors_momentum, mixer_vectors, vector_rate
    )
    gains_moment, gains_new = grouped_step(gains_total, gains_momentum, norm_gains, vector_rate)
    return (
        block_output,
        input_grad,
        gains_total,
        branch_sum[:, None],
        vectors_total,
        gates_total,
        output_sum[None],
        expand_sum[:, None],
        contract_sum[None],
        gains_new,
        branch_new[:, None],
        vectors_new,
        gates_new,
        output_new[None],
        expand_new[:, None],
        contract_new[None],
        gains_moment,
        branch_moment[:, None],
        vectors_moment,
        gates_moment,
        output_moment[None],
        expand_moment[:, None],
        contract_moment[None],
    )


def solution(mesh):
    return jax.shard_map(
        shards,
        mesh=mesh,
        in_specs=(
            P("dp", "col"),
            P("dp", None),
            P("dp", "col"),
            P(None, "col"),
            P(None, "col", "row"),
            P(None, "row"),
            P(None, "row", None, None),
            P("row", "col"),
            P(None, "col", "row"),
            P("row", "col"),
            P(None, "col"),
            P(None, "col", "dp", "row"),
            P(None, "row"),
            P(None, "row", None, None),
            P("row", "dp", "col"),
            P(None, "col", "dp", "row"),
            P("row", "dp", "col"),
        ),
        out_specs=(
            P("dp", "col"),
            P("dp", "col"),
            P(None, "col"),
            P(None, "col", "dp", "row"),
            P(None, "row"),
            P(None, "row", None, None),
            P("row", "dp", "col"),
            P(None, "col", "dp", "row"),
            P("row", "dp", "col"),
            P(None, "col"),
            P(None, "col", "dp", "row"),
            P(None, "row"),
            P(None, "row", None, None),
            P("row", "dp", "col"),
            P(None, "col", "dp", "row"),
            P("row", "dp", "col"),
            P(None, "col"),
            P(None, "col", "dp", "row"),
            P(None, "row"),
            P(None, "row", None, None),
            P("row", "dp", "col"),
            P(None, "col", "dp", "row"),
            P("row", "dp", "col"),
        ),
        check_vma=False,
    )
```
